32 devices in a mesh: dp: 8 (over z, x), mp: 4 (over y, core).
Axes of the slice: x: 2, y: 2, z: 4, core: 2. Of those that a mesh axis runs over, the one named last changes fastest.
Arguments:
- tokens_in: bfloat16 [128, 128, 768], P('dp', 'mp'), may hold values from -6 to 6
- seg: int32 [128, 128], replicated, may hold values from 0 to 3, as said below
- route: int32 [128], replicated, may hold values from 0 to 127, as said below
- w_qkv: bfloat16 [768, 3, 768], P(None, None, 'mp'), may hold values from -0.21875 to 0.21875
- b_qv: float32 [2, 768], P(None, 'mp'), may hold values from -3 to 3
- w_out: bfloat16 [768, 768], P('mp'), may hold values from -0.625 to 0.625
- b_out: float32 [768], replicated, may hold values from -2 to 2
- gain_attn: float32 [768], replicated, may hold values from 0.5 to 1.5
- bias_attn: float32 [768], replicated, may hold values from -2 to 2
- w_in: bfloat16 [768, 3072], P(None, 'mp'), may hold values from -0.21875 to 0.21875
- b_in: float32 [3072], P('mp'), may hold values from -3 to 3
- w_down: bfloat16 [3072, 768], P('mp'), may hold values from -0.109375 to 0.109375
- b_down: float32 [768], replicated, may hold values from -2 to 2
- gain_ffn: float32 [768], replicated, may hold values from 0.5 to 1.5
- bias_ffn: float32 [768], replicated, may hold values from -2 to 2
- out_grad: bfloat16 [128, 128, 768], P('dp'), may hold values from -6 to 6
- pool_grad: float32 [128, 4, 768], P('dp'), may hold values from -24 to 24
Outputs:
- tokens_out: bfloat16 [128, 128, 768], P('dp', 'mp')
- pooled: float32 [128, 4, 768], P('dp')
- grad_x: bfloat16 [128, 128, 768], P('dp', 'mp')
- grad_w_qkv: float32 [768, 3, 768], P(None, None, 'mp')
- grad_b_qv: float32 [2, 768], P(None, 'mp')
- grad_w_out: float32 [768, 768], P('mp')
- grad_b_out: float32 [768], replicated
- grad_gain_attn: float32 [768], replicated
- grad_bias_attn: float32 [768], replicated
- grad_w_in: float32 [768, 3072], P(None, 'mp')
- grad_b_in: float32 [3072], P('mp')
- grad_w_down: float32 [3072, 768], P('mp')
- grad_b_down: float32 [768], replicated
- grad_gain_ffn: float32 [768], replicated
- grad_bias_ffn: float32 [768], replicated
The draws below stay inside these ranges and needn't reach their ends.
Inputs may be any that keep to these rules, and one draw needn't show every extreme that they name: route is a permutation of the 128 rows; regrouped row q belongs to index q // 16 of dp; the rows of one index of dp go to 8 different indices, exactly 2 to each. `seg`: each row holds 4 segments in order, each of one or more positions; segment numbers never fall along a row; one segment of each row covers three quarters of the row or more.
All inputs are finite; a program needn't handle non-finite values.
Results may differ from the reference program's by a relative error of at most 0.013.
Values may be sent and summed in bfloat16 or wider, within the bound.
No kernel may reach another device: no remote copies, remote signals or barrier semaphores. Data moves between devices by JAX's collectives and lax.ppermute only.
A program may use at most 192 MiB of HBM per device.

```python
import math
import jax
import jax.numpy as jnp
from jax import lax

D = 768
H = 12
HD = 64
FF = 3072
SEQ = 128
SEGS = 4
ROWS_DEV = 16
ROWS = 128
N_DP = 8


def draw_route(key, part):
    key = jax.random.fold_in(key, 11)
    perm_key, offset_key, rotate_key, order_key = jax.random.split(key, 4)
    stride = max(1, N_DP // ROWS_DEV)
    shuffle = jax.random.permutation(perm_key, N_DP)
    offset = jax.random.randint(offset_key, (), 0, N_DP)
    rotate = jax.random.randint(rotate_key, (), 0, ROWS_DEV)
    local_order = jax.vmap(lambda subkey: jax.random.permutation(subkey, ROWS_DEV))(jax.random.split(order_key, N_DP))
    source = jnp.arange(N_DP)[:, None]
    target = shuffle[(source + offset + local_order * stride) % N_DP]
    placed = (local_order + rotate) % ROWS_DEV
    return (target * ROWS_DEV + placed).reshape(-1).astype(jnp.int32)


def draw_seg(key, part):
    key = jax.random.fold_in(key, 23)
    long_key, size_key = jax.random.split(key, 2)
    longest = jax.random.randint(long_key, (ROWS, 1), 0, SEGS)
    short_most = max(1, (SEQ // 4 - 1) // (SEGS - 1))
    pieces = jax.random.randint(size_key, (ROWS, SEGS), 1, short_most + 1)
    column = jnp.arange(SEGS)[None, :]
    pieces = jnp.where(column == longest, 0, pieces)
    pieces = jnp.where(column == longest, SEQ - jnp.sum(pieces, axis=1, keepdims=True), pieces)
    bounds = jnp.cumsum(pieces, axis=1)
    places = jnp.arange(SEQ)[None, :, None]
    return jnp.sum((places >= bounds[:, None, :SEGS - 1]).astype(jnp.int32), axis=2).astype(jnp.int32)


def block_scale(stream_key, extent, cuts, smallest, top_value):
    loudness, own = 1.0, jax.random.fold_in(stream_key, 6)
    for axis_at, blocks in cuts:
        heights = jnp.exp(jax.random.uniform(jax.random.fold_in(own, axis_at), (blocks,), jnp.float32, smallest / len(cuts), top_value / len(cuts)))
        loudness = loudness * jnp.repeat(heights, extent[axis_at] // blocks).reshape([-1 if axis == axis_at else 1 for axis in range(len(extent))])
    return loudness


def noise(rng, shape, deviation, most, cuts=(), kind=jnp.bfloat16):
    values = deviation * jax.random.normal(rng, shape, jnp.float32)
    if cuts:
        values = values * block_scale(rng, shape, cuts, -0.22, 0.18)
    return jnp.clip(values, -most, most).astype(kind)


def setup_inputs(seed: int = 0) -> dict:
    keys = jax.random.split(jax.random.key(seed), 18)
    return {
        "tokens_in": noise(keys[0], (ROWS, SEQ, D), 1.0, 6.0, ((0, 8), (1, 4))),
        "seg": draw_seg(jax.random.fold_in(keys[17], 71), 0),
        "route": draw_route(jax.random.fold_in(keys[17], 71), 0),
        "w_qkv": noise(keys[3], (D, 3, H * HD), D ** -0.5, 0.21875, ((2, 4),)),
        "b_qv": noise(keys[4], (2, H * HD), 0.5, 3.0, ((1, 4),), jnp.float32),
        "w_out": noise(keys[5], (H * HD, D), (H * HD // 8) ** -0.5, 0.625, ((0, 4),)),
        "b_out": noise(keys[6], (D,), 0.3, 2.0, (), jnp.float32),
        "gain_attn": jnp.clip(1.0 + 0.1 * jax.random.normal(keys[7], (D,), jnp.float32), 0.5, 1.5),
        "bias_attn": noise(keys[8], (D,), 0.3, 2.0, (), jnp.float32),
        "w_in": noise(keys[9], (D, FF), D ** -0.5, 0.21875, ((1, 4),)),
        "b_in": noise(keys[10], (FF,), 0.5, 3.0, ((0, 4),), jnp.float32),
        "w_down": noise(keys[11], (FF, D), FF ** -0.5, 0.109375, ((0, 4),)),
        "b_down": noise(keys[12], (D,), 0.3, 2.0, (), jnp.float32),
        "gain_ffn": jnp.clip(1.0 + 0.1 * jax.random.normal(keys[13], (D,), jnp.float32), 0.5, 1.5),
        "bias_ffn": noise(keys[14], (D,), 0.3, 2.0, (), jnp.float32),
        "out_grad": noise(keys[15], (ROWS, SEQ, D), 1.0, 6.0, ((0, 8),)),
        "pool_grad": noise(keys[16], (ROWS, SEGS, D), 4.0, 24.0, ((0, 8),), jnp.float32),
    }


@jax.custom_vjp
def low(v):
    return lax.optimization_barrier(v.astype(jnp.bfloat16)).astype(jnp.float32)

@jax.custom_vjp
def low_back(v):
    return v

def low_keep(v):
    return (low(v), None)

def low_pass(kept, grad):
    return (grad,)

def back_keep(v):
    return (v, None)

def back_low(kept, grad):
    return (low(grad),)
low.defvjp(low_keep, low_pass)
low_back.defvjp(back_keep, back_low)

def matmul(pattern, first_op, second_op):
    return jnp.einsum(pattern, first_op, second_op, precision=lax.Precision.HIGHEST)

def layer_norm(values, scale_gain, shift_bias):
    centre = values - lax.optimization_barrier(jnp.mean(values, axis=-1, keepdims=True))
    spread = lax.optimization_barrier(jnp.mean(centre * centre, axis=-1, keepdims=True))
    return centre * lax.rsqrt(spread + 1e-12) * scale_gain + shift_bias

def encoder(weights, inputs, segment):
    w_qkv, b_qv, w_out, b_out, gain_attn, bias_attn, w_in, b_in, w_down, b_down, gain_ffn, bias_ffn = weights
    row_count = inputs.shape[0]
    head_shape = (row_count, SEQ, H, HD)
    projected = matmul('rsd,dcf->rscf', inputs, w_qkv)
    queries = low(low_back(projected[:, :, 0] + b_qv[0])).reshape(head_shape)
    keys_all = low(low_back(projected[:, :, 1])).reshape(head_shape)
    values_all = low(low_back(projected[:, :, 2] + b_qv[1])).reshape(head_shape)
    scores = low_back(matmul('rqhe,rkhe->rhqk', queries, keys_all) * HD ** (-0.5))
    allowed = (segment[:, :, None] == segment[:, None, :])[:, None]
    scores = jnp.where(allowed, scores, -1e+30)
    row_peak = lax.optimization_barrier(jnp.max(scores, axis=-1, keepdims=True))
    raised = jnp.exp(scores - row_peak)
    attention = raised / lax.optimization_barrier(jnp.sum(raised, axis=-1, keepdims=True))
    attended = low(low_back(matmul('rhqk,rkhe->rqhe', low(attention), values_all))).reshape(row_count, SEQ, H * HD)
    branch = low_back(matmul('rsf,fd->rsd', attended, w_out))
    normed = low(layer_norm(inputs + branch + b_out, gain_attn, bias_attn))
    hidden = low_back(matmul('rsd,df->rsf', normed, w_in) + b_in)
    active = low(jax.nn.gelu(hidden, approximate=False))
    output = normed + low_back(matmul('rsf,fd->rsd', active, w_down)) + b_down
    block_out = layer_norm(output, gain_ffn, bias_ffn)
    member = (segment[:, :, None] == jnp.arange(SEGS)[None, None, :]).astype(jnp.float32)
    counts = lax.optimization_barrier(jnp.sum(member, axis=1))
    pooled = matmul('rsg,rsd->rgd', member, block_out) / counts[:, :, None]
    return (block_out, pooled)

def reference(tokens_in, seg, route, w_qkv, b_qv, w_out, b_out, gain_attn, bias_attn, w_in, b_in, w_down, b_down, gain_ffn, bias_ffn, out_grad, pool_grad):
    weights = tuple((entry.astype(jnp.float32) for entry in (w_qkv, b_qv, w_out, b_out, gain_attn, bias_attn, w_in, b_in, w_down, b_down, gain_ffn, bias_ffn)))
    row_total = tokens_in.shape[0]
    regrouped = jnp.zeros_like(tokens_in).at[route].set(tokens_in)
    grouped_seg = jnp.zeros_like(seg).at[route].set(seg)
    grouped_pool = jnp.zeros_like(pool_grad).at[route].set(pool_grad)
    group_rows = math.gcd(row_total, 32)
    group_count = row_total // group_rows

    def blocked(whole):
        return whole.reshape((group_count, group_rows) + whole.shape[1:])

    def advance(summed, slices):
        inputs, segment, grad_out, grad_pool = slices

        def forward(weight_set, values):
            return encoder(weight_set, values, segment)
        outputs, backward = jax.vjp(forward, weights, inputs.astype(jnp.float32))
        grad_weights, grad_inputs = backward((grad_out.astype(jnp.float32), grad_pool))
        summed = jax.tree.map(jnp.add, summed, grad_weights)
        return (summed, (outputs[0].astype(jnp.bfloat16), outputs[1], grad_inputs.astype(jnp.bfloat16)))
    initial = jax.tree.map(jnp.zeros_like, weights)
    summed, (block_out, pooled, grad_input) = lax.scan(advance, initial, (blocked(regrouped), blocked(grouped_seg), blocked(out_grad), blocked(grouped_pool)))
    block_out = block_out.reshape(tokens_in.shape)
    pooled = pooled.reshape(pool_grad.shape)[route]
    grad_input = grad_input.reshape(tokens_in.shape)[route]
    return (block_out, pooled, grad_input, summed[0], summed[1], summed[2], summed[3], summed[4], summed[5], summed[6], summed[7], summed[8], summed[9], summed[10], summed[11])
```

```python
import jax
import jax.numpy as jnp
from jax import lax
from jax.experimental import pallas as pl
from jax.experimental.pallas import tpu as pltpu
from jax.sharding import PartitionSpec as P

HD = 64
SEGS = 4


EPSILON = 1e-12
MASKED = -1e30
f32 = jnp.float32
bf16 = jnp.bfloat16


def normalize(values):
    centre = values - jnp.mean(values, axis=-1, keepdims=True)
    scale_inv = lax.rsqrt(jnp.mean(centre * centre, axis=-1, keepdims=True) + EPSILON)
    return (centre * scale_inv, scale_inv[..., 0])


def norm_back(grad_hat, normed_hat, inverse):
    mean_grad = jnp.mean(grad_hat, axis=-1, keepdims=True)
    mean_proj = jnp.mean(grad_hat * normed_hat, axis=-1, keepdims=True)
    return inverse[..., None] * (grad_hat - mean_grad - normed_hat * mean_proj)


def pack_rows(values, position, filled):
    picked = jnp.take(values, position, axis=0)
    shape_mask = filled.reshape((-1,) + (1,) * (values.ndim - 1))
    return jnp.where(shape_mask, picked, jnp.zeros_like(picked))


def per_device_general(
    tokens_in,
    seg,
    route,
    w_qkv,
    b_qv,
    w_out,
    b_out,
    gain_attn,
    bias_attn,
    w_in,
    b_in,
    w_down,
    b_down,
    gain_ffn,
    bias_ffn,
    out_grad,
    pool_grad,
):
    f32 = jnp.float32
    bf16 = jnp.bfloat16
    devices = lax.axis_size("dp")
    row_local = tokens_in.shape[0]
    quarter = tokens_in.shape[1]
    all_rows = route.shape[0]
    capacity = max(1, row_local // devices)
    buffer_len = devices * capacity
    my_index = lax.axis_index("dp")
    target_dev = route // row_local
    dest_grid = target_dev.reshape(devices, row_local)
    before = jnp.arange(row_local)[None, :] < jnp.arange(row_local)[:, None]
    same_dest = dest_grid[:, :, None] == dest_grid[:, None, :]
    earlier_count = (
        jnp.sum(jnp.where(same_dest & before[None], 1, 0), axis=2).reshape(-1).astype(jnp.int32)
    )
    slot_out = target_dev * capacity + earlier_count
    slot_in = jnp.arange(all_rows, dtype=jnp.int32) // row_local * capacity + earlier_count
    own_slots = lax.dynamic_slice_in_dim(slot_out, my_index * row_local, row_local)
    local_rows = jnp.arange(row_local, dtype=jnp.int32)
    send_pos = jnp.zeros(buffer_len, jnp.int32).at[own_slots].set(local_rows)
    send_fill = jnp.zeros(buffer_len, jnp.bool_).at[own_slots].set(True)
    arrive = jnp.where(target_dev == my_index, route - my_index * row_local, row_local)
    recv_pos = jnp.zeros(row_local, jnp.int32).at[arrive].set(slot_in, mode="drop")
    anchor = (
        jnp.zeros(row_local, jnp.int32)
        .at[arrive]
        .set(jnp.arange(all_rows, dtype=jnp.int32), mode="drop")
    )
    back_pos = jnp.zeros(buffer_len, jnp.int32).at[recv_pos].set(local_rows)
    back_fill = jnp.zeros(buffer_len, jnp.bool_).at[recv_pos].set(True)
    arrived = lax.all_to_all(
        pack_rows(tokens_in, send_pos, send_fill), "dp", split_axis=0, concat_axis=0, tiled=True
    )
    rows_x = jnp.take(arrived, recv_pos, axis=0)
    segment = jnp.take(seg, anchor, axis=0)
    full_len = segment.shape[1]
    mp_index = lax.axis_index("mp")

    def own_part(values):
        return lax.dynamic_slice_in_dim(values, mp_index * quarter, quarter, 1)

    gathered = lax.all_gather(rows_x, "mp", axis=1, tiled=True)
    head_width = w_qkv.shape[2]
    local_heads = head_width // HD
    head_shape = (row_local, full_len, local_heads, HD)
    projected = jnp.einsum("rsd,dcf->rscf", gathered, w_qkv, preferred_element_type=f32)
    query_heads = (projected[:, :, 0] + b_qv[0]).astype(bf16).reshape(head_shape)
    key_heads = projected[:, :, 1].astype(bf16).reshape(head_shape)
    value_heads = (projected[:, :, 2] + b_qv[1]).astype(bf16).reshape(head_shape)
    allowed = (segment[:, :, None] == segment[:, None, :])[:, None]
    factor = HD ** (-0.5)

    def scores_of():
        raw_scores = (
            jnp.einsum("rqhe,rkhe->rhqk", query_heads, key_heads, preferred_element_type=f32)
            * factor
        )
        return jnp.where(allowed, raw_scores, MASKED)

    scores = scores_of()
    row_peak = jnp.max(scores, axis=-1, keepdims=True)
    raised = jnp.exp(scores - row_peak)
    weight_total = jnp.sum(raised, axis=-1, keepdims=True)
    log_total = row_peak + jnp.log(weight_total)
    attention = raised / weight_total
    attended = jnp.einsum(
        "rhqk,rkhe->rqhe", attention.astype(bf16), value_heads, preferred_element_type=f32
    )
    attended = attended.astype(bf16).reshape(row_local, full_len, head_width)
    branch = jnp.einsum("rsf,fd->rsd", attended, w_out, preferred_element_type=f32)
    summed_branch = lax.psum_scatter(branch, "mp", scatter_dimension=1, tiled=True)
    hat_attn, inv_attn = normalize(rows_x.astype(f32) + summed_branch + b_out)
    normed_low = (hat_attn * gain_attn + bias_attn).astype(bf16)
    normed_all = lax.all_gather(normed_low, "mp", axis=1, tiled=True)
    hidden = jnp.einsum("rsd,df->rsf", normed_all, w_in, preferred_element_type=f32) + b_in
    active, gelu_back = jax.vjp(lambda values: jax.nn.gelu(values, approximate=False), hidden)
    active_low = active.astype(bf16)
    ffn_part = jnp.einsum("rsf,fd->rsd", active_low, w_down, preferred_element_type=f32)
    ffn_total = lax.psum(ffn_part, "mp")
    hat_ffn, inv_ffn = normalize(normed_all.astype(f32) + ffn_total + b_down)
    block_out = hat_ffn * gain_ffn + bias_ffn
    output_rows = own_part(block_out).astype(bf16)
    member = (segment[:, :, None] == jnp.arange(SEGS)[None, None, :]).astype(f32)
    counts = jnp.sum(member, axis=1)
    pooled_rows = (
        jnp.einsum("rsg,rsd->rgd", member, block_out, precision=lax.Precision.HIGHEST)
        / counts[:, :, None]
    )
    pooled_back = lax.all_to_all(
        pack_rows(pooled_rows, back_pos, back_fill).astype(jnp.bfloat16),
        "dp",
        split_axis=0,
        concat_axis=0,
        tiled=True,
    ).astype(jnp.float32)
    pooled = jnp.take(pooled_back, own_slots, axis=0)
    pool_arrived = lax.all_to_all(
        pack_rows(pool_grad, send_pos, send_fill), "dp", split_axis=0, concat_axis=0, tiled=True
    )
    pool_rows = jnp.take(pool_arrived, recv_pos, axis=0)
    grad_final = out_grad.astype(f32) + jnp.einsum(
        "rsg,rgd->rsd", member, pool_rows / counts[:, :, None], precision=lax.Precision.HIGHEST
    )
    grad_mix = norm_back(grad_final * gain_ffn, hat_ffn, inv_ffn)
    grad_gain_ffn = jnp.sum(grad_final * hat_ffn, axis=(0, 1))
    grad_bias_ffn = jnp.sum(grad_final, axis=(0, 1))
    grad_b_down = jnp.sum(grad_mix, axis=(0, 1))
    mix_low = grad_mix.astype(bf16)
    grad_w_down = jnp.einsum("rsf,rsd->fd", active_low, mix_low, preferred_element_type=f32)
    grad_active = jnp.einsum("rsd,fd->rsf", mix_low, w_down, preferred_element_type=f32)
    grad_hidden = gelu_back(grad_active)[0].astype(bf16)
    grad_w_in = jnp.einsum("rsd,rsf->df", normed_all, grad_hidden, preferred_element_type=f32)
    grad_b_in = jnp.sum(grad_hidden.astype(f32), axis=(0, 1))
    normed_part = jnp.einsum("rsf,df->rsd", grad_hidden, w_in, preferred_element_type=f32)
    grad_normed = lax.psum_scatter(normed_part, "mp", scatter_dimension=1, tiled=True) + own_part(
        grad_mix
    )
    gain_attn_part = jnp.sum(grad_normed * hat_attn, axis=(0, 1))
    bias_attn_part = jnp.sum(grad_normed, axis=(0, 1))
    grad_inner = norm_back(grad_normed * gain_attn, hat_attn, inv_attn)
    stat_terms = jnp.stack([jnp.sum(grad_inner, axis=(0, 1)), gain_attn_part, bias_attn_part])[None]
    inner_all, stats_all = (
        lax.all_gather(grad_inner.astype(jnp.bfloat16), "mp", axis=1, tiled=True).astype(
            grad_inner.dtype
        ),
        lax.all_gather(stat_terms.astype(jnp.bfloat16), "mp", axis=0, tiled=True).astype(
            stat_terms.dtype
        ),
    )
    stat_sums = jnp.sum(stats_all, axis=0)
    inner_low = inner_all.astype(bf16)
    grad_w_out = jnp.einsum("rsf,rsd->fd", attended, inner_low, preferred_element_type=f32)
    grad_attended = (
        jnp.einsum("rsd,fd->rsf", inner_low, w_out, preferred_element_type=f32)
        .astype(bf16)
        .reshape(head_shape)
    )
    again = jnp.exp(scores_of() - log_total)
    grad_prob = jnp.einsum(
        "rqhe,rkhe->rhqk", grad_attended, value_heads, preferred_element_type=f32
    )
    grad_values = jnp.einsum(
        "rhqk,rqhe->rkhe", again.astype(bf16), grad_attended, preferred_element_type=f32
    )
    grad_scores = (again * (grad_prob - jnp.sum(grad_prob * again, axis=-1, keepdims=True))).astype(
        bf16
    )
    grad_query = (
        jnp.einsum("rhqk,rkhe->rqhe", grad_scores, key_heads, preferred_element_type=f32) * factor
    ).astype(bf16)
    grad_keys = (
        jnp.einsum("rhqk,rqhe->rkhe", grad_scores, query_heads, preferred_element_type=f32) * factor
    ).astype(bf16)
    flat_shape = (row_local, full_len, head_width)
    grad_mixed = jnp.stack(
        [
            grad_query.reshape(flat_shape),
            grad_keys.reshape(flat_shape),
            grad_values.astype(bf16).reshape(flat_shape),
        ],
        axis=2,
    )
    grad_w_qkv = jnp.einsum("rsd,rscf->dcf", gathered, grad_mixed, preferred_element_type=f32)
    grad_b_qv = jnp.stack(
        [
            jnp.sum(grad_mixed[:, :, 0].astype(f32), axis=(0, 1)),
            jnp.sum(grad_mixed[:, :, 2].astype(f32), axis=(0, 1)),
        ]
    )
    input_part = jnp.einsum("rscf,dcf->rsd", grad_mixed, w_qkv, preferred_element_type=f32)
    grad_rows = (
        lax.psum_scatter(input_part, "mp", scatter_dimension=1, tiled=True) + grad_inner
    ).astype(bf16)
    grad_home = lax.all_to_all(
        pack_rows(grad_rows, back_pos, back_fill), "dp", split_axis=0, concat_axis=0, tiled=True
    )
    grad_input = jnp.take(grad_home, own_slots, axis=0)
    vector_grads = jnp.stack(
        [stat_sums[0], stat_sums[1], stat_sums[2], grad_b_down, grad_gain_ffn, grad_bias_ffn]
    )
    totals = lax.psum(
        (grad_w_qkv, grad_b_qv, grad_w_out, grad_w_in, grad_b_in, grad_w_down, vector_grads), "dp"
    )
    return (
        output_rows,
        pooled,
        grad_input,
        totals[0],
        totals[1],
        totals[2],
        totals[6][0],
        totals[6][1],
        totals[6][2],
        totals[3],
        totals[4],
        totals[5],
        totals[6][3],
        totals[6][4],
        totals[6][5],
    )


VM = pl.BlockSpec(memory_space=pltpu.VMEM)
SM = pl.BlockSpec(memory_space=pltpu.SMEM)
HB = pl.BlockSpec(memory_space=pl.ANY)
HM = pl.BlockSpec(memory_space=pltpu.HBM)
ROOM = 48 * 1024 * 1024


def shape_of(shape, dtype=bf16):
    return jax.ShapeDtypeStruct(shape, dtype)


def call(
    body, outs, out_specs, in_specs, scratch=(), us=2, room=ROOM, name=None, after=()
):
    n, extra = len(in_specs), len(after)

    def trimmed(*refs):
        body(*refs[:n], *refs[n + extra :])

    made = pl.pallas_call(
        trimmed,
        out_shape=outs,
        in_specs=list(in_specs) + [HB] * extra,
        out_specs=out_specs,
        scratch_shapes=list(scratch),
        compiler_params=pltpu.CompilerParams(vmem_limit_bytes=room),
        cost_estimate=pl.CostEstimate(flops=int(us * 1.15e9), bytes_accessed=0, transcendentals=0),
        name=name,
    )
    return lambda *args: made(*args, *after)


def mm(a, b):
    return lax.dot_general(a, b, (((1,), (0,)), ((), ())), preferred_element_type=f32)


def mm_nt(a, b):
    return lax.dot_general(a, b, (((1,), (1,)), ((), ())), preferred_element_type=f32)


def mm_tn(a, b):
    return lax.dot_general(a, b, (((0,), (0,)), ((), ())), preferred_element_type=f32)


def split3(values):
    high = values.astype(bf16)
    rest = values - high.astype(f32)
    middle = rest.astype(bf16)
    low = (rest - middle.astype(f32)).astype(bf16)
    return high, middle, low


def prep_rows(sent, tokens, b_qv, b_in, dims):
    devices, count, rows, quarter, full, width = dims
    here = rows // count
    head_width = b_qv.shape[1]
    tile = here * quarter

    def body(sent_ref, tok, bqv_ref, bin_ref, x0, x1, x2, x3, extra, sems):
        xs = (x0, x1, x2, x3)
        copies = []
        for kk in reversed(range(count)):
            for j in range(here):
                at = kk * here + j
                copies.append(
                    pltpu.make_async_copy(
                        tok.at[sent_ref[at]], xs[kk].at[pl.ds(j * quarter, quarter)], sems.at[at]
                    )
                )
        for copy in copies:
            copy.start()
        extra[...] = jnp.zeros_like(extra)
        for j, term in enumerate(split3(bqv_ref[...])):
            extra[j : j + 1, 0:head_width] = term[0:1]
            extra[j : j + 1, 256 : 256 + head_width] = term[1:2]
        for j, term in enumerate(split3(bin_ref[...])):
            extra[3 + j : 4 + j, :] = term
        tails = [
            pltpu.make_async_copy(extra, xs[kk].at[pl.ds(tile, 16)], sems.at[rows + kk])
            for kk in range(count)
        ]
        for copy in tails:
            copy.start()
        for copy in copies + tails:
            copy.wait()

    return call(
        body,
        [shape_of((tile + 16, width))] * count,
        [HB] * count,
        [SM, HM, VM, VM],
        [pltpu.VMEM((16, width), bf16), pltpu.SemaphoreType.DMA((rows + count,))],
        us=2,
        name="prep_rows",
    )(sent, tokens, b_qv, b_in.reshape(1, -1))


def prep_halves(ids, w_q, w_out, w_in, w_down, after):
    width = w_q.shape[1]
    halves = [w.shape[0] // 2 for w in (w_q, w_out, w_in, w_down)]

    def body(ids_ref, wq, wo, wi, wd, q, oi, dn, sems):
        parity = ids_ref[2]

        def copy(src, half, dst, at):
            return pltpu.make_async_copy(
                src.at[pl.ds(pl.multiple_of(parity * half, 16), half)], dst, sems.at[at]
            )

        copies = [
            copy(wq, halves[0], q, 0),
            copy(wo, halves[1], oi.at[pl.ds(0, halves[1])], 1),
            copy(wi, halves[2], oi.at[pl.ds(halves[1], halves[2])], 2),
            copy(wd, halves[3], dn, 3),
        ]
        for c in copies:
            c.start()
        for c in copies:
            c.wait()

    return call(
        body,
        [
            shape_of((halves[0], width)),
            shape_of((halves[1] + halves[2], width)),
            shape_of((halves[3], width)),
        ],
        [VM] * 3,
        [SM] + [HM] * 4,
        [pltpu.SemaphoreType.DMA((4,))],
        us=2,
        name="prep_halves",
        after=after,
    )(ids, w_q, w_out, w_in, w_down)


def prep_cot(asked, out_grad, dims, after):
    devices, count, rows, quarter, full, width = dims
    cap, reach = rows // devices, devices // count

    def body(asked_ref, og, *refs):
        outs, sems = refs[:reach], refs[reach]
        copies = []
        for k in range(reach):
            for c in range(cap):
                at = k * cap + c
                copies.append(
                    pltpu.make_async_copy(og.at[asked_ref[at]], outs[k].at[c], sems.at[at])
                )
        for copy in copies:
            copy.start()
        for copy in copies:
            copy.wait()

    return call(
        body,
        [shape_of((cap, full, width))] * reach,
        [HB] * reach,
        [SM, HM],
        [pltpu.SemaphoreType.DMA((reach * cap,))],
        us=2,
        name="prep_cot",
        after=after,
    )(asked, out_grad)


def bias_rows(piece, at, count):
    terms = piece[at : at + 16, :].astype(f32)
    first = 0 if count == 0 else 3
    return terms[first : first + 1] + terms[first + 1 : first + 2] + terms[first + 2 : first + 3]


def head_masks(head_width):
    lane = lax.broadcasted_iota(jnp.int32, (1, head_width), 1)
    return [(lane >= h * HD) & (lane < (h + 1) * HD) for h in range(head_width // HD)]


def stack_heads(values, masks):
    zero = jnp.zeros_like(values)
    return jnp.concatenate([jnp.where(mask, values, zero) for mask in masks], axis=0)


def pick_heads(stacked, masks):
    size = stacked.shape[0] // len(masks)
    out = stacked[:size]
    for h in range(1, len(masks)):
        out = jnp.where(masks[h], stacked[h * size : (h + 1) * size], out)
    return out


def load_parts(parts, parity, half, dst, offset, sems, at):
    if len(parts) == 1:
        return [pltpu.make_async_copy(parts[0], dst.at[pl.ds(offset, 2 * half)], sems.at[at])]
    first = pl.multiple_of(parity * half, 16)
    second = pl.multiple_of((1 - parity) * half, 16)
    return [
        pltpu.make_async_copy(parts[0], dst.at[pl.ds(offset + first, half)], sems.at[at]),
        pltpu.make_async_copy(parts[1], dst.at[pl.ds(offset + second, half)], sems.at[at + 1]),
    ]


def attend(ids, segr, pieces, parts, pair, dims, keep_x, after=()):
    devices, count, rows, quarter, full, width = dims
    here = rows // count
    tokens = here * full
    tile = here * quarter
    inner = sum(ref.shape[0] for ref in parts[0])
    head_width = inner // 3
    n_heads = head_width // HD
    n_parts = [len(p) for p in parts]
    flat = [ref for p in parts for ref in p]

    def body(ids_ref, segr_ref, *refs):
        piece_refs = refs[:count]
        w_refs = refs[count : count + len(flat)]
        out = list(refs[count + len(flat) :])
        if keep_x:
            x_out = out.pop(0)
        ol_out, qkv_out, p_out, x_ref, w_ref, sems = out
        copies = []
        at = 0
        for b, n in enumerate(n_parts):
            copies += load_parts(
                w_refs[at : at + n], ids_ref[2], inner // 2, w_ref.at[b], 0, sems, at
            )
            at += n
        for copy in copies:
            copy.start()
        for r in range(here):
            for kk in range(count):
                x_ref[r * full + kk * quarter : r * full + (kk + 1) * quarter, :] = piece_refs[kk][
                    r * quarter : (r + 1) * quarter, :
                ]
        if keep_x:
            x_out[...] = x_ref[...]
        masks = head_masks(head_width)
        for copy in copies:
            copy.wait()
        for b in range(2):
            bias = bias_rows(piece_refs[pair[b]], tile, 0)
            bias_q, bias_v = bias[:, 0:head_width], bias[:, 256 : 256 + head_width]

            @pl.loop(0, here)
            def _(r):
                start = pl.multiple_of(r * full, full)
                projected = mm_nt(x_ref[pl.ds(start, full), :], w_ref[b])
                query = (projected[:, 0:head_width] + bias_q).astype(bf16)
                key = projected[:, head_width : 2 * head_width].astype(bf16)
                value = (projected[:, 2 * head_width :] + bias_v).astype(bf16)
                line = segr_ref[pl.ds(r, 1), :].astype(f32)
                wide = jnp.broadcast_to(line, (full, full))
                allowed = wide == wide.T
                stacked = stack_heads(query, masks)
                raw = mm_nt(stacked, key) * (HD ** -0.5)
                allowed3 = jnp.concatenate([allowed] * n_heads, axis=0)
                scores = jnp.where(allowed3, raw, MASKED)
                raised = jnp.exp(scores - jnp.max(scores, axis=1, keepdims=True))
                prob = raised / jnp.sum(raised, axis=1, keepdims=True)
                low = prob.astype(bf16)
                attended = pick_heads(mm(low, value), masks).astype(bf16)
                ol_out[b, pl.ds(start, full), :] = attended
                qkv_out[b, 0, pl.ds(start, full), :] = query
                qkv_out[b, 1, pl.ds(start, full), :] = key
                qkv_out[b, 2, pl.ds(start, full), :] = value
                p_out[b, r] = low

    outs = [
        shape_of((2, tokens, head_width)),
        shape_of((2, 3, tokens, head_width)),
        shape_of((2, here, n_heads * full, full)),
    ]
    if keep_x:
        outs = [shape_of((tokens, width))] + outs
    return call(
        body,
        outs,
        [VM] * len(outs),
        [SM, VM] + [VM] * count + [HB] * len(flat),
        [
            pltpu.VMEM((tokens, width), bf16),
            pltpu.VMEM((2, inner, width), bf16),
            pltpu.SemaphoreType.DMA((len(flat),)),
        ],
        us=10,
        name="attend",
        after=after,
    )(ids, segr, *pieces, *flat)


def gelu_pair(u):
    z = jnp.abs(u) * (0.5 ** 0.5)
    t = 1.0 / (1.0 + 0.3275911 * z)
    poly = t * (
        0.254829592
        + t * (-0.284496736 + t * (1.421413741 + t * (-1.453152027 + t * 1.061405429)))
    )
    bell = jnp.exp(-0.5 * u * u)
    tail = 0.5 * poly * bell
    cdf = jnp.where(u >= 0, 1.0 - tail, tail)
    return u * cdf, cdf + u * bell * 0.3989422804014327


def norm_rows(values):
    centre = values - jnp.mean(values, axis=1, keepdims=True)
    inverse = lax.rsqrt(jnp.mean(centre * centre, axis=1, keepdims=True) + EPSILON)
    return centre * inverse, inverse


def ffn(ids, sent, segr, x, ols, pieces, vecs, ogs, pool_grad, out_in_parts, down_parts, dims):
    devices, count, rows, quarter, full, width = dims
    here, cap, reach = rows // count, rows // devices, devices // count
    tokens = here * full
    tile = here * quarter
    head_width = ols[0].shape[2]
    hidden = width
    flat_oi = [ref for p in out_in_parts for ref in p]
    flat_dn = [ref for p in down_parts for ref in p]
    n_oi, n_dn = len(flat_oi), len(flat_dn)
    half_out, half_in = head_width // 2, width // 2

    def body(ids_ref, sent_ref, segr_ref, x_ref, ol_a, ol_b, *refs):
        refs = list(refs)
        piece_refs = [refs.pop(0) for _ in range(count)]
        vec_ref = refs.pop(0)
        og_refs = [refs.pop(0) for _ in range(reach)]
        pool_ref = refs.pop(0)
        oi_refs = [refs.pop(0) for _ in range(n_oi)]
        dn_refs = [refs.pop(0) for _ in range(n_dn)]
        (
            al_out, hat_out, inv_out, hl_out, gp_out, tk0, tk1, pooled_out, dz_out, low_out,
            sums_out, down_out,
            wo, wi, wd, og_buf, acc, hl, gp, sems, out_sems,
        ) = refs
        mi, parity = ids_ref[1], ids_ref[2]
        first, later, last = [], [], []
        at = 0
        for kk in range(count):
            own = out_in_parts[kk]
            if len(own) == 2 and own[0].shape[0] == 2 * half_out:
                first.append(
                    pltpu.make_async_copy(oi_refs[at], wo.at[kk], sems.at[2 * at])
                )
                later.append(
                    pltpu.make_async_copy(oi_refs[at + 1], wi.at[kk], sems.at[2 * at + 2])
                )
            else:
                for j in range(2):
                    place = parity if j == 0 else 1 - parity
                    src = oi_refs[at + j]
                    first.append(
                        pltpu.make_async_copy(
                            src.at[pl.ds(0, half_out)],
                            wo.at[kk, pl.ds(pl.multiple_of(place * half_out, 16), half_out)],
                            sems.at[2 * (at + j)],
                        )
                    )
                    later.append(
                        pltpu.make_async_copy(
                            src.at[pl.ds(half_out, half_in)],
                            wi.at[kk, pl.ds(pl.multiple_of(place * half_in, 16), half_in)],
                            sems.at[2 * (at + j) + 1],
                        )
                    )
            at += 2
        base = 2 * n_oi
        at = 0
        for kk in range(count):
            n = len(down_parts[kk])
            last += load_parts(dn_refs[at : at + n], parity, width // 2, wd.at[kk], 0, sems, base + at)
            at += n
        base += n_dn
        pool_at = base
        cots = []
        for k in range(reach):
            for c in range(cap):
                r = k * cap + c
                for kk in range(count):
                    cots.append(
                        pltpu.make_async_copy(
                            og_refs[k].at[c, pl.ds(pl.multiple_of((mi ^ kk) * quarter, quarter), quarter)],
                            og_buf.at[pl.ds(r * full + kk * quarter, quarter)],
                            sems.at[pool_at + r * count + kk],
                        )
                    )
        for copy in first + later + last + cots:
            copy.start()
        b_out, gain_a, bias_a = vec_ref[0:1], vec_ref[1:2], vec_ref[2:3]
        b_down, gain_f, bias_f = vec_ref[3:4], vec_ref[4:5], vec_ref[5:6]
        for copy in first:
            copy.wait()

        @pl.loop(0, here)
        def _(r):
            span = pl.ds(pl.multiple_of(r * full, full), full)
            total = x_ref[span, :].astype(f32) + b_out
            for kk in range(count):
                ol = (ol_a, ol_b)[kk // 2]
                total = total + mm(ol[kk % 2, span, :], wo[kk])
            hat, inverse = norm_rows(total)
            hat_out[span, :] = hat
            inv_out[span, :] = jnp.broadcast_to(inverse, (full, 128))
            al_out[span, :] = (hat * gain_a + bias_a).astype(bf16)

        for copy in later + last:
            copy.wait()
        half = tokens // 2
        outs = []
        for kk in range(count):
            bias = bias_rows(piece_refs[kk], tile, 3)
            for m in range(2):
                span = slice(m * half, (m + 1) * half)
                u = mm(al_out[span, :], wi[kk]) + bias
                active, slope = gelu_pair(u)
                active = active.astype(bf16)
                hl[kk, span, :] = active
                gp[kk, span, :] = slope.astype(bf16)
                part = mm(active, wd[kk])
                if kk == 0:
                    acc[span, :] = part
                else:
                    acc[span, :] += part
            for j, (src, dst) in enumerate(((hl, hl_out), (gp, gp_out))):
                copy = pltpu.make_async_copy(src.at[kk], dst.at[kk], out_sems.at[2 * kk + j])
                copy.start()
                outs.append(copy)
        for copy in cots:
            copy.wait()
        sums_out[...] = jnp.zeros_like(sums_out)
        for r in range(here):
            span = slice(r * full, (r + 1) * full)
            hat, inverse = norm_rows(al_out[span, :].astype(f32) + acc[span, :] + b_down)
            final = hat * gain_f + bias_f
            (tk0, tk1)[r // cap][r % cap] = final.astype(bf16)
            line = jnp.broadcast_to(segr_ref[r : r + 1, :].astype(f32), (full, full)).T[:, 0:1]
            cot = og_buf[span, :].astype(f32)
            row = sent_ref[r]
            for g in range(SEGS):
                inside = line == float(g)
                number = jnp.sum(jnp.where(inside, 1.0, 0.0), axis=0, keepdims=True)
                share = 1.0 / number
                pooled_out[r * SEGS + g : r * SEGS + g + 1, :] = (
                    jnp.sum(jnp.where(inside, final, 0.0), axis=0, keepdims=True) * share
                )
                cot = cot + jnp.where(inside, pool_ref[row, g : g + 1, :] * share, 0.0)
            e = cot * gain_f
            mean_e = jnp.mean(e, axis=1, keepdims=True)
            mean_p = jnp.mean(e * hat, axis=1, keepdims=True)
            dz = inverse * (e - mean_e - hat * mean_p)
            dz_out[span, :] = dz
            low_out[span, :] = dz.astype(bf16)
            sums_out[0:1, :] += jnp.sum(dz, axis=0, keepdims=True)
            sums_out[1:2, :] += jnp.sum(cot * hat, axis=0, keepdims=True)
            sums_out[2:3, :] += jnp.sum(cot, axis=0, keepdims=True)
        for b, kk in enumerate((1, 3)):
            for c in range(3):
                cols = slice(c * 256, (c + 1) * 256)
                down_out[b, cols, :] = mm_tn(hl[kk, :, cols], low_out[...]).astype(bf16)
        for copy in outs:
            copy.wait()

    wide = (tokens, width)
    return call(
        body,
        [
            shape_of(wide), shape_of(wide, f32), shape_of((tokens, 128), f32),
            shape_of((count,) + wide), shape_of((count,) + wide),
            shape_of((cap, full, width)), shape_of((cap, full, width)),
            shape_of((here * SEGS, width), f32), shape_of(wide, f32), shape_of(wide),
            shape_of((8, width), f32), shape_of((2, hidden, width)),
        ],
        [VM, VM, VM, HB, HB] + [VM] * 7,
        [SM, SM, VM, VM, VM, VM] + [VM] * count + [VM] + [HB] * reach + [VM] + [HB] * (n_oi + n_dn),
        [
            pltpu.VMEM((count, head_width, width), bf16),
            pltpu.VMEM((count, width, hidden), bf16),
            pltpu.VMEM((count, hidden, width), bf16),
            pltpu.VMEM(wide, bf16),
            pltpu.VMEM(wide, f32),
            pltpu.VMEM((count,) + wide, bf16),
            pltpu.VMEM((count,) + wide, bf16),
            pltpu.SemaphoreType.DMA((2 * n_oi + n_dn + here * count,)),
            pltpu.SemaphoreType.DMA((2 * count,)),
        ],
        us=20,
        name="ffn",
    )(ids, sent, segr, x, ols[0], ols[1], *pieces, vecs, *ogs, pool_grad, *flat_oi, *flat_dn)


def ffn_back(ids, low, gp, al, down_parts, dims):
    devices, count, rows, quarter, full, width = dims
    tokens = low.shape[0]
    hidden = width
    flat = [ref for p in down_parts for ref in p]
    n = len(flat)

    def body(ids_ref, low_ref, gp_ref, al_ref, *refs):
        dn_refs = refs[:n]
        du_out, in_out, bin_out, wd, gpb, du, sems, out_sems = refs[n:]
        copies = []
        at = 0
        for kk in range(count):
            m = len(down_parts[kk])
            copies.append(
                load_parts(dn_refs[at : at + m], ids_ref[2], width // 2, wd.at[kk], 0, sems, at)
                + [pltpu.make_async_copy(gp_ref.at[kk], gpb.at[kk], sems.at[n + kk])]
            )
            at += m
        outs = []
        turn = (1, 3, 2, 0)
        for kk in turn:
            for copy in copies[kk]:
                copy.start()
        half = tokens // 2
        for kk in turn:
            for copy in copies[kk]:
                copy.wait()
            total = jnp.zeros((1, hidden), f32)
            for m in range(2):
                span = slice(m * half, (m + 1) * half)
                part = (mm_nt(low_ref[span, :], wd[kk]) * gpb[kk, span, :].astype(f32)).astype(bf16)
                du[kk, span, :] = part
                total = total + jnp.sum(part.astype(f32), axis=0, keepdims=True)
            bin_out[kk : kk + 1, :] = total
            copy = pltpu.make_async_copy(du.at[kk], du_out.at[kk], out_sems.at[kk])
            copy.start()
            outs.append(copy)
        for b, kk in enumerate((1, 3)):
            for c in range(3):
                cols = slice(c * 256, (c + 1) * 256)
                in_out[b, cols, :] = mm_tn(al_ref[:, cols], du[kk]).astype(bf16)
        for copy in outs:
            copy.wait()

    return call(
        body,
        [
            shape_of((count, tokens, hidden)),
            shape_of((2, width, hidden)),
            shape_of((count, hidden), f32),
        ],
        [HB, VM, VM],
        [SM, VM, HB, VM] + [HB] * n,
        [
            pltpu.VMEM((count, hidden, width), bf16),
            pltpu.VMEM((count, tokens, hidden), bf16),
            pltpu.VMEM((count, tokens, hidden), bf16),
            pltpu.SemaphoreType.DMA((n + count,)),
            pltpu.SemaphoreType.DMA((count,)),
        ],
        us=9,
        name="ffn_back",
    )(ids, low, gp, al, *flat)


def norm_back_attn(ids, du, al, dz, hat, inv, vecs, out_in_parts, dims, half_out, after=()):
    devices, count, rows, quarter, full, width = dims
    tokens = al.shape[0]
    hidden = width
    flat = [ref for p in out_in_parts for ref in p]
    n = len(flat)
    half_in = width // 2

    def body(ids_ref, du_ref, dz_ref, hat_ref, inv_ref, vec_ref, *refs):
        oi_refs = refs[:n]
        dz1_out, low_out, sums_out, wi, dub, acc, sems = refs[n:]
        parity = ids_ref[2]
        copies = []
        at = 0
        for kk in range(count):
            own = out_in_parts[kk]
            group = [pltpu.make_async_copy(du_ref.at[kk], dub.at[kk], sems.at[2 * n + kk])]
            if len(own) == 1:
                group.append(pltpu.make_async_copy(oi_refs[at], wi.at[kk], sems.at[2 * at]))
            else:
                for j in range(2):
                    place = parity if j == 0 else 1 - parity
                    group.append(
                        pltpu.make_async_copy(
                            oi_refs[at + j].at[pl.ds(half_out, half_in)],
                            wi.at[kk, pl.ds(pl.multiple_of(place * half_in, 16), half_in)],
                            sems.at[2 * (at + j)],
                        )
                    )
            at += len(own)
            copies.append(group)
        for group in copies:
            for copy in group:
                copy.start()
        half = tokens // 2
        for kk in range(count):
            for copy in copies[kk]:
                copy.wait()
            for m in range(2):
                span = slice(m * half, (m + 1) * half)
                part = mm_nt(dub[kk, span, :], wi[kk])
                if kk == 0:
                    acc[span, :] = part + dz_ref[span, :]
                else:
                    acc[span, :] += part
        gain_a = vec_ref[1:2]
        sums_out[...] = jnp.zeros_like(sums_out)

        @pl.loop(0, tokens // full)
        def _(r):
            span = pl.ds(pl.multiple_of(r * full, full), full)
            da = acc[span, :]
            hat_r = hat_ref[span, :]
            e = da * gain_a
            mean_e = jnp.mean(e, axis=1, keepdims=True)
            mean_p = jnp.mean(e * hat_r, axis=1, keepdims=True)
            dz1 = inv_ref[span, 0:1] * (e - mean_e - hat_r * mean_p)
            dz1_out[span, :] = dz1
            low_out[span, :] = dz1.astype(bf16)
            sums_out[0:1, :] += jnp.sum(dz1, axis=0, keepdims=True)
            sums_out[1:2, :] += jnp.sum(da * hat_r, axis=0, keepdims=True)
            sums_out[2:3, :] += jnp.sum(da, axis=0, keepdims=True)

    wide = (tokens, width)
    return call(
        body,
        [shape_of(wide, f32), shape_of(wide), shape_of((8, width), f32)],
        [VM] * 3,
        [SM, HB, VM, VM, VM, VM] + [HB] * n,
        [
            pltpu.VMEM((count, width, hidden), bf16),
            pltpu.VMEM((count, tokens, hidden), bf16),
            pltpu.VMEM(wide, f32),
            pltpu.SemaphoreType.DMA((2 * n + count,)),
        ],
        us=8,
        name="norm_back",
        after=after,
    )(ids, du, dz, hat, inv, vecs, *flat)


def attend_back(ids, low, x, blocks, extras, dims, after=()):
    devices, count, rows, quarter, full, width = dims
    here = rows // count
    tokens = x.shape[0]
    head_width = blocks[0][2].shape[2]
    inner = 3 * head_width
    flat = [ref for b in blocks for ref in b[5]]
    n = len(flat)
    half_out = head_width // 2
    nb = len(blocks)

    def body(ids_ref, low_ref, x_ref, bin_ref, ffn_ref, norm_ref, *refs):
        data = refs[: 3 * nb]
        w_refs = refs[3 * nb : 3 * nb + n]
        mix_out, grad_out, wo, sums, sems = refs[3 * nb + n :]
        parity = ids_ref[2]
        copies = []
        at = 0
        for b in range(nb):
            own = blocks[b][5]
            if len(own) == 1:
                copies.append(pltpu.make_async_copy(w_refs[at], wo.at[b], sems.at[at]))
            else:
                for j in range(2):
                    place = parity if j == 0 else 1 - parity
                    copies.append(
                        pltpu.make_async_copy(
                            w_refs[at + j].at[pl.ds(0, half_out)],
                            wo.at[b, pl.ds(pl.multiple_of(place * half_out, 16), half_out)],
                            sems.at[at + j],
                        )
                    )
            at += len(own)
        for copy in copies:
            copy.start()
        for copy in copies:
            copy.wait()
        masks = head_masks(head_width)
        sums[...] = jnp.zeros_like(sums)
        for b in range(nb):
            kk, place = blocks[b][:2]
            ol_ref, qkv_ref, p_ref = data[3 * b : 3 * b + 3]

            @pl.loop(0, here)
            def _(r):
                span = pl.ds(pl.multiple_of(r * full, full), full)
                dol = mm_nt(low_ref[span, :], wo[b]).astype(bf16)
                query, key, value = (qkv_ref[place, i, span, :] for i in range(3))
                low_p = p_ref[place, r]
                prob = low_p.astype(f32)
                dos = stack_heads(dol, masks)
                dp = mm_nt(dos, value)
                ds = (prob * (dp - jnp.sum(dp * prob, axis=1, keepdims=True))).astype(bf16)
                dv = mm_tn(low_p, dos).astype(bf16)
                dq = (pick_heads(mm(ds, key), masks) * (HD ** -0.5)).astype(bf16)
                dk = (mm_tn(ds, stack_heads(query, masks)) * (HD ** -0.5)).astype(bf16)
                mix_out[b, span, 0:head_width] = dq
                mix_out[b, span, head_width : 2 * head_width] = dk
                mix_out[b, span, 2 * head_width :] = dv
                sums[b : b + 1, 0:head_width] += jnp.sum(dq.astype(f32), axis=0, keepdims=True)
                sums[b : b + 1, 256 : 256 + head_width] += jnp.sum(
                    dv.astype(f32), axis=0, keepdims=True
                )

            for c in range(3):
                part = slice(c * head_width, (c + 1) * head_width)
                grad_out[b, part, :] = mm_tn(mix_out[b, :, part], x_ref[...]).astype(bf16)
            grad_out[b, inner:width, :] = mm_tn(ol_ref[place], low_ref[...]).astype(bf16)
            lines = jnp.concatenate(
                [sums[b : b + 1], bin_ref[kk : kk + 1], norm_ref[0:3], ffn_ref[0:3]], axis=0
            )
            grad_out[b, width : width + 16, :] = two_terms(lines)

    return call(
        body,
        [shape_of((nb, tokens, inner)), shape_of((nb, width + 16, width))],
        [VM] * 2,
        [SM] + [VM] * (5 + 3 * nb) + [HB] * n,
        [
            pltpu.VMEM((nb, head_width, width), bf16),
            pltpu.VMEM((8, width), f32),
            pltpu.SemaphoreType.DMA((n,)),
        ],
        us=13,
        name="attend_back",
        after=after,
    )(ids, low, x, *extras, *[v for b in blocks for v in b[2:5]], *flat)


def two_terms(lines):
    high = lines.astype(bf16)
    return jnp.concatenate([high, (lines - high.astype(f32)).astype(bf16)], axis=0)


def one_term(lines):
    return lines[0:8].astype(f32) + lines[8:16].astype(f32)


def peer_grad(lhs, rhs, got, after=()):
    tokens, width = rhs.shape
    hidden = lhs.shape[-1]

    def body(lhs_ref, rhs_ref, got_ref, out, a_buf, g_buf, sems):
        copies = [
            pltpu.make_async_copy(lhs_ref.at[2], a_buf, sems.at[0]),
            pltpu.make_async_copy(got_ref.at[1], g_buf, sems.at[1]),
        ]
        for copy in copies:
            copy.start()
        for copy in copies:
            copy.wait()
        for c in range(hidden // 256):
            cols = slice(c * 256, (c + 1) * 256)
            out[cols, :] = (mm_tn(a_buf[:, cols], rhs_ref[...]) + g_buf[cols, :].astype(f32)).astype(
                bf16
            )

    return call(
        body,
        shape_of((hidden, width)),
        VM,
        [HB, VM, HB],
        [
            pltpu.VMEM((tokens, hidden), bf16),
            pltpu.VMEM((hidden, width), bf16),
            pltpu.SemaphoreType.DMA((2,)),
        ],
        us=3,
        name="peer_grad",
        after=after,
    )(lhs, rhs, got)


def shards(acc, ids_ref, devices, bits, size, send, keep):
    for p in range(devices):
        mirror = sum(((p >> j) & 1) << (bits - 1 - j) for j in range(bits))
        rows = acc[pl.ds(pl.multiple_of((ids_ref[0] ^ mirror) * size, 16), size), :]
        if p < devices // 2:
            keep[p * size : (p + 1) * size, :] = rows
        else:
            q = p - devices // 2
            send[q * size : (q + 1) * size, :] = rows.astype(bf16)


def own_grad(ids, lhs, rhs, got, crossed, devices, lhs_own, after=()):
    tokens = rhs.shape[-2]
    width = rhs.shape[-1]
    hidden = lhs.shape[-1]
    bits = devices.bit_length() - 1
    size = hidden // devices

    def body(ids_ref, lhs_ref, rhs_ref, got_ref, cross_ref, send, keep, a_buf, b_buf, g_buf, acc, sems):
        copies = [
            pltpu.make_async_copy(lhs_ref.at[0] if lhs_own else lhs_ref, a_buf, sems.at[0]),
            pltpu.make_async_copy(rhs_ref if lhs_own else rhs_ref.at[0], b_buf, sems.at[1]),
            pltpu.make_async_copy(got_ref.at[0], g_buf, sems.at[2]),
        ]
        for copy in copies:
            copy.start()
        for copy in copies:
            copy.wait()
        for c in range(hidden // 256):
            cols = slice(c * 256, (c + 1) * 256)
            acc[cols, :] = (
                mm_tn(a_buf[:, cols], b_buf[...])
                + g_buf[cols, :].astype(f32)
                + cross_ref[cols, :].astype(f32)
            )
        shards(acc, ids_ref, devices, bits, size, send, keep)

    return call(
        body,
        [shape_of((hidden // 2, width)), shape_of((hidden // 2, width), f32)],
        [VM, VM],
        [SM, HB, HB, HB, VM],
        [
            pltpu.VMEM((tokens, hidden), bf16),
            pltpu.VMEM((tokens, width), bf16),
            pltpu.VMEM((hidden, width), bf16),
            pltpu.VMEM((hidden, width), f32),
            pltpu.SemaphoreType.DMA((3,)),
        ],
        us=3,
        name="own_grad",
        after=after,
    )(ids, lhs, rhs, got, crossed)


def peer_grad_in(al, du, got, after=()):
    tokens, width = al.shape
    hidden = du.shape[-1]

    def body(al_ref, du_ref, got_ref, out, b_buf, g_buf, sems):
        copies = [
            pltpu.make_async_copy(du_ref.at[2], b_buf, sems.at[0]),
            pltpu.make_async_copy(got_ref.at[1], g_buf, sems.at[1]),
        ]
        for copy in copies:
            copy.start()
        for copy in copies:
            copy.wait()
        for c in range(width // 256):
            cols = slice(c * 256, (c + 1) * 256)
            out[cols, :] = (mm_tn(al_ref[:, cols], b_buf[...]) + g_buf[cols, :].astype(f32)).astype(
                bf16
            )

    return call(
        body,
        shape_of((width, hidden)),
        VM,
        [VM, HB, HB],
        [
            pltpu.VMEM((tokens, hidden), bf16),
            pltpu.VMEM((width, hidden), bf16),
            pltpu.SemaphoreType.DMA((2,)),
        ],
        us=3,
        name="peer_grad_in",
        after=after,
    )(al, du, got)


def peer_last(grads, got, at, after=()):
    _, high, width = grads.shape

    def body(a_ref, g_ref, out):
        out[0 : high - 16, :] = (
            a_ref[at, 0 : high - 16, :].astype(f32) + g_ref[1, 0 : high - 16, :].astype(f32)
        ).astype(bf16)
        out[high - 16 :, :] = two_terms(
            one_term(a_ref[at, high - 16 :, :]) + one_term(g_ref[1, high - 16 :, :])
        )

    return call(
        body, shape_of((high, width)), VM, [VM, VM], us=2, name="peer_last", after=after
    )(grads, got)


def own_last(ids, grads, got, crossed, at, devices, after=()):
    _, high, width = grads.shape
    body_rows = high - 16
    bits = devices.bit_length() - 1
    size = body_rows // devices

    def body(ids_ref, a_ref, g_ref, c_ref, send, keep, vec, acc):
        acc[...] = (
            a_ref[at, 0:body_rows, :].astype(f32)
            + g_ref[0, 0:body_rows, :].astype(f32)
            + c_ref[0:body_rows, :].astype(f32)
        )
        shards(acc, ids_ref, devices, bits, size, send, keep)
        lines = (
            one_term(a_ref[at, body_rows:, :])
            + one_term(g_ref[0, body_rows:, :])
            + one_term(c_ref[body_rows:, :])
        )
        send[body_rows // 2 :, :] = two_terms(lines)
        vec[...] = lines

    return call(
        body,
        [
            shape_of((body_rows // 2 + 16, width)),
            shape_of((body_rows // 2, width), f32),
            shape_of((8, width), f32),
        ],
        [VM] * 3,
        [SM, VM, VM, VM],
        [pltpu.VMEM((body_rows, width), f32)],
        us=3,
        name="own_last",
        after=after,
    )(ids, grads, got, crossed)


def halve(keep, got, vec=None):
    high, width = keep.shape
    last = vec is not None
    tail = 16 if last else 0
    return_send = True

    def body(*refs):
        keep_ref, got_ref = refs[:2]
        rest = refs[2:]
        if last:
            vec_ref, rest = rest[0], rest[1:]
        send, kept = rest[:2]
        half = high // 2
        kept[...] = keep_ref[0:half, :] + got_ref[0:half, :].astype(f32)
        send[0:half, :] = (keep_ref[half:, :] + got_ref[half:high, :].astype(f32)).astype(bf16)
        if last:
            lines = vec_ref[...] + one_term(got_ref[high:, :])
            send[half:, :] = two_terms(lines)
            rest[2][...] = lines

    outs = [shape_of((high // 2 + tail, width)), shape_of((high // 2, width), f32)]
    args = [keep, got]
    if last:
        outs.append(shape_of((8, width), f32))
        args.append(vec)
    return call(
        body, outs, [VM] * len(outs), [VM] * len(args), us=1, name="halve"
    )(*args)


def end_halving(keep, got, vec=None):
    high, width = keep.shape
    last = vec is not None

    def body(*refs):
        keep_ref, got_ref = refs[:2]
        rest = refs[2:]
        if last:
            vec_ref, rest = rest[0], rest[1:]
        rest[0][...] = (keep_ref[...] + got_ref[0:high, :].astype(f32)).astype(bf16)
        if last:
            rest[1][...] = vec_ref[...] + one_term(got_ref[high:, :])

    outs = [shape_of((high, width))]
    args = [keep, got]
    if last:
        outs.append(shape_of((8, width), f32))
        args.append(vec)
    return call(
        body, outs, [VM] * len(outs), [VM] * len(args), us=1, name="end_halving"
    )(*args)


def reduce_dp(send, keep, vec, devices):
    bits = devices.bit_length() - 1
    for j in range(bits - 1):
        got = swap(send, "dp", 1 << j)
        out = halve(keep, got, vec)
        send, keep = out[:2]
        vec = out[2] if vec is not None else None
    got = swap(send, "dp", 1 << (bits - 1))
    out = end_halving(keep, got, vec)
    pieces = [out[0]]
    for j in reversed(range(bits)):
        whole = pieces[0] if len(pieces) == 1 else jnp.concatenate(pieces, axis=0)
        pieces.append(swap(whole, "dp", 1 << j))
    return pieces, (out[1] if vec is not None else None)


def place_shards(ids_ref, pieces, devices, size, put):
    bits = devices.bit_length() - 1
    p = 0
    for piece in pieces:
        for q in range(piece.shape[0] // size):
            mirror = sum(((p >> j) & 1) << (bits - 1 - j) for j in range(bits))
            at = pl.multiple_of((ids_ref[0] ^ mirror) * size, 8)
            put(at, piece[q * size : (q + 1) * size, :].astype(f32))
            p += 1


def whole_grad(ids, pieces, devices):
    size, width = pieces[0].shape
    n = len(pieces)

    def body(ids_ref, *refs):
        out = refs[n]

        def put(at, rows):
            out[pl.ds(at, size), :] = rows

        place_shards(ids_ref, refs[:n], devices, size, put)

    return call(
        body,
        shape_of((size * devices, width), f32),
        VM,
        [SM] + [VM] * n,
        us=2,
        name="whole_grad",
    )(ids, *pieces)


def grad_input_rows(ids, dz1, mixes, parts, pooled, dims, after=()):
    devices, count, rows, quarter, full, width = dims
    here = rows // count
    tokens = here * full
    tile = here * quarter
    inner = mixes[0].shape[2]
    flat = [ref for p in parts for ref in p]
    n = len(flat)
    turn = (1, 3, 2, 0)

    def body(ids_ref, dz_ref, m_a, m_b, pool_ref, *refs):
        w_refs = refs[:n]
        outs = refs[n : n + count]
        wq, acc, sems = refs[n + count :]
        copies = []
        at = 0
        for kk in range(count):
            m = len(parts[kk])
            copies.append(
                load_parts(w_refs[at : at + m], ids_ref[2], inner // 2, wq.at[kk], 0, sems, at)
            )
            at += m
        for kk in turn:
            for copy in copies[kk]:
                copy.start()
        half = tokens // 2
        for i, kk in enumerate(turn):
            for copy in copies[kk]:
                copy.wait()
            mix = (m_a, m_b)[i // 2]
            for m in range(2):
                span = slice(m * half, (m + 1) * half)
                part = mm(mix[i % 2, span, :], wq[kk])
                if i == 0:
                    acc[span, :] = part + dz_ref[span, :]
                else:
                    acc[span, :] += part
        for kk in range(count):
            for r in range(here):
                outs[kk][r * quarter : (r + 1) * quarter, :] = acc[
                    r * full + kk * quarter : r * full + (kk + 1) * quarter, :
                ].astype(bf16)
            outs[kk][tile:, :] = pool_ref[...].astype(bf16)

    return call(
        body,
        [shape_of((tile + here * SEGS, width))] * count,
        [VM] * count,
        [SM] + [VM] * 4 + [HB] * n,
        [
            pltpu.VMEM((count, inner, width), bf16),
            pltpu.VMEM((tokens, width), f32),
            pltpu.SemaphoreType.DMA((n,)),
        ],
        us=6,
        name="grad_input_rows",
        after=after,
    )(ids, dz1, *mixes, pooled, *flat)


def land_grad(sent, pieces, dims):
    devices, count, rows, quarter, full, width = dims
    here = rows // count
    tile = here * quarter

    def body(sent_ref, *refs):
        piece_refs = refs[:count]
        out, pooled, sems = refs[count:]
        copies = []
        for kk in range(count):
            for j in range(here):
                at = kk * here + j
                copy = pltpu.make_async_copy(
                    piece_refs[kk].at[pl.ds(j * quarter, quarter)], out.at[sent_ref[at]], sems.at[at]
                )
                copy.start()
                copies.append(copy)
                pooled[sent_ref[at]] = piece_refs[kk][
                    tile : tile + here * SEGS, :
                ].astype(f32)[j * SEGS : (j + 1) * SEGS]
        for copy in copies:
            copy.wait()

    return call(
        body,
        [shape_of((rows, quarter, width)), shape_of((rows, SEGS, width), f32)],
        [HB, VM],
        [SM] + [VM] * count,
        [pltpu.SemaphoreType.DMA((rows,))],
        us=2,
        name="land_grad",
    )(sent, *pieces)


def turn_output(ids, hops, dims, after=()):
    devices, count, rows, quarter, full, width = dims
    here, cap, reach = rows // count, rows // devices, devices // count

    def body(ids_ref, *refs):
        hop_refs = refs[:reach]
        outs = refs[reach : reach + count]
        sems = refs[reach + count]
        handler = lax.div(ids_ref[0], reach)
        copies = []
        for kk in range(count):
            block = ids_ref[1] ^ kk ^ handler
            for k in range(reach):
                for c in range(cap):
                    j = k * cap + c
                    copy = pltpu.make_async_copy(
                        hop_refs[k].at[c, pl.ds(pl.multiple_of(block * quarter, quarter), quarter)],
                        outs[kk].at[pl.ds(j * quarter, quarter)],
                        sems.at[kk * here + j],
                    )
                    copy.start()
                    copies.append(copy)
        for copy in copies:
            copy.wait()

    return call(
        body,
        [shape_of((here * quarter, width))] * count,
        [HB] * count,
        [SM] + [HB] * reach,
        [pltpu.SemaphoreType.DMA((rows,))],
        us=2,
        name="turn_output",
        after=after,
    )(ids, *hops)


def land_output(spots, pieces, dims):
    devices, count, rows, quarter, full, width = dims
    here = rows // count

    def body(spots_ref, *refs):
        piece_refs = refs[:count]
        out, sems = refs[count:]
        copies = []
        for kk in range(count):
            for j in range(here):
                at = kk * here + j
                copy = pltpu.make_async_copy(
                    piece_refs[kk].at[pl.ds(j * quarter, quarter)], out.at[spots_ref[at]], sems.at[at]
                )
                copy.start()
                copies.append(copy)
        for copy in copies:
            copy.wait()

    return call(
        body,
        shape_of((rows, quarter, width)),
        HB,
        [SM] + [HB] * count,
        [pltpu.SemaphoreType.DMA((rows,))],
        us=2,
        name="land_output",
    )(spots, *pieces)


def swap(values, axis, bit):
    return lax.ppermute(values, axis, [(i, i ^ bit) for i in range(lax.axis_size(axis))])


def per_device(
    tokens_in, seg, route, w_qkv, b_qv, w_out, b_out, gain_attn, bias_attn, w_in, b_in, w_down,
    b_down, gain_ffn, bias_ffn, out_grad, pool_grad,
):
    devices, count = lax.axis_size("dp"), lax.axis_size("mp")
    rows, quarter, width = tokens_in.shape
    full = seg.shape[1]
    dims = (devices, count, rows, quarter, full, width)
    here, cap, reach = rows // count, rows // devices, devices // count
    my, mi = lax.axis_index("dp"), lax.axis_index("mp")
    parity = lax.rem(my, 2)
    ints = jnp.int32
    ids = jnp.stack([my, mi, parity]).astype(ints)
    head_width = w_qkv.shape[2]
    inner = 3 * head_width

    places = jnp.arange(rows, dtype=ints)
    routes = route.reshape(devices, rows)
    key = routes // rows * rows + places[None]
    rank = jnp.sum((key[:, None, :] < key[:, :, None]).astype(ints), axis=2)
    placed = rank[:, :, None] == places[None, None, :]
    table = jnp.sum(jnp.where(placed, routes[:, :, None], 0), axis=1)
    own_rank = lax.dynamic_index_in_dim(rank, my, 0, keepdims=False)
    steps = jnp.arange(reach, dtype=ints)
    copies = jnp.arange(cap, dtype=ints)
    blocks = jnp.arange(count, dtype=ints)
    near = lax.rem(my // count - steps + reach, reach)
    slots = (
        ((mi ^ blocks)[:, None, None] * reach + near[None, :, None]) * cap + copies[None, None, :]
    ).reshape(rows)
    sent = jnp.sum(jnp.where(own_rank[None, :] == slots[:, None], places[None, :], 0), axis=1)
    pair = lax.dynamic_slice_in_dim(table, my * cap, cap, 1) - my * rows
    sources = (mi ^ blocks)[:, None] + count * lax.rem(my + steps, reach)[None, :]
    spots = jnp.sum(
        jnp.where(
            sources[:, :, None, None] == jnp.arange(devices, dtype=ints)[None, None, :, None],
            pair[None, None],
            0,
        ),
        axis=2,
    ).reshape(rows)
    asked = spots[: reach * cap]
    mine = my * rows + sent[:here]
    lines = jnp.sum(
        jnp.where(
            mine[:, None, None] == jnp.arange(devices * rows, dtype=ints)[None, :, None], seg[None], 0
        ),
        axis=1,
    ).reshape(here, count, quarter)
    lines = jnp.sum(
        jnp.where((mi ^ blocks)[:, None, None, None] == blocks[None, None, :, None], lines[None], 0),
        axis=2,
    )
    segr = jnp.pad(lines.transpose(1, 0, 2).reshape(here, full), ((0, 8 - here), (0, 0)))

    def to_place(k):
        return [
            (s * count + f, (reach * f + (s // count - k) % reach) * count + s % count)
            for s in range(devices)
            for f in range(count)
        ]

    def from_place(k):
        return [(b, a) for a, b in to_place(k)]

    sends = prep_rows(sent, tokens_in, b_qv, b_in, dims)
    pieces = [sends[0]] + [swap(sends[k], "mp", k) for k in range(1, count)]
    wq = w_qkv.transpose(1, 2, 0).reshape(inner, width)
    half_q, half_oi, half_dn = prep_halves(ids, wq, w_out, w_in, w_down, (sends[0],))

    def cross(half, after=None):
        direct = swap(half, "mp", 2)
        if after is not None:
            direct, _ = lax.optimization_barrier((direct, after))
        return direct, swap(direct, "dp", 1)

    def sibling(values):
        return tuple(swap(v, "mp", 1) for v in values)

    far_q = cross(half_q)
    q_parts = [(wq,), sibling((wq,)), far_q, sibling(far_q)]
    vecs = jnp.stack(
        [b_out, gain_attn, bias_attn, b_down, gain_ffn, bias_ffn, gain_ffn, bias_ffn]
    )
    x, ol_a, qkv_a, p_a = attend(
        ids, segr, pieces, q_parts[:2], (0, 1), dims, True, (far_q[0],)
    )
    far_oi = cross(half_oi, ol_a)
    oi_parts = [(w_out, w_in), sibling((w_out, w_in)), far_oi, sibling(far_oi)]
    far_dn = cross(half_dn)
    dn_parts = [(w_down,), sibling((w_down,)), far_dn, sibling(far_dn)]
    in_parts = [p[1:] if k < 2 else p for k, p in enumerate(oi_parts)]
    wo_parts = [p[:1] if k < 2 else p for k, p in enumerate(oi_parts)]

    og_sends = prep_cot(asked, out_grad, dims, (ol_a,))
    ogs = [lax.ppermute(og_sends[k], ("dp", "mp"), from_place(k)) for k in range(reach)]
    ol_b, qkv_b, p_b = attend(
        ids, segr, pieces, q_parts[2:], (2, 3), dims, False, (og_sends[0],)
    )
    (
        al, hat, inv, hl, gp, tk0, tk1, pooled, dz, low, ffn_sums, down_pair,
    ) = ffn(
        ids, sent, segr, x, (ol_a, ol_b), pieces, vecs, ogs, pool_grad, oi_parts, dn_parts, dims
    )
    got_down = swap(down_pair, "mp", 1)
    hops = [lax.ppermute(t, ("dp", "mp"), to_place(k)) for k, t in enumerate((tk0, tk1))]
    du, in_pair, bin_sums = ffn_back(ids, low, gp, al, dn_parts, dims)
    got_in = swap(in_pair, "mp", 1)
    down_far = peer_grad(hl, low, got_down, (bin_sums,))
    crossed_down = swap(down_far, "mp", 2)
    dz1, low1, norm_sums = norm_back_attn(
        ids, du, al, dz, hat, inv, vecs, in_parts, dims, head_width // 2, (down_far,)
    )
    in_far = peer_grad_in(al, du, got_in, (norm_sums,))
    crossed_in = swap(in_far, "mp", 2)
    extras = (bin_sums, ffn_sums, norm_sums)
    mix_a, grads_a = attend_back(
        ids, low1, x,
        [(1, 1, ol_a, qkv_a, p_a, wo_parts[1]), (3, 1, ol_b, qkv_b, p_b, wo_parts[3])],
        extras, dims, (in_far,),
    )
    got_last = swap(grads_a, "mp", 1)
    send_down, keep_down = own_grad(
        ids, hl, low, got_down, crossed_down, devices, True, (grads_a,)
    )
    mix_b, grads_b = attend_back(
        ids, low1, x,
        [(2, 0, ol_b, qkv_b, p_b, wo_parts[2]), (0, 0, ol_a, qkv_a, p_a, wo_parts[0])],
        extras, dims, (send_down,),
    )
    last_far = peer_last(grads_b, got_last, 0)
    crossed_last = swap(last_far, "mp", 2)
    gx = grad_input_rows(ids, dz1, (mix_a, mix_b), q_parts, pooled, dims, (last_far,))
    gx_got = [gx[0]] + [swap(gx[k], "mp", k) for k in range(1, count)]
    grad_input, pooled_out = land_grad(sent, gx_got, dims)

    turned = turn_output(ids, hops, dims, (gx[0],))
    landed = [turned[0]] + [swap(turned[k], "mp", k) for k in range(1, count)]
    tokens_out = land_output(spots, landed, dims)

    down_shards, _ = reduce_dp(send_down, keep_down, None, devices)
    g_down = whole_grad(ids, down_shards, devices)
    send, keep = own_grad(ids, al, du, got_in, crossed_in, devices, False, (gx[0],))
    in_shards, _ = reduce_dp(send, keep, None, devices)
    g_in = whole_grad(ids, in_shards, devices)
    send, keep, vec = own_last(ids, grads_b, got_last, crossed_last, 1, devices)
    last_shards, vec = reduce_dp(send, keep, vec, devices)
    g_last = whole_grad(ids, last_shards, devices)
    g_qkv = g_last[:inner].reshape(3, head_width, width).transpose(2, 0, 1)
    g_bqv = jnp.stack([vec[0, :head_width], vec[0, 256 : 256 + head_width]])
    return (
        tokens_out, pooled_out, grad_input, g_qkv, g_bqv, g_last[inner:],
        vec[2], vec[3], vec[4], g_in, vec[1], g_down, vec[5], vec[6], vec[7],
    )


def solution(mesh):
    devices, count = mesh.shape["dp"], mesh.shape["mp"]

    def body(*args):
        rows = args[0].shape[0]
        even = rows % devices == 0 and devices % count == 0 and count == 4
        even = even and devices & (devices - 1) == 0 and rows // count == 2 * (rows // devices)
        return (per_device if even else per_device_general)(*args)

    return jax.shard_map(
        body,
        mesh=mesh,
        in_specs=(
            P("dp", "mp", None),
            P(),
            P(),
            P(None, None, "mp"),
            P(None, "mp"),
            P("mp", None),
            P(),
            P(),
            P(),
            P(None, "mp"),
            P("mp"),
            P("mp", None),
            P(),
            P(),
            P(),
            P("dp", None, None),
            P("dp", None, None),
        ),
        out_specs=(
            P("dp", "mp", None),
            P("dp", None, None),
            P("dp", "mp", None),
            P(None, None, "mp"),
            P(None, "mp"),
            P("mp", None),
            P(),
            P(),
            P(),
            P(None, "mp"),
            P("mp"),
            P("mp", None),
            P(),
            P(),
            P(),
        ),
        check_vma=False,
    )
```

```python
import jax
import jax.numpy as jnp
from jax import lax
from jax.experimental import pallas as pl
from jax.experimental.pallas import tpu as pltpu
from jax.sharding import PartitionSpec as P

HD = 64
SEGS = 4


EPSILON = 1e-12
MASKED = -1e30
f32 = jnp.float32
bf16 = jnp.bfloat16


def normalize(values):
    centre = values - jnp.mean(values, axis=-1, keepdims=True)
    scale_inv = lax.rsqrt(jnp.mean(centre * centre, axis=-1, keepdims=True) + EPSILON)
    return (centre * scale_inv, scale_inv[..., 0])


def norm_back(grad_hat, normed_hat, inverse):
    mean_grad = jnp.mean(grad_hat, axis=-1, keepdims=True)
    mean_proj = jnp.mean(grad_hat * normed_hat, axis=-1, keepdims=True)
    return inverse[..., None] * (grad_hat - mean_grad - normed_hat * mean_proj)


def pack_rows(values, position, filled):
    picked = jnp.take(values, position, axis=0)
    shape_mask = filled.reshape((-1,) + (1,) * (values.ndim - 1))
    return jnp.where(shape_mask, picked, jnp.zeros_like(picked))


def per_device_general(
    tokens_in,
    seg,
    route,
    w_qkv,
    b_qv,
    w_out,
    b_out,
    gain_attn,
    bias_attn,
    w_in,
    b_in,
    w_down,
    b_down,
    gain_ffn,
    bias_ffn,
    out_grad,
    pool_grad,
):
    f32 = jnp.float32
    bf16 = jnp.bfloat16
    devices = lax.axis_size("dp")
    row_local = tokens_in.shape[0]
    quarter = tokens_in.shape[1]
    all_rows = route.shape[0]
    capacity = max(1, row_local // devices)
    buffer_len = devices * capacity
    my_index = lax.axis_index("dp")
    target_dev = route // row_local
    dest_grid = target_dev.reshape(devices, row_local)
    before = jnp.arange(row_local)[None, :] < jnp.arange(row_local)[:, None]
    same_dest = dest_grid[:, :, None] == dest_grid[:, None, :]
    earlier_count = (
        jnp.sum(jnp.where(same_dest & before[None], 1, 0), axis=2).reshape(-1).astype(jnp.int32)
    )
    slot_out = target_dev * capacity + earlier_count
    slot_in = jnp.arange(all_rows, dtype=jnp.int32) // row_local * capacity + earlier_count
    own_slots = lax.dynamic_slice_in_dim(slot_out, my_index * row_local, row_local)
    local_rows = jnp.arange(row_local, dtype=jnp.int32)
    send_pos = jnp.zeros(buffer_len, jnp.int32).at[own_slots].set(local_rows)
    send_fill = jnp.zeros(buffer_len, jnp.bool_).at[own_slots].set(True)
    arrive = jnp.where(target_dev == my_index, route - my_index * row_local, row_local)
    recv_pos = jnp.zeros(row_local, jnp.int32).at[arrive].set(slot_in, mode="drop")
    anchor = (
        jnp.zeros(row_local, jnp.int32)
        .at[arrive]
        .set(jnp.arange(all_rows, dtype=jnp.int32), mode="drop")
    )
    back_pos = jnp.zeros(buffer_len, jnp.int32).at[recv_pos].set(local_rows)
    back_fill = jnp.zeros(buffer_len, jnp.bool_).at[recv_pos].set(True)
    arrived = lax.all_to_all(
        pack_rows(tokens_in, send_pos, send_fill), "dp", split_axis=0, concat_axis=0, tiled=True
    )
    rows_x = jnp.take(arrived, recv_pos, axis=0)
    segment = jnp.take(seg, anchor, axis=0)
    full_len = segment.shape[1]
    mp_index = lax.axis_index("mp")

    def own_part(values):
        return lax.dynamic_slice_in_dim(values, mp_index * quarter, quarter, 1)

    gathered = lax.all_gather(rows_x, "mp", axis=1, tiled=True)
    head_width = w_qkv.shape[2]
    local_heads = head_width // HD
    head_shape = (row_local, full_len, local_heads, HD)
    projected = jnp.einsum("rsd,dcf->rscf", gathered, w_qkv, preferred_element_type=f32)
    query_heads = (projected[:, :, 0] + b_qv[0]).astype(bf16).reshape(head_shape)
    key_heads = projected[:, :, 1].astype(bf16).reshape(head_shape)
    value_heads = (projected[:, :, 2] + b_qv[1]).astype(bf16).reshape(head_shape)
    allowed = (segment[:, :, None] == segment[:, None, :])[:, None]
    factor = HD ** (-0.5)

    def scores_of():
        raw_scores = (
            jnp.einsum("rqhe,rkhe->rhqk", query_heads, key_heads, preferred_element_type=f32)
            * factor
        )
        return jnp.where(allowed, raw_scores, MASKED)

    scores = scores_of()
    row_peak = jnp.max(scores, axis=-1, keepdims=True)
    raised = jnp.exp(scores - row_peak)
    weight_total = jnp.sum(raised, axis=-1, keepdims=True)
    log_total = row_peak + jnp.log(weight_total)
    attention = raised / weight_total
    attended = jnp.einsum(
        "rhqk,rkhe->rqhe", attention.astype(bf16), value_heads, preferred_element_type=f32
    )
    attended = attended.astype(bf16).reshape(row_local, full_len, head_width)
    branch = jnp.einsum("rsf,fd->rsd", attended, w_out, preferred_element_type=f32)
    summed_branch = lax.psum_scatter(branch, "mp", scatter_dimension=1, tiled=True)
    hat_attn, inv_attn = normalize(rows_x.astype(f32) + summed_branch + b_out)
    normed_low = (hat_attn * gain_attn + bias_attn).astype(bf16)
    normed_all = lax.all_gather(normed_low, "mp", axis=1, tiled=True)
    hidden = jnp.einsum("rsd,df->rsf", normed_all, w_in, preferred_element_type=f32) + b_in
    active, gelu_back = jax.vjp(lambda values: jax.nn.gelu(values, approximate=False), hidden)
    active_low = active.astype(bf16)
    ffn_part = jnp.einsum("rsf,fd->rsd", active_low, w_down, preferred_element_type=f32)
    ffn_total = lax.psum(ffn_part, "mp")
    hat_ffn, inv_ffn = normalize(normed_all.astype(f32) + ffn_total + b_down)
    block_out = hat_ffn * gain_ffn + bias_ffn
    output_rows = own_part(block_out).astype(bf16)
    member = (segment[:, :, None] == jnp.arange(SEGS)[None, None, :]).astype(f32)
    counts = jnp.sum(member, axis=1)
    pooled_rows = (
        jnp.einsum("rsg,rsd->rgd", member, block_out, precision=lax.Precision.HIGHEST)
        / counts[:, :, None]
    )
    pooled_back = lax.all_to_all(
        pack_rows(pooled_rows, back_pos, back_fill).astype(jnp.bfloat16),
        "dp",
        split_axis=0,
        concat_axis=0,
        tiled=True,
    ).astype(jnp.float32)
    pooled = jnp.take(pooled_back, own_slots, axis=0)
    pool_arrived = lax.all_to_all(
        pack_rows(pool_grad, send_pos, send_fill), "dp", split_axis=0, concat_axis=0, tiled=True
    )
    pool_rows = jnp.take(pool_arrived, recv_pos, axis=0)
    grad_final = out_grad.astype(f32) + jnp.einsum(
        "rsg,rgd->rsd", member, pool_rows / counts[:, :, None], precision=lax.Precision.HIGHEST
    )
    grad_mix = norm_back(grad_final * gain_ffn, hat_ffn, inv_ffn)
    grad_gain_ffn = jnp.sum(grad_final * hat_ffn, axis=(0, 1))
    grad_bias_ffn = jnp.sum(grad_final, axis=(0, 1))
    grad_b_down = jnp.sum(grad_mix, axis=(0, 1))
    mix_low = grad_mix.astype(bf16)
    grad_w_down = jnp.einsum("rsf,rsd->fd", active_low, mix_low, preferred_element_type=f32)
    grad_active = jnp.einsum("rsd,fd->rsf", mix_low, w_down, preferred_element_type=f32)
    grad_hidden = gelu_back(grad_active)[0].astype(bf16)
    grad_w_in = jnp.einsum("rsd,rsf->df", normed_all, grad_hidden, preferred_element_type=f32)
    grad_b_in = jnp.sum(grad_hidden.astype(f32), axis=(0, 1))
    normed_part = jnp.einsum("rsf,df->rsd", grad_hidden, w_in, preferred_element_type=f32)
    grad_normed = lax.psum_scatter(normed_part, "mp", scatter_dimension=1, tiled=True) + own_part(
        grad_mix
    )
    gain_attn_part = jnp.sum(grad_normed * hat_attn, axis=(0, 1))
    bias_attn_part = jnp.sum(grad_normed, axis=(0, 1))
    grad_inner = norm_back(grad_normed * gain_attn, hat_attn, inv_attn)
    stat_terms = jnp.stack([jnp.sum(grad_inner, axis=(0, 1)), gain_attn_part, bias_attn_part])[None]
    inner_all, stats_all = (
        lax.all_gather(grad_inner.astype(jnp.bfloat16), "mp", axis=1, tiled=True).astype(
            grad_inner.dtype
        ),
        lax.all_gather(stat_terms.astype(jnp.bfloat16), "mp", axis=0, tiled=True).astype(
            stat_terms.dtype
        ),
    )
    stat_sums = jnp.sum(stats_all, axis=0)
    inner_low = inner_all.astype(bf16)
    grad_w_out = jnp.einsum("rsf,rsd->fd", attended, inner_low, preferred_element_type=f32)
    grad_attended = (
        jnp.einsum("rsd,fd->rsf", inner_low, w_out, preferred_element_type=f32)
        .astype(bf16)
        .reshape(head_shape)
    )
    again = jnp.exp(scores_of() - log_total)
    grad_prob = jnp.einsum(
        "rqhe,rkhe->rhqk", grad_attended, value_heads, preferred_element_type=f32
    )
    grad_values = jnp.einsum(
        "rhqk,rqhe->rkhe", again.astype(bf16), grad_attended, preferred_element_type=f32
    )
    grad_scores = (again * (grad_prob - jnp.sum(grad_prob * again, axis=-1, keepdims=True))).astype(
        bf16
    )
    grad_query = (
        jnp.einsum("rhqk,rkhe->rqhe", grad_scores, key_heads, preferred_element_type=f32) * factor
    ).astype(bf16)
    grad_keys = (
        jnp.einsum("rhqk,rqhe->rkhe", grad_scores, query_heads, preferred_element_type=f32) * factor
    ).astype(bf16)
    flat_shape = (row_local, full_len, head_width)
    grad_mixed = jnp.stack(
        [
            grad_query.reshape(flat_shape),
            grad_keys.reshape(flat_shape),
            grad_values.astype(bf16).reshape(flat_shape),
        ],
        axis=2,
    )
    grad_w_qkv = jnp.einsum("rsd,rscf->dcf", gathered, grad_mixed, preferred_element_type=f32)
    grad_b_qv = jnp.stack(
        [
            jnp.sum(grad_mixed[:, :, 0].astype(f32), axis=(0, 1)),
            jnp.sum(grad_mixed[:, :, 2].astype(f32), axis=(0, 1)),
        ]
    )
    input_part = jnp.einsum("rscf,dcf->rsd", grad_mixed, w_qkv, preferred_element_type=f32)
    grad_rows = (
        lax.psum_scatter(input_part, "mp", scatter_dimension=1, tiled=True) + grad_inner
    ).astype(bf16)
    grad_home = lax.all_to_all(
        pack_rows(grad_rows, back_pos, back_fill), "dp", split_axis=0, concat_axis=0, tiled=True
    )
    grad_input = jnp.take(grad_home, own_slots, axis=0)
    vector_grads = jnp.stack(
        [stat_sums[0], stat_sums[1], stat_sums[2], grad_b_down, grad_gain_ffn, grad_bias_ffn]
    )
    totals = lax.psum(
        (grad_w_qkv, grad_b_qv, grad_w_out, grad_w_in, grad_b_in, grad_w_down, vector_grads), "dp"
    )
    return (
        output_rows,
        pooled,
        grad_input,
        totals[0],
        totals[1],
        totals[2],
        totals[6][0],
        totals[6][1],
        totals[6][2],
        totals[3],
        totals[4],
        totals[5],
        totals[6][3],
        totals[6][4],
        totals[6][5],
    )


VM = pl.BlockSpec(memory_space=pltpu.VMEM)
SM = pl.BlockSpec(memory_space=pltpu.SMEM)
HB = pl.BlockSpec(memory_space=pl.ANY)
HM = pl.BlockSpec(memory_space=pltpu.HBM)
MIB = 1024 * 1024
PACE = 2e9


def shape_of(shape, dtype=bf16):
    return jax.ShapeDtypeStruct(shape, dtype)


def call(
    body, outs, out_specs, in_specs, scratch=(), us=2, room=16, name=None, after=()
):
    n, extra = len(in_specs), len(after)

    def trimmed(*refs):
        body(*refs[:n], *refs[n + extra :])

    made = pl.pallas_call(
        trimmed,
        out_shape=outs,
        in_specs=list(in_specs) + [HB] * extra,
        out_specs=out_specs,
        scratch_shapes=list(scratch),
        compiler_params=pltpu.CompilerParams(vmem_limit_bytes=room * MIB),
        cost_estimate=pl.CostEstimate(flops=int(us * PACE), bytes_accessed=0, transcendentals=0),
        name=name,
    )
    return lambda *args: made(*args, *after)


def mm(a, b):
    return lax.dot_general(a, b, (((1,), (0,)), ((), ())), preferred_element_type=f32)


def mm_nt(a, b):
    return lax.dot_general(a, b, (((1,), (1,)), ((), ())), preferred_element_type=f32)


def mm_tn(a, b):
    return lax.dot_general(a, b, (((0,), (0,)), ((), ())), preferred_element_type=f32)


def split3(values):
    high = values.astype(bf16)
    rest = values - high.astype(f32)
    middle = rest.astype(bf16)
    low = (rest - middle.astype(f32)).astype(bf16)
    return high, middle, low


def piece_places(refs, size):
    return [(refs[0], 0), (refs[1], 0), (refs[2], 0), (refs[3], size)]


def exchange(own, near, far):
    crossed = swap(far, "mp", 2)
    return [own, swap(near, "mp", 1), crossed, swap(crossed, "mp", 1)]


def prep_rows(route, seg, tokens, b_qv, b_in, weights, dims):
    devices, count, rows, quarter, full, width = dims
    here, cap = rows // count, rows // devices
    head_width = b_qv.shape[1]
    tile = here * quarter
    total = devices * rows
    halves = [w.shape[0] // 2 for w in weights]

    def body(
        route_ref, seg_ref, tok, bqv_ref, bin_ref, wq, wo, x0, x1, far, segr, sent_ref, spots_ref,
        ids_ref, lists, sems,
    ):
        my, mi = lax.axis_index("dp"), lax.axis_index("mp")
        crossing = []
        base = 2 * (tile + 16)
        for n, (src, half) in enumerate(zip((wq, wo), halves)):
            crossing.append(
                pltpu.make_async_copy(
                    src.at[pl.ds(pl.multiple_of(lax.rem(my, 2) * half, 16), half)],
                    far.at[pl.ds(base, half)],
                    sems.at[rows + 2 + n],
                )
            )
            crossing[n].start()
            base += half
        ids_ref[0] = my
        ids_ref[1] = mi
        ids_ref[2] = lax.rem(my, 2)
        places = piece_places((x0, x1, far, far), tile + 16)
        across = jnp.broadcast_to(route_ref[...].reshape(1, total), (total, total)).astype(f32)
        down = across.T.astype(jnp.int32)
        across = across.astype(jnp.int32)
        r = lax.broadcasted_iota(jnp.int32, (total, total), 0)
        c = lax.broadcasted_iota(jnp.int32, (total, total), 1)
        key_down = lax.div(down, rows) * total + r
        key_across = lax.div(across, rows) * total + c
        before = (lax.div(r, rows) == lax.div(c, rows)) & (key_across < key_down)
        rank = jnp.sum(jnp.where(before, 1.0, 0.0), axis=1, keepdims=True).astype(jnp.int32)
        at = lax.rem(c, rows)
        partner = my ^ ((mi ^ lax.div(at, here)) + count * lax.rem(lax.div(at, cap), here // cap))
        copy_at = lax.rem(at, cap)
        source = lax.div(r, rows)
        going = (source == my) & (rank == partner * cap + copy_at)
        coming = (source == partner) & (rank == my * cap + copy_at)
        lists[0:1, :] = jnp.sum(
            jnp.where(going, lax.rem(r, rows), 0).astype(f32), axis=0, keepdims=True
        ).astype(jnp.int32)
        lists[1:2, :] = jnp.sum(
            jnp.where(coming, down - my * rows, 0).astype(f32), axis=0, keepdims=True
        ).astype(jnp.int32)
        moves = [
            pltpu.make_async_copy(lists.at[0], sent_ref, sems.at[rows]),
            pltpu.make_async_copy(lists.at[1], spots_ref, sems.at[rows + 1]),
        ]
        for move in moves:
            move.start()
        zero = jnp.zeros((16, width), bf16)
        tail = x0.at[pl.ds(tile, 16)]
        tail[...] = zero
        for n, term in enumerate(split3(bqv_ref[...])):
            tail[n : n + 1, 0:head_width] = term[0:1]
            tail[n : n + 1, 256 : 256 + head_width] = term[1:2]
        for n, term in enumerate(split3(bin_ref[...].reshape(1, width))):
            tail[3 + n : 4 + n, :] = term
        for ref, base in places[1:]:
            ref[base + tile : base + tile + 16, :] = tail[...]
        for move in moves:
            move.wait()
        copies = []
        for kk in reversed(range(count)):
            for n in range(here):
                k = kk * here + n
                copies.append(
                    pltpu.make_async_copy(
                        tok.at[sent_ref[k]],
                        places[kk][0].at[pl.ds(places[kk][1] + n * quarter, quarter)],
                        sems.at[k],
                    )
                )
        for copy in copies:
            copy.start()
        for n in range(here):
            segr[n : n + 1, :] = seg_ref[pl.ds(my * rows + sent_ref[n], 1), :]
        segr[here:8, :] = jnp.zeros((8 - here, full), jnp.int32)
        lane = lax.broadcasted_iota(jnp.int32, (8, full), 1)
        lines = segr[...]
        bit = 1
        while bit < count:
            step = bit * quarter
            swapped = jnp.where(
                lax.rem(lax.div(lane, step), 2) == 0,
                pltpu.roll(lines, full - step, 1),
                pltpu.roll(lines, step, 1),
            )
            lines = jnp.where(lax.rem(lax.div(mi, bit), 2) == 1, swapped, lines)
            bit *= 2
        segr[...] = lines
        for copy in copies + crossing:
            copy.wait()

    return call(
        body,
        [
            shape_of((tile + 16, width)),
            shape_of((tile + 16, width)),
            shape_of((2 * (tile + 16) + sum(halves), width)),
        ]
        + [
            shape_of((8, full), jnp.int32),
            shape_of((total,), jnp.int32),
            shape_of((total,), jnp.int32),
            shape_of((3,), jnp.int32),
        ],
        [VM] * 4 + [SM] * 3,
        [VM, VM, HM, VM, VM, HM, HM],
        [pltpu.VMEM((8, total), jnp.int32), pltpu.SemaphoreType.DMA((rows + 4,))],
        us=3,
        name="prep_rows",
        room=60,
    )(route, seg, tokens, b_qv, b_in, *weights)


def prep_halves(weights, bit, after=()):
    width = weights[0].shape[1]
    halves = [w.shape[0] // 2 for w in weights]
    n = len(weights)

    def body(*refs):
        out, sems = refs[n:]
        parity = lax.rem(lax.div(lax.axis_index("dp"), bit), 2)
        copies = []
        base = 0
        for at, half in enumerate(halves):
            copies.append(
                pltpu.make_async_copy(
                    refs[at].at[pl.ds(pl.multiple_of(parity * half, 16), half)],
                    out.at[pl.ds(base, half)],
                    sems.at[at],
                )
            )
            base += half
        for copy in copies:
            copy.start()
        for copy in copies:
            copy.wait()

    return call(
        body,
        shape_of((sum(halves), width)),
        VM,
        [HM] * n,
        [pltpu.SemaphoreType.DMA((n,))],
        us=1,
        name="prep_halves",
        room=4,
        after=after,
    )(*weights)


def prep_cot(asked, out_grad, dims, after):
    devices, count, rows, quarter, full, width = dims
    cap, reach = rows // devices, devices // count

    def body(asked_ref, og, *refs):
        outs, sems = refs[:reach], refs[reach]
        copies = []
        for k in range(reach):
            for c in range(cap):
                at = k * cap + c
                copies.append(
                    pltpu.make_async_copy(og.at[asked_ref[at]], outs[k].at[c], sems.at[at])
                )
        for copy in copies:
            copy.start()
        for copy in copies:
            copy.wait()

    return call(
        body,
        [shape_of((cap, full, width))] * reach,
        [VM] * reach,
        [SM, HM],
        [pltpu.SemaphoreType.DMA((reach * cap,))],
        us=2,
        name="prep_cot",
        room=6,
        after=after,
    )(asked, out_grad)


def bias_rows(piece, at, count):
    terms = piece[at : at + 16, :].astype(f32)
    first = 0 if count == 0 else 3
    return terms[first : first + 1] + terms[first + 1 : first + 2] + terms[first + 2 : first + 3]


def head_masks(head_width):
    lane = lax.broadcasted_iota(jnp.int32, (1, head_width), 1)
    return [(lane >= h * HD) & (lane < (h + 1) * HD) for h in range(head_width // HD)]


def stack_heads(values, masks):
    zero = jnp.zeros_like(values)
    return jnp.concatenate([jnp.where(mask, values, zero) for mask in masks], axis=0)


def pick_heads(stacked, masks):
    size = stacked.shape[0] // len(masks)
    out = stacked[:size]
    for h in range(1, len(masks)):
        out = jnp.where(masks[h], stacked[h * size : (h + 1) * size], out)
    return out


def parity_of(ids_ref, bit):
    return lax.rem(lax.div(ids_ref[0], bit), 2)


def load_parts(refs, bases, parity, half, dst, sems, at, row=0):
    if len(refs) == 1:
        return [pltpu.make_async_copy(refs[0], dst, sems.at[at])]
    copies = []
    for j, place in enumerate((parity, 1 - parity)):
        copies.append(
            pltpu.make_async_copy(
                refs[j].at[pl.ds(bases[j] + row, half)],
                dst.at[pl.ds(pl.multiple_of(place * half, 16), half)],
                sems.at[at + j],
            )
        )
    return copies


def bases_of(part):
    return [base for _, base in part]


def attend(ids, segr, pieces, parts, pair, inner, dims, keep_x, after=()):
    devices, count, rows, quarter, full, width = dims
    here = rows // count
    tokens = here * full
    tile = here * quarter
    head_width = inner // 3
    n_heads = head_width // HD
    n_parts = [len(p) for p in parts]
    flat = [ref for p in parts for ref, _ in p]

    def body(ids_ref, segr_ref, *refs):
        places = piece_places(refs[:count], tile + 16)
        w_refs = refs[count : count + len(flat)]
        out = list(refs[count + len(flat) :])
        if keep_x:
            x_out = out.pop(0)
        ol_out, qkv_out, p_out, x_ref, w_ref, sems = out
        copies = []
        at = 0
        for b, n in enumerate(n_parts):
            copies += load_parts(
                w_refs[at : at + n], bases_of(parts[b]), ids_ref[2], inner // 2, w_ref.at[b], sems, at
            )
            at += n
        for copy in copies:
            copy.start()
        for r in range(here):
            for kk in range(count):
                ref, base = places[kk]
                x_ref[r * full + kk * quarter : r * full + (kk + 1) * quarter, :] = ref[
                    base + r * quarter : base + (r + 1) * quarter, :
                ]
        if keep_x:
            x_out[...] = x_ref[...]
        masks = head_masks(head_width)
        for copy in copies:
            copy.wait()
        for b in range(2):
            ref, base = places[pair[b]]
            bias = bias_rows(ref, base + tile, 0)
            bias_q, bias_v = bias[:, 0:head_width], bias[:, 256 : 256 + head_width]

            @pl.loop(0, here)
            def _(r):
                start = pl.multiple_of(r * full, full)
                projected = mm_nt(x_ref[pl.ds(start, full), :], w_ref[b])
                query = (projected[:, 0:head_width] + bias_q).astype(bf16)
                key = projected[:, head_width : 2 * head_width].astype(bf16)
                value = (projected[:, 2 * head_width :] + bias_v).astype(bf16)
                line = segr_ref[pl.ds(r, 1), :].astype(f32)
                wide = jnp.broadcast_to(line, (full, full))
                allowed = wide == wide.T
                stacked = stack_heads(query, masks)
                raw = mm_nt(stacked, key) * (HD ** -0.5)
                allowed3 = jnp.concatenate([allowed] * n_heads, axis=0)
                scores = jnp.where(allowed3, raw, MASKED)
                raised = jnp.exp(scores - jnp.max(scores, axis=1, keepdims=True))
                prob = raised / jnp.sum(raised, axis=1, keepdims=True)
                low = prob.astype(bf16)
                attended = pick_heads(mm(low, value), masks).astype(bf16)
                ol_out[b, pl.ds(start, full), :] = attended
                qkv_out[b, 0, pl.ds(start, full), :] = query
                qkv_out[b, 1, pl.ds(start, full), :] = key
                qkv_out[b, 2, pl.ds(start, full), :] = value
                p_out[b, r] = low

    outs = [
        shape_of((2, tokens, head_width)),
        shape_of((2, 3, tokens, head_width)),
        shape_of((2, here, n_heads * full, full)),
    ]
    if keep_x:
        outs = [shape_of((tokens, width))] + outs
    return call(
        body,
        outs,
        [VM] * len(outs),
        [SM, VM] + [VM] * count + [HB] * len(flat),
        [
            pltpu.VMEM((tokens, width), bf16),
            pltpu.VMEM((2, inner, width), bf16),
            pltpu.SemaphoreType.DMA((len(flat),)),
        ],
        us=10,
        name="attend",
        room=18,
        after=after,
    )(ids, segr, *pieces, *flat)


def gelu_pair(u):
    z = jnp.abs(u) * (0.5 ** 0.5)
    t = 1.0 / (1.0 + 0.3275911 * z)
    poly = t * (
        0.254829592
        + t * (-0.284496736 + t * (1.421413741 + t * (-1.453152027 + t * 1.061405429)))
    )
    bell = jnp.exp(-0.5 * u * u)
    tail = 0.5 * poly * bell
    cdf = jnp.where(u >= 0, 1.0 - tail, tail)
    return u * cdf, cdf + u * bell * 0.3989422804014327


def norm_rows(values):
    centre = values - jnp.mean(values, axis=1, keepdims=True)
    inverse = lax.rsqrt(jnp.mean(centre * centre, axis=1, keepdims=True) + EPSILON)
    return centre * inverse, inverse


def ffn_near(ids, x, ols, pieces, vecs, out_parts, near_in, near_down, inner, dims, after=()):
    devices, count, rows, quarter, full, width = dims
    here = rows // count
    tokens = here * full
    tile = here * quarter
    head_width = ols[0].shape[2]
    hidden = width
    flat = [ref for p in out_parts for ref, _ in p]
    n = len(flat)

    def body(ids_ref, x_ref, ol_a, ol_b, *refs):
        refs = list(refs)
        places = piece_places([refs.pop(0) for _ in range(count)], tile + 16)
        vec_refs = [refs.pop(0) for _ in range(3)]
        wo_refs = [refs.pop(0) for _ in range(n)]
        wi_refs = [refs.pop(0) for _ in range(2)]
        wd_refs = [refs.pop(0) for _ in range(2)]
        al_out, hat_out, inv_out, acc_out, hl_out, gp_out, wo, wi, wd, sems = refs
        first, later = [], []
        at = 0
        for kk in range(count):
            m = len(out_parts[kk])
            first += load_parts(
                wo_refs[at : at + m], bases_of(out_parts[kk]), ids_ref[2], head_width // 2, wo.at[kk],
                sems, at, inner // 2,
            )
            at += m
        for b in range(2):
            later.append(
                [
                    pltpu.make_async_copy(wi_refs[b], wi.at[b], sems.at[n + 2 * b]),
                    pltpu.make_async_copy(wd_refs[b], wd.at[b], sems.at[n + 2 * b + 1]),
                ]
            )
        for copy in first + later[0] + later[1]:
            copy.start()
        b_out, gain_a, bias_a = (v[...].reshape(1, width) for v in vec_refs)
        for copy in first:
            copy.wait()
        for r in range(here):
            span = slice(r * full, (r + 1) * full)
            total = x_ref[span, :].astype(f32) + b_out
            for kk in range(count):
                ol = (ol_a, ol_b)[kk // 2]
                total = total + mm(ol[kk % 2, span, :], wo[kk])
            hat, inverse = norm_rows(total)
            hat_out[span, :] = hat
            inv_out[span, :] = jnp.broadcast_to(inverse, (full, 128))
            al_out[span, :] = (hat * gain_a + bias_a).astype(bf16)
        half = tokens // 2
        for b in range(2):
            for copy in later[b]:
                copy.wait()
            ref, base = places[b]
            bias = bias_rows(ref, base + tile, 3)
            for m in range(2):
                span = slice(m * half, (m + 1) * half)
                u = mm(al_out[span, :], wi[b]) + bias
                active, slope = gelu_pair(u)
                active = active.astype(bf16)
                hl_out[b, span, :] = active
                gp_out[b, span, :] = slope.astype(bf16)
                part = mm(active, wd[b])
                if b == 0:
                    acc_out[span, :] = part
                else:
                    acc_out[span, :] += part

    wide = (tokens, width)
    return call(
        body,
        [
            shape_of(wide), shape_of(wide, f32), shape_of((tokens, 128), f32), shape_of(wide, f32),
            shape_of((2,) + wide), shape_of((2,) + wide),
        ],
        [VM] * 6,
        [SM, VM, VM, VM] + [VM] * (count + 3) + [HB] * (n + 4),
        [
            pltpu.VMEM((count, head_width, width), bf16),
            pltpu.VMEM((2, width, hidden), bf16),
            pltpu.VMEM((2, hidden, width), bf16),
            pltpu.SemaphoreType.DMA((n + 4,)),
        ],
        us=11,
        name="ffn_near",
        room=26,
        after=after,
    )(ids, x, ols[0], ols[1], *pieces, *vecs, *flat, *near_in, *near_down)


def ffn_far(ids, al, pieces, parts, dims, after=()):
    devices, count, rows, quarter, full, width = dims
    here = rows // count
    tokens = here * full
    tile = here * quarter
    hidden = width
    flat = [ref for p in parts for ref, _ in p]
    n = len(flat)

    def body(ids_ref, al_ref, *refs):
        places = piece_places(refs[:count], tile + 16)
        w_refs = refs[count : count + n]
        hl_out, gp_out, wi, sems = refs[count + n :]
        copies = []
        at = 0
        for b in range(2):
            m = len(parts[b])
            copies.append(
                load_parts(
                    w_refs[at : at + m], bases_of(parts[b]), ids_ref[2], width // 2, wi.at[b], sems, at
                )
            )
            at += m
        for copy in copies[0] + copies[1]:
            copy.start()
        half = tokens // 2
        for b in range(2):
            for copy in copies[b]:
                copy.wait()
            ref, base = places[2 + b]
            bias = bias_rows(ref, base + tile, 3)
            for m in range(2):
                span = slice(m * half, (m + 1) * half)
                active, slope = gelu_pair(mm(al_ref[span, :], wi[b]) + bias)
                hl_out[b, span, :] = active.astype(bf16)
                gp_out[b, span, :] = slope.astype(bf16)

    wide = (tokens, width)
    return call(
        body,
        [shape_of((2,) + wide), shape_of((2,) + wide)],
        [VM] * 2,
        [SM, VM] + [VM] * count + [HB] * n,
        [pltpu.VMEM((2, width, hidden), bf16), pltpu.SemaphoreType.DMA((n,))],
        us=6,
        name="ffn_far",
        room=14,
        after=after,
    )(ids, al, *pieces, *flat)


def ffn_down(ids, sent, segr, al, acc, hls, vecs, ogs, pool_grad, parts, dims):
    devices, count, rows, quarter, full, width = dims
    here, cap, reach = rows // count, rows // devices, devices // count
    tokens = here * full
    hidden = width
    flat = [ref for p in parts for ref, _ in p]
    n = len(flat)

    def body(ids_ref, sent_ref, segr_ref, al_ref, near_ref, hl_near, hl_far, *refs):
        refs = list(refs)
        vec_refs = [refs.pop(0) for _ in range(3)]
        og_refs = [refs.pop(0) for _ in range(reach)]
        pool_ref = refs.pop(0)
        w_refs = [refs.pop(0) for _ in range(n)]
        tk0, tk1, pooled_out, dz_out, low_out, sums_out, down_out, wd, near, og_buf, acc_ref, sems = refs
        mi, parity = ids_ref[1], parity_of(ids_ref, 2)
        groups = []
        at = 0
        for b in range(2):
            m = len(parts[b])
            groups.append(
                load_parts(
                    w_refs[at : at + m], bases_of(parts[b]), parity, width // 2, wd.at[b], sems, at
                )
            )
            at += m
        sibling_hl = pltpu.make_async_copy(hl_near.at[1], near, sems.at[n])
        cots = []
        for k in range(reach):
            for c in range(cap):
                r = k * cap + c
                for kk in range(count):
                    cots.append(
                        pltpu.make_async_copy(
                            og_refs[k].at[c, pl.ds(pl.multiple_of((mi ^ kk) * quarter, quarter), quarter)],
                            og_buf.at[pl.ds(r * full + kk * quarter, quarter)],
                            sems.at[n + 1 + r * count + kk],
                        )
                    )
        for copy in groups[0] + groups[1] + cots + [sibling_hl]:
            copy.start()
        b_down, gain_f, bias_f = (v[...].reshape(1, width) for v in vec_refs)
        half = tokens // 2
        for b in range(2):
            for copy in groups[b]:
                copy.wait()
            for m in range(2):
                span = slice(m * half, (m + 1) * half)
                part = mm(hl_far[b, span, :], wd[b])
                if b == 0:
                    acc_ref[span, :] = part + near_ref[span, :]
                else:
                    acc_ref[span, :] += part
        for copy in cots:
            copy.wait()
        sums_out[...] = jnp.zeros_like(sums_out)
        for r in range(here):
            span = slice(r * full, (r + 1) * full)
            hat, inverse = norm_rows(al_ref[span, :].astype(f32) + acc_ref[span, :] + b_down)
            final = hat * gain_f + bias_f
            final_low = final.astype(bf16)
            for kk in range(count):
                (tk0, tk1)[r // cap][
                    kk, (r % cap) * quarter : (r % cap + 1) * quarter, :
                ] = final_low[kk * quarter : (kk + 1) * quarter, :]
            line = jnp.broadcast_to(segr_ref[r : r + 1, :].astype(f32), (full, full)).T[:, 0:1]
            cot = og_buf[span, :].astype(f32)
            row = sent_ref[r]
            for g in range(SEGS):
                inside = line == float(g)
                number = jnp.sum(jnp.where(inside, 1.0, 0.0), axis=0, keepdims=True)
                share = 1.0 / number
                pooled_out[r * SEGS + g : r * SEGS + g + 1, :] = (
                    jnp.sum(jnp.where(inside, final, 0.0), axis=0, keepdims=True) * share
                )
                cot = cot + jnp.where(inside, pool_ref[row, g : g + 1, :] * share, 0.0)
            e = cot * gain_f
            mean_e = jnp.mean(e, axis=1, keepdims=True)
            mean_p = jnp.mean(e * hat, axis=1, keepdims=True)
            dz = inverse * (e - mean_e - hat * mean_p)
            dz_out[span, :] = dz
            low_out[span, :] = dz.astype(bf16)
            sums_out[0:1, :] += jnp.sum(dz, axis=0, keepdims=True)
            sums_out[1:2, :] += jnp.sum(cot * hat, axis=0, keepdims=True)
            sums_out[2:3, :] += jnp.sum(cot, axis=0, keepdims=True)
        sibling_hl.wait()
        for b in range(2):
            for c in range(hidden // 256):
                cols = slice(c * 256, (c + 1) * 256)
                left = near[:, cols] if b == 0 else hl_far[1, :, cols]
                down_out[b, cols, :] = mm_tn(left, low_out[...]).astype(bf16)

    wide = (tokens, width)
    return call(
        body,
        [
            shape_of((count, cap * quarter, width)), shape_of((count, cap * quarter, width)),
            shape_of((here * SEGS, width), f32), shape_of(wide, f32), shape_of(wide),
            shape_of((8, width), f32), shape_of((2, hidden, width)),
        ],
        [VM] * 7,
        [SM, SM, VM, VM, VM, HB, VM] + [VM] * 3 + [HB] * reach + [VM] + [HB] * n,
        [
            pltpu.VMEM((2, hidden, width), bf16),
            pltpu.VMEM(wide, bf16),
            pltpu.VMEM(wide, bf16),
            pltpu.VMEM(wide, f32),
            pltpu.SemaphoreType.DMA((n + 1 + here * count,)),
        ],
        us=9,
        name="ffn_down",
        room=26,
    )(ids, sent, segr, al, acc, *hls, *vecs, *ogs, pool_grad, *flat)


def ffn_back(ids, low, gps, parts, dims):
    devices, count, rows, quarter, full, width = dims
    tokens = low.shape[0]
    hidden = width
    flat = [ref for p in parts for ref, _ in p]
    n = len(flat)

    def body(ids_ref, low_ref, gp_near, gp_far, *refs):
        dn_refs = refs[:n]
        du_out, bin_out, wd, gpb, du, sems, out_sems = refs[n:]
        parity = parity_of(ids_ref, 2)
        copies = []
        at = 0
        for kk in range(count):
            m = len(parts[kk])
            copies.append(
                load_parts(
                    dn_refs[at : at + m], bases_of(parts[kk]), parity, width // 2, wd.at[kk], sems, at
                )
                + [
                    pltpu.make_async_copy(
                        (gp_near, gp_far)[kk // 2].at[kk % 2], gpb.at[kk], sems.at[n + kk]
                    )
                ]
            )
            at += m
        outs = []
        turn = (1, 3, 2, 0)
        for kk in turn:
            for copy in copies[kk]:
                copy.start()
        half = tokens // 2
        for kk in turn:
            for copy in copies[kk]:
                copy.wait()
            total = jnp.zeros((1, hidden), f32)
            for m in range(2):
                span = slice(m * half, (m + 1) * half)
                part = (mm_nt(low_ref[span, :], wd[kk]) * gpb[kk, span, :].astype(f32)).astype(bf16)
                du[kk, span, :] = part
                total = total + jnp.sum(part.astype(f32), axis=0, keepdims=True)
            bin_out[kk : kk + 1, :] = total
            copy = pltpu.make_async_copy(du.at[kk], du_out.at[kk], out_sems.at[kk])
            copy.start()
            outs.append(copy)
        for copy in outs:
            copy.wait()

    return call(
        body,
        [shape_of((count, tokens, hidden)), shape_of((count, hidden), f32)],
        [HB, VM],
        [SM, VM, HB, HB] + [HB] * n,
        [
            pltpu.VMEM((count, hidden, width), bf16),
            pltpu.VMEM((count, tokens, hidden), bf16),
            pltpu.VMEM((count, tokens, hidden), bf16),
            pltpu.SemaphoreType.DMA((n + count,)),
            pltpu.SemaphoreType.DMA((count,)),
        ],
        us=5,
        name="ffn_back",
        room=22,
    )(ids, low, *gps, *flat)


def norm_back_attn(ids, du, al, dz, hat, inv, gain, parts, dims, after=()):
    devices, count, rows, quarter, full, width = dims
    tokens = al.shape[0]
    hidden = width
    flat = [ref for p in parts for ref, _ in p]
    n = len(flat)

    def body(ids_ref, du_ref, al_ref, dz_ref, hat_ref, inv_ref, vec_ref, *refs):
        oi_refs = refs[:n]
        dz1_out, low_out, sums_out, in_out, wi, dub, acc, sems = refs[n:]
        copies = []
        at = 0
        for kk in range(count):
            m = len(parts[kk])
            copies.append(
                [pltpu.make_async_copy(du_ref.at[kk], dub.at[kk], sems.at[n + kk])]
                + load_parts(
                    oi_refs[at : at + m], bases_of(parts[kk]), ids_ref[2], width // 2, wi.at[kk], sems, at
                )
            )
            at += m
        for group in copies:
            for copy in group:
                copy.start()
        half = tokens // 2
        for kk in range(count):
            for copy in copies[kk]:
                copy.wait()
            for m in range(2):
                span = slice(m * half, (m + 1) * half)
                part = mm_nt(dub[kk, span, :], wi[kk])
                if kk == 0:
                    acc[span, :] = part + dz_ref[span, :]
                else:
                    acc[span, :] += part
        gain_a = vec_ref[...].reshape(1, width)
        sums_out[...] = jnp.zeros_like(sums_out)

        @pl.loop(0, tokens // full)
        def _(r):
            span = pl.ds(pl.multiple_of(r * full, full), full)
            da = acc[span, :]
            hat_r = hat_ref[span, :]
            e = da * gain_a
            mean_e = jnp.mean(e, axis=1, keepdims=True)
            mean_p = jnp.mean(e * hat_r, axis=1, keepdims=True)
            dz1 = inv_ref[span, 0:1] * (e - mean_e - hat_r * mean_p)
            dz1_out[span, :] = dz1
            low_out[span, :] = dz1.astype(bf16)
            sums_out[0:1, :] += jnp.sum(dz1, axis=0, keepdims=True)
            sums_out[1:2, :] += jnp.sum(da * hat_r, axis=0, keepdims=True)
            sums_out[2:3, :] += jnp.sum(da, axis=0, keepdims=True)

        for b, kk in enumerate((1, 3)):
            for c in range(width // 256):
                cols = slice(c * 256, (c + 1) * 256)
                in_out[b, cols, :] = mm_tn(al_ref[:, cols], dub[kk]).astype(bf16)

    wide = (tokens, width)
    return call(
        body,
        [
            shape_of(wide, f32), shape_of(wide), shape_of((8, width), f32),
            shape_of((2, width, hidden)),
        ],
        [VM] * 4,
        [SM, HB, VM, VM, VM, VM, VM] + [HB] * n,
        [
            pltpu.VMEM((count, width, hidden), bf16),
            pltpu.VMEM((count, tokens, hidden), bf16),
            pltpu.VMEM(wide, f32),
            pltpu.SemaphoreType.DMA((n + count,)),
        ],
        us=8,
        name="norm_back",
        room=26,
        after=after,
    )(ids, du, al, dz, hat, inv, gain, *flat)


def attend_back(ids, low, x, blocks, extras, dims, after=()):
    devices, count, rows, quarter, full, width = dims
    here = rows // count
    tokens = x.shape[0]
    head_width = blocks[0][2].shape[2]
    inner = 3 * head_width
    flat = [ref for b in blocks for ref, _ in b[5]]
    n = len(flat)
    half_out = head_width // 2
    nb = len(blocks)

    def body(ids_ref, low_ref, x_ref, bin_ref, ffn_ref, norm_ref, *refs):
        data = refs[: 3 * nb]
        w_refs = refs[3 * nb : 3 * nb + n]
        mix_out, grad_out, wo, sums, sems = refs[3 * nb + n :]
        copies = []
        at = 0
        for b in range(nb):
            m = len(blocks[b][5])
            copies += load_parts(
                w_refs[at : at + m], bases_of(blocks[b][5]), ids_ref[2], half_out, wo.at[b], sems, at,
                inner // 2,
            )
            at += m
        for copy in copies:
            copy.start()
        for copy in copies:
            copy.wait()
        masks = head_masks(head_width)
        sums[...] = jnp.zeros_like(sums)
        for b in range(nb):
            kk, place = blocks[b][:2]
            ol_ref, qkv_ref, p_ref = data[3 * b : 3 * b + 3]

            @pl.loop(0, here)
            def _(r):
                span = pl.ds(pl.multiple_of(r * full, full), full)
                dol = mm_nt(low_ref[span, :], wo[b]).astype(bf16)
                query, key, value = (qkv_ref[place, i, span, :] for i in range(3))
                low_p = p_ref[place, r]
                prob = low_p.astype(f32)
                dos = stack_heads(dol, masks)
                dp = mm_nt(dos, value)
                ds = (prob * (dp - jnp.sum(dp * prob, axis=1, keepdims=True))).astype(bf16)
                dv = mm_tn(low_p, dos).astype(bf16)
                dq = (pick_heads(mm(ds, key), masks) * (HD ** -0.5)).astype(bf16)
                dk = (mm_tn(ds, stack_heads(query, masks)) * (HD ** -0.5)).astype(bf16)
                mix_out[b, span, 0:head_width] = dq
                mix_out[b, span, head_width : 2 * head_width] = dk
                mix_out[b, span, 2 * head_width :] = dv
                sums[b : b + 1, 0:head_width] += jnp.sum(dq.astype(f32), axis=0, keepdims=True)
                sums[b : b + 1, 256 : 256 + head_width] += jnp.sum(
                    dv.astype(f32), axis=0, keepdims=True
                )

            for c in range(3):
                part = slice(c * head_width, (c + 1) * head_width)
                grad_out[b, part, :] = mm_tn(mix_out[b, :, part], x_ref[...]).astype(bf16)
            grad_out[b, inner:width, :] = mm_tn(ol_ref[place], low_ref[...]).astype(bf16)
            lines = jnp.concatenate(
                [sums[b : b + 1], bin_ref[kk : kk + 1], norm_ref[0:3], ffn_ref[0:3]], axis=0
            )
            grad_out[b, width : width + 16, :] = two_terms(lines)

    return call(
        body,
        [shape_of((nb, tokens, inner)), shape_of((nb, width + 16, width))],
        [VM] * 2,
        [SM] + [VM] * (5 + 3 * nb) + [HB] * n,
        [
            pltpu.VMEM((nb, head_width, width), bf16),
            pltpu.VMEM((8, width), f32),
            pltpu.SemaphoreType.DMA((n,)),
        ],
        us=13,
        name="attend_back",
        room=26,
        after=after,
    )(ids, low, x, *extras, *[v for b in blocks for v in b[2:5]], *flat)


def two_terms(lines):
    high = lines.astype(bf16)
    return jnp.concatenate([high, (lines - high.astype(f32)).astype(bf16)], axis=0)


def one_term(lines):
    return lines[0:8].astype(f32) + lines[8:16].astype(f32)


def peer_grad(lhs, rhs, got, at, after=()):
    tokens, width = rhs.shape
    hidden = lhs.shape[-1]

    def body(lhs_ref, rhs_ref, got_ref, out, a_buf, g_buf, sems):
        copies = [
            pltpu.make_async_copy(lhs_ref.at[at], a_buf, sems.at[0]),
            pltpu.make_async_copy(got_ref.at[1], g_buf, sems.at[1]),
        ]
        for copy in copies:
            copy.start()
        for copy in copies:
            copy.wait()
        for c in range(hidden // 256):
            cols = slice(c * 256, (c + 1) * 256)
            out[cols, :] = (mm_tn(a_buf[:, cols], rhs_ref[...]) + g_buf[cols, :].astype(f32)).astype(
                bf16
            )

    return call(
        body,
        shape_of((hidden, width)),
        VM,
        [HB, VM, HB],
        [
            pltpu.VMEM((tokens, hidden), bf16),
            pltpu.VMEM((hidden, width), bf16),
            pltpu.SemaphoreType.DMA((2,)),
        ],
        us=3,
        name="peer_grad",
        room=10,
        after=after,
    )(lhs, rhs, got)


def shards(acc, ids_ref, devices, bits, size, send, keep):
    for p in range(devices):
        mirror = sum(((p >> j) & 1) << (bits - 1 - j) for j in range(bits))
        rows = acc[pl.ds(pl.multiple_of((ids_ref[0] ^ mirror) * size, 16), size), :]
        if p < devices // 2:
            keep[p * size : (p + 1) * size, :] = rows
        else:
            q = p - devices // 2
            send[q * size : (q + 1) * size, :] = rows.astype(bf16)


def own_grad(ids, lhs, rhs, got, crossed, devices, lhs_own, after=()):
    tokens = rhs.shape[-2]
    width = rhs.shape[-1]
    hidden = lhs.shape[-1]
    bits = devices.bit_length() - 1
    size = hidden // devices

    def body(ids_ref, lhs_ref, rhs_ref, got_ref, cross_ref, send, keep, a_buf, b_buf, g_buf, acc, sems):
        copies = [
            pltpu.make_async_copy(lhs_ref.at[0] if lhs_own else lhs_ref, a_buf, sems.at[0]),
            pltpu.make_async_copy(rhs_ref if lhs_own else rhs_ref.at[0], b_buf, sems.at[1]),
            pltpu.make_async_copy(got_ref.at[0], g_buf, sems.at[2]),
        ]
        for copy in copies:
            copy.start()
        for copy in copies:
            copy.wait()
        for c in range(hidden // 256):
            cols = slice(c * 256, (c + 1) * 256)
            acc[cols, :] = (
                mm_tn(a_buf[:, cols], b_buf[...])
                + g_buf[cols, :].astype(f32)
                + cross_ref[cols, :].astype(f32)
            )
        shards(acc, ids_ref, devices, bits, size, send, keep)

    return call(
        body,
        [shape_of((hidden // 2, width)), shape_of((hidden // 2, width), f32)],
        [VM, VM],
        [SM, HB, HB, HB, VM],
        [
            pltpu.VMEM((tokens, hidden), bf16),
            pltpu.VMEM((tokens, width), bf16),
            pltpu.VMEM((hidden, width), bf16),
            pltpu.VMEM((hidden, width), f32),
            pltpu.SemaphoreType.DMA((3,)),
        ],
        us=3,
        name="own_grad",
        room=14,
        after=after,
    )(ids, lhs, rhs, got, crossed)


def peer_grad_in(al, du, got, after=()):
    tokens, width = al.shape
    hidden = du.shape[-1]

    def body(al_ref, du_ref, got_ref, out, b_buf, g_buf, sems):
        copies = [
            pltpu.make_async_copy(du_ref.at[2], b_buf, sems.at[0]),
            pltpu.make_async_copy(got_ref.at[1], g_buf, sems.at[1]),
        ]
        for copy in copies:
            copy.start()
        for copy in copies:
            copy.wait()
        for c in range(width // 256):
            cols = slice(c * 256, (c + 1) * 256)
            out[cols, :] = (mm_tn(al_ref[:, cols], b_buf[...]) + g_buf[cols, :].astype(f32)).astype(
                bf16
            )

    return call(
        body,
        shape_of((width, hidden)),
        VM,
        [VM, HB, HB],
        [
            pltpu.VMEM((tokens, hidden), bf16),
            pltpu.VMEM((width, hidden), bf16),
            pltpu.SemaphoreType.DMA((2,)),
        ],
        us=3,
        name="peer_grad_in",
        room=10,
        after=after,
    )(al, du, got)


def peer_last(grads, got, at, after=()):
    _, high, width = grads.shape

    def body(a_ref, g_ref, out):
        out[0 : high - 16, :] = (
            a_ref[at, 0 : high - 16, :].astype(f32) + g_ref[1, 0 : high - 16, :].astype(f32)
        ).astype(bf16)
        out[high - 16 :, :] = two_terms(
            one_term(a_ref[at, high - 16 :, :]) + one_term(g_ref[1, high - 16 :, :])
        )

    return call(
        body, shape_of((high, width)), VM, [VM, VM], us=2, name="peer_last",
        room=12,
        after=after,
    )(grads, got)


def own_last(ids, grads, got, crossed, at, devices, after=()):
    _, high, width = grads.shape
    body_rows = high - 16
    bits = devices.bit_length() - 1
    size = body_rows // devices

    def body(ids_ref, a_ref, g_ref, c_ref, send, keep, vec, acc):
        acc[...] = (
            a_ref[at, 0:body_rows, :].astype(f32)
            + g_ref[0, 0:body_rows, :].astype(f32)
            + c_ref[0:body_rows, :].astype(f32)
        )
        shards(acc, ids_ref, devices, bits, size, send, keep)
        lines = (
            one_term(a_ref[at, body_rows:, :])
            + one_term(g_ref[0, body_rows:, :])
            + one_term(c_ref[body_rows:, :])
        )
        send[body_rows // 2 :, :] = two_terms(lines)
        vec[...] = lines

    return call(
        body,
        [
            shape_of((body_rows // 2 + 16, width)),
            shape_of((body_rows // 2, width), f32),
            shape_of((8, width), f32),
        ],
        [VM] * 3,
        [SM, VM, VM, VM],
        [pltpu.VMEM((body_rows, width), f32)],
        us=3,
        name="own_last",
        room=16,
        after=after,
    )(ids, grads, got, crossed)


def cut(keep, got, vec, after=()):
    high, width = keep.shape
    last = vec is not None
    tail = 16 if last else 0
    size = high // 4

    def body(*refs):
        keep_ref, got_ref = refs[:2]
        rest = refs[2:]
        if last:
            vec_ref, rest = rest[0], rest[1:]
            lines = vec_ref[...] + one_term(got_ref[high:, :])
            rest[4][...] = lines
        for p in range(4):
            span = slice(p * size, (p + 1) * size)
            total = keep_ref[span, :] + got_ref[span, :].astype(f32)
            if p == 0:
                rest[3][...] = total
            else:
                rest[p - 1][0:size, :] = total.astype(bf16)
                if last:
                    rest[p - 1][size:, :] = two_terms(lines)

    outs = [shape_of((size + tail, width))] * 3 + [shape_of((size, width), f32)]
    args = [keep, got]
    if last:
        outs.append(shape_of((8, width), f32))
        args.append(vec)
    return call(
        body, outs, [VM] * len(outs), [VM] * len(args), us=1, name="cut", room=8, after=after
    )(*args)


def gather_sum(keep, gots, vec, after=()):
    high, width = keep.shape
    last = vec is not None
    n = len(gots)

    def body(*refs):
        keep_ref, got_refs, rest = refs[0], refs[1 : 1 + n], refs[1 + n :]
        if last:
            vec_ref, rest = rest[0], rest[1:]
            lines = vec_ref[...]
            for got in got_refs:
                lines = lines + one_term(got[high:, :])
            rest[1][...] = lines
        total = keep_ref[...]
        for got in got_refs:
            total = total + got[0:high, :].astype(f32)
        rest[0][...] = total.astype(bf16)

    outs = [shape_of((high, width))]
    args = [keep, *gots]
    if last:
        outs.append(shape_of((8, width), f32))
        args.append(vec)
    return call(
        body, outs, [VM] * len(outs), [VM] * len(args), us=1, name="gather_sum", room=8, after=after
    )(*args)


def join(pieces, after=()):
    size, width = pieces[0].shape
    n = len(pieces)

    def body(*refs):
        for p in range(n):
            refs[n][p * size : (p + 1) * size, :] = refs[p][...]

    return call(
        body, shape_of((n * size, width)), VM, [VM] * n, us=1, name="join", room=4, after=after
    )(*pieces)


MASKS = (4, 2, 6)


def place_shards(ids_ref, pieces, devices, size, put):
    bits = devices.bit_length() - 1
    p = 0
    for piece in pieces:
        for q in range(piece.shape[0] // size):
            mirror = sum(((p >> j) & 1) << (bits - 1 - j) for j in range(bits))
            at = pl.multiple_of((ids_ref[0] ^ mirror) * size, 8)
            put(at, piece[q * size : (q + 1) * size, :].astype(f32))
            p += 1


def whole_grad(ids, pieces, devices, cuts, after=()):
    size, width = pieces[0].shape
    n = len(pieces)

    def body(ids_ref, *refs):
        outs = refs[n : n + len(cuts)]
        acc = refs[n + len(cuts)] if len(cuts) > 1 else outs[0]

        def put(at, rows):
            acc[pl.ds(at, size), :] = rows

        place_shards(ids_ref, refs[:n], devices, size, put)
        if len(cuts) > 1:
            base = 0
            for out, rows in zip(outs, cuts):
                out[...] = acc[base : base + rows, :]
                base += rows

    return call(
        body,
        [shape_of((rows, width), f32) for rows in cuts],
        [VM] * len(cuts),
        [SM] + [VM] * n,
        [pltpu.VMEM((size * devices, width), f32)] if len(cuts) > 1 else [],
        us=2,
        name="whole_grad",
        room=12,
        after=after,
    )(ids, *pieces)


def grad_input_rows(ids, dz1, mixes, parts, pooled, dims, after=()):
    devices, count, rows, quarter, full, width = dims
    here = rows // count
    tokens = here * full
    tile = here * quarter
    inner = mixes[0].shape[2]
    flat = [ref for p in parts for ref, _ in p]
    n = len(flat)
    turn = (1, 3, 2, 0)

    def body(ids_ref, dz_ref, m_a, m_b, pool_ref, *refs):
        w_refs = refs[:n]
        own, near, far = refs[n : n + 3]
        wq, acc, sems = refs[n + 3 :]
        copies = []
        at = 0
        for kk in range(count):
            m = len(parts[kk])
            copies.append(
                load_parts(w_refs[at : at + m], bases_of(parts[kk]), ids_ref[2], inner // 2, wq.at[kk], sems, at)
            )
            at += m
        for kk in turn:
            for copy in copies[kk]:
                copy.start()
        half = tokens // 2
        for i, kk in enumerate(turn):
            for copy in copies[kk]:
                copy.wait()
            mix = (m_a, m_b)[i // 2]
            for m in range(2):
                span = slice(m * half, (m + 1) * half)
                part = mm(mix[i % 2, span, :], wq[kk])
                if i == 0:
                    acc[span, :] = part + dz_ref[span, :]
                else:
                    acc[span, :] += part
        size = tile + here * SEGS
        for kk, (ref, base) in enumerate(piece_places((own, near, far, far), size)):
            for r in range(here):
                ref[base + r * quarter : base + (r + 1) * quarter, :] = acc[
                    r * full + kk * quarter : r * full + (kk + 1) * quarter, :
                ].astype(bf16)
            ref[base + tile : base + size, :] = pool_ref[...].astype(bf16)

    return call(
        body,
        [shape_of((m * (tile + here * SEGS), width)) for m in (1, 1, 2)],
        [VM] * 3,
        [SM] + [VM] * 4 + [HB] * n,
        [
            pltpu.VMEM((count, inner, width), bf16),
            pltpu.VMEM((tokens, width), f32),
            pltpu.SemaphoreType.DMA((n,)),
        ],
        us=6,
        name="grad_input_rows",
        room=22,
        after=after,
    )(ids, dz1, *mixes, pooled, *flat)


def land_grad(sent, pieces, dims, after=()):
    devices, count, rows, quarter, full, width = dims
    here = rows // count
    tile = here * quarter
    size = tile + here * SEGS

    def body(sent_ref, *refs):
        places = piece_places(refs[:count], size)
        out, pooled, sems = refs[count:]
        copies = []
        for kk, (ref, base) in enumerate(places):
            for j in range(here):
                at = kk * here + j
                copy = pltpu.make_async_copy(
                    ref.at[pl.ds(base + j * quarter, quarter)], out.at[sent_ref[at]], sems.at[at]
                )
                copy.start()
                copies.append(copy)
        for kk, (ref, base) in enumerate(places):
            lines = ref[base + tile : base + size, :].astype(f32)
            for j in range(here):
                pooled[sent_ref[kk * here + j]] = lines[j * SEGS : (j + 1) * SEGS]
        for copy in copies:
            copy.wait()

    return call(
        body,
        [shape_of((rows, quarter, width)), shape_of((rows, SEGS, width), f32)],
        [HB, VM],
        [SM] + [VM] * count,
        [pltpu.SemaphoreType.DMA((rows,))],
        us=2,
        name="land_grad",
        room=8,
        after=after,
    )(sent, *pieces)


def turn_output(hops, dims, after=()):
    devices, count, rows, quarter, full, width = dims
    cap, reach = rows // devices, devices // count
    part = cap * quarter
    tile = reach * part

    def body(*refs):
        hop_refs = refs[:reach]
        near, far, sems = refs[reach:]
        copies = []
        for kk, (ref, base) in enumerate(((near, 0), (far, 0), (far, tile))):
            for k in range(reach):
                copies.append(
                    pltpu.make_async_copy(
                        hop_refs[k].at[kk + 1],
                        ref.at[pl.ds(base + k * part, part)],
                        sems.at[kk * reach + k],
                    )
                )
        for copy in copies:
            copy.start()
        for copy in copies:
            copy.wait()

    return call(
        body,
        [shape_of((tile, width)), shape_of((2 * tile, width))],
        [VM, VM],
        [HB] * reach,
        [pltpu.SemaphoreType.DMA((3 * reach,))],
        us=2,
        name="turn_output",
        room=8,
        after=after,
    )(*hops)


def land_output(spots, hops, pieces, dims, after=()):
    devices, count, rows, quarter, full, width = dims
    here, cap, reach = rows // count, rows // devices, devices // count
    tile = here * quarter

    def body(spots_ref, *refs):
        hop_refs = refs[:reach]
        places = piece_places((None,) + refs[reach : reach + count - 1], tile)
        out, sems = refs[reach + count - 1 :]
        copies = []
        for kk in range(count):
            for j in range(here):
                at = kk * here + j
                if kk == 0:
                    src = hop_refs[j // cap].at[0, pl.ds((j % cap) * quarter, quarter)]
                else:
                    ref, base = places[kk]
                    src = ref.at[pl.ds(base + j * quarter, quarter)]
                copies.append(pltpu.make_async_copy(src, out.at[spots_ref[at]], sems.at[at]))
        for copy in copies:
            copy.start()
        for copy in copies:
            copy.wait()

    return call(
        body,
        shape_of((rows, quarter, width)),
        HB,
        [SM] + [VM] * (reach + count - 1),
        [pltpu.SemaphoreType.DMA((rows,))],
        us=2,
        name="land_output",
        room=8,
        after=after,
    )(spots, *hops, *pieces)


def swap(values, axis, bit):
    return lax.ppermute(values, axis, [(i, i ^ bit) for i in range(lax.axis_size(axis))])


def per_device(
    tokens_in, seg, route, w_qkv, b_qv, w_out, b_out, gain_attn, bias_attn, w_in, b_in, w_down,
    b_down, gain_ffn, bias_ffn, out_grad, pool_grad,
):
    devices, count = lax.axis_size("dp"), lax.axis_size("mp")
    rows, quarter, width = tokens_in.shape
    full = seg.shape[1]
    dims = (devices, count, rows, quarter, full, width)
    reach = devices // count
    head_width = w_qkv.shape[2]
    inner = 3 * head_width

    def hop(values, k):
        return lax.ppermute(
            values,
            ("dp", "mp"),
            [
                (s * count + f, (s ^ (f + count * k)) * count + f)
                for s in range(devices)
                for f in range(count)
            ],
        )

    wq = w_qkv.transpose(1, 2, 0).reshape(inner, width)
    half_rows = (inner + head_width) // 2
    *sends, segr, sent, spots, ids = prep_rows(
        route, seg, tokens_in, b_qv, b_in, (wq, w_out), dims
    )
    pieces = exchange(*sends)

    def sibling(values):
        return tuple(swap(v, "mp", 1) for v in values)

    def later(values, after):
        return lax.optimization_barrier((values, after))[0]

    def crossed(half, bit, first, second):
        direct = later(swap(half, "mp", 2), first)
        relayed = swap(direct, "dp", bit)
        far = (direct, relayed)
        return [
            [(v, 0) for v in far],
            [(swap(direct, "mp", 1), 0), (swap(later(relayed, second), "mp", 1), 0)],
        ]

    below = sends[2].shape[0] - half_rows
    relay_q = swap(pieces[2][below:], "dp", 1)
    near_q, near_o = sibling((wq, w_out))
    near_i, near_d = sibling((w_in, w_down))
    half_in = prep_halves((w_in,), 1, (pieces[2],))
    x, ol_a, qkv_a, p_a = attend(
        ids, segr, pieces, [[(wq, 0)], [(near_q, 0)]], (0, 1), inner, dims, True,
        (near_o, near_i, near_d, half_in),
    )
    relay_q3 = swap(later(relay_q, x), "mp", 1)
    far_q = [(pieces[2], below), (relay_q, 0)]
    far_q3 = [(pieces[3], below), (relay_q3, 0)]
    half_dn = prep_halves((w_down,), 2, (x,))
    og_sends = prep_cot(spots, out_grad, dims, (half_dn,))
    ogs = [hop(og_sends[k], k) for k in range(reach)]
    ol_b, qkv_b, p_b = attend(
        ids, segr, pieces, [far_q, far_q3], (2, 3), inner, dims, False, (og_sends[0],)
    )
    q_parts = [[(wq, 0)], [(near_q, 0)], far_q, far_q3]
    wo_parts = [[(w_out, 0)], [(near_o, 0)], far_q, far_q3]
    al, hat, inv, acc, hl, gp = ffn_near(
        ids, x, (ol_a, ol_b), pieces, (b_out, gain_attn, bias_attn), wo_parts, (w_in, near_i),
        (w_down, near_d), inner, dims,
    )
    in_parts = [[(w_in, 0)], [(near_i, 0)], *crossed(half_in, 1, x, ol_b)]
    dn_parts = [[(w_down, 0)], [(near_d, 0)], *crossed(half_dn, 2, ol_b, al)]
    hl_far, gp_far = ffn_far(ids, al, pieces, in_parts[2:], dims)
    tk0, tk1, pooled, dz, low, ffn_sums, down_pair = ffn_down(
        ids, sent, segr, al, acc, (hl, hl_far), (b_down, gain_ffn, bias_ffn), ogs, pool_grad,
        dn_parts[2:], dims,
    )
    got_down = swap(down_pair, "mp", 1)
    du, bin_sums = ffn_back(ids, low, (gp, gp_far), dn_parts, dims)
    down_far = peer_grad(hl_far, low, got_down, 0, (bin_sums,))
    hops = [hop(t, k) for k, t in enumerate(lax.optimization_barrier((tk0, tk1, down_far))[:2])]
    crossed_down = swap(down_far, "mp", 2)
    dz1, low1, norm_sums, in_pair = norm_back_attn(
        ids, du, al, dz, hat, inv, gain_attn, in_parts, dims, (down_far,)
    )
    got_in = swap(in_pair, "mp", 1)
    extras = (bin_sums, ffn_sums, norm_sums)
    mix_a, grads_a = attend_back(
        ids, low1, x,
        [(1, 1, ol_a, qkv_a, p_a, wo_parts[1]), (3, 1, ol_b, qkv_b, p_b, wo_parts[3])],
        extras, dims,
    )
    got_last = swap(grads_a, "mp", 1)
    in_far = peer_grad_in(al, du, got_in, (grads_a,))
    crossed_in = swap(in_far, "mp", 2)
    turned = turn_output(hops, dims, (in_far,))
    send_down, keep_down = own_grad(
        ids, hl, low, got_down, crossed_down, devices, True, (turned[0],)
    )
    mix_b, grads_b = attend_back(
        ids, low1, x,
        [(2, 0, ol_b, qkv_b, p_b, wo_parts[2]), (0, 0, ol_a, qkv_a, p_a, wo_parts[0])],
        extras, dims, (send_down,),
    )
    last_far = peer_last(grads_b, got_last, 0)
    crossed_last = swap(last_far, "mp", 2)

    def places_of(parts):
        return [swap(part, "dp", mask) for part, mask in zip(parts, MASKS)]

    cut_down = cut(keep_down, swap(send_down, "dp", 1), None, (last_far,))
    down_places = places_of(cut_down[:3])
    gx = grad_input_rows(ids, dz1, (mix_a, mix_b), q_parts, pooled, dims, (cut_down[0],))
    (shard_down,) = gather_sum(cut_down[3], down_places, None, (gx[0],))
    down_spread = [shard_down] + places_of([shard_down] * 3)
    send_in, keep_in = own_grad(
        ids, al, du, got_in, crossed_in, devices, False, (shard_down,)
    )
    in_half = swap(send_in, "dp", 1)
    half_down = join(down_spread, (send_in,))
    down_spread.append(swap(half_down, "dp", 1))
    cut_in = cut(keep_in, in_half, None, (half_down,))
    in_places = places_of(cut_in[:3])
    send, keep, vec = own_last(
        ids, grads_b, got_last, crossed_last, 1, devices, (cut_in[0],)
    )
    last_half = swap(send, "dp", 1)
    (shard_in,) = gather_sum(cut_in[3], in_places, None, (send,))
    in_spread = [shard_in] + places_of([shard_in] * 3)
    cut_last = cut(keep, last_half, vec, (shard_in,))
    last_places = places_of(cut_last[:3])
    *gx, turned_near, turned_far, _ = lax.optimization_barrier((*gx, *turned, cut_last[0]))
    landed = exchange(None, turned_near, turned_far)[1:]
    gx_landed = exchange(*gx)
    half_in = join(in_spread, (cut_last[0],))
    in_spread.append(swap(half_in, "dp", 1))
    shard_last, vec = gather_sum(cut_last[3], last_places, cut_last[4], (half_in,))
    last_spread = [shard_last] + places_of([shard_last] * 3)
    tokens_out = land_output(spots, hops, landed, dims, (shard_last,))
    grad_input, pooled_out = land_grad(sent, gx_landed, dims, (shard_last,))
    (g_down,) = whole_grad(ids, down_spread, devices, (width,), (shard_last,))
    half_last = join(last_spread, (g_down,))
    last_spread.append(swap(half_last, "dp", 1))
    (g_in,) = whole_grad(ids, in_spread, devices, (width,), (half_last,))
    g_qkv, g_out = whole_grad(ids, last_spread, devices, (inner, head_width))
    g_qkv = g_qkv.reshape(3, head_width, width).transpose(2, 0, 1)
    g_bqv = jnp.stack([vec[0, :head_width], vec[0, 256 : 256 + head_width]])
    return (
        tokens_out, pooled_out, grad_input, g_qkv, g_bqv, g_out,
        vec[2], vec[3], vec[4], g_in, vec[1], g_down, vec[5], vec[6], vec[7],
    )


def solution(mesh):
    devices, count = mesh.shape["dp"], mesh.shape["mp"]

    def body(*args):
        rows = args[0].shape[0]
        even = rows % devices == 0 and devices % count == 0 and count == 4
        even = even and devices & (devices - 1) == 0 and rows // count == 2 * (rows // devices)
        return (per_device if even else per_device_general)(*args)

    return jax.shard_map(
        body,
        mesh=mesh,
        in_specs=(
            P("dp", "mp", None),
            P(),
            P(),
            P(None, None, "mp"),
            P(None, "mp"),
            P("mp", None),
            P(),
            P(),
            P(),
            P(None, "mp"),
            P("mp"),
            P("mp", None),
            P(),
            P(),
            P(),
            P("dp", None, None),
            P("dp", None, None),
        ),
        out_specs=(
            P("dp", "mp", None),
            P("dp", None, None),
            P("dp", "mp", None),
            P(None, None, "mp"),
            P(None, "mp"),
            P("mp", None),
            P(),
            P(),
            P(),
            P(None, "mp"),
            P("mp"),
            P("mp", None),
            P(),
            P(),
            P(),
        ),
        check_vma=False,
    )
```

```python
import jax
import jax.numpy as jnp
from jax import lax
from jax.experimental import pallas as pl
from jax.experimental.pallas import tpu as pltpu
from jax.sharding import PartitionSpec as P

HD = 64
SEGS = 4


EPSILON = 1e-12
MASKED = -1e30
f32 = jnp.float32
bf16 = jnp.bfloat16


def normalize(values):
    centre = values - jnp.mean(values, axis=-1, keepdims=True)
    scale_inv = lax.rsqrt(jnp.mean(centre * centre, axis=-1, keepdims=True) + EPSILON)
    return (centre * scale_inv, scale_inv[..., 0])


def norm_back(grad_hat, normed_hat, inverse):
    mean_grad = jnp.mean(grad_hat, axis=-1, keepdims=True)
    mean_proj = jnp.mean(grad_hat * normed_hat, axis=-1, keepdims=True)
    return inverse[..., None] * (grad_hat - mean_grad - normed_hat * mean_proj)


def pack_rows(values, position, filled):
    picked = jnp.take(values, position, axis=0)
    shape_mask = filled.reshape((-1,) + (1,) * (values.ndim - 1))
    return jnp.where(shape_mask, picked, jnp.zeros_like(picked))


def per_device_general(
    tokens_in,
    seg,
    route,
    w_qkv,
    b_qv,
    w_out,
    b_out,
    gain_attn,
    bias_attn,
    w_in,
    b_in,
    w_down,
    b_down,
    gain_ffn,
    bias_ffn,
    out_grad,
    pool_grad,
):
    f32 = jnp.float32
    bf16 = jnp.bfloat16
    devices = lax.axis_size("dp")
    row_local = tokens_in.shape[0]
    quarter = tokens_in.shape[1]
    all_rows = route.shape[0]
    capacity = max(1, row_local // devices)
    buffer_len = devices * capacity
    my_index = lax.axis_index("dp")
    target_dev = route // row_local
    dest_grid = target_dev.reshape(devices, row_local)
    before = jnp.arange(row_local)[None, :] < jnp.arange(row_local)[:, None]
    same_dest = dest_grid[:, :, None] == dest_grid[:, None, :]
    earlier_count = (
        jnp.sum(jnp.where(same_dest & before[None], 1, 0), axis=2).reshape(-1).astype(jnp.int32)
    )
    slot_out = target_dev * capacity + earlier_count
    slot_in = jnp.arange(all_rows, dtype=jnp.int32) // row_local * capacity + earlier_count
    own_slots = lax.dynamic_slice_in_dim(slot_out, my_index * row_local, row_local)
    local_rows = jnp.arange(row_local, dtype=jnp.int32)
    send_pos = jnp.zeros(buffer_len, jnp.int32).at[own_slots].set(local_rows)
    send_fill = jnp.zeros(buffer_len, jnp.bool_).at[own_slots].set(True)
    arrive = jnp.where(target_dev == my_index, route - my_index * row_local, row_local)
    recv_pos = jnp.zeros(row_local, jnp.int32).at[arrive].set(slot_in, mode="drop")
    anchor = (
        jnp.zeros(row_local, jnp.int32)
        .at[arrive]
        .set(jnp.arange(all_rows, dtype=jnp.int32), mode="drop")
    )
    back_pos = jnp.zeros(buffer_len, jnp.int32).at[recv_pos].set(local_rows)
    back_fill = jnp.zeros(buffer_len, jnp.bool_).at[recv_pos].set(True)
    arrived = lax.all_to_all(
        pack_rows(tokens_in, send_pos, send_fill), "dp", split_axis=0, concat_axis=0, tiled=True
    )
    rows_x = jnp.take(arrived, recv_pos, axis=0)
    segment = jnp.take(seg, anchor, axis=0)
    full_len = segment.shape[1]
    mp_index = lax.axis_index("mp")

    def own_part(values):
        return lax.dynamic_slice_in_dim(values, mp_index * quarter, quarter, 1)

    gathered = lax.all_gather(rows_x, "mp", axis=1, tiled=True)
    head_width = w_qkv.shape[2]
    local_heads = head_width // HD
    head_shape = (row_local, full_len, local_heads, HD)
    projected = jnp.einsum("rsd,dcf->rscf", gathered, w_qkv, preferred_element_type=f32)
    query_heads = (projected[:, :, 0] + b_qv[0]).astype(bf16).reshape(head_shape)
    key_heads = projected[:, :, 1].astype(bf16).reshape(head_shape)
    value_heads = (projected[:, :, 2] + b_qv[1]).astype(bf16).reshape(head_shape)
    allowed = (segment[:, :, None] == segment[:, None, :])[:, None]
    factor = HD ** (-0.5)

    def scores_of():
        raw_scores = (
            jnp.einsum("rqhe,rkhe->rhqk", query_heads, key_heads, preferred_element_type=f32)
            * factor
        )
        return jnp.where(allowed, raw_scores, MASKED)

    scores = scores_of()
    row_peak = jnp.max(scores, axis=-1, keepdims=True)
    raised = jnp.exp(scores - row_peak)
    weight_total = jnp.sum(raised, axis=-1, keepdims=True)
    log_total = row_peak + jnp.log(weight_total)
    attention = raised / weight_total
    attended = jnp.einsum(
        "rhqk,rkhe->rqhe", attention.astype(bf16), value_heads, preferred_element_type=f32
    )
    attended = attended.astype(bf16).reshape(row_local, full_len, head_width)
    branch = jnp.einsum("rsf,fd->rsd", attended, w_out, preferred_element_type=f32)
    summed_branch = lax.psum_scatter(branch, "mp", scatter_dimension=1, tiled=True)
    hat_attn, inv_attn = normalize(rows_x.astype(f32) + summed_branch + b_out)
    normed_low = (hat_attn * gain_attn + bias_attn).astype(bf16)
    normed_all = lax.all_gather(normed_low, "mp", axis=1, tiled=True)
    hidden = jnp.einsum("rsd,df->rsf", normed_all, w_in, preferred_element_type=f32) + b_in
    active, gelu_back = jax.vjp(lambda values: jax.nn.gelu(values, approximate=False), hidden)
    active_low = active.astype(bf16)
    ffn_part = jnp.einsum("rsf,fd->rsd", active_low, w_down, preferred_element_type=f32)
    ffn_total = lax.psum(ffn_part, "mp")
    hat_ffn, inv_ffn = normalize(normed_all.astype(f32) + ffn_total + b_down)
    block_out = hat_ffn * gain_ffn + bias_ffn
    output_rows = own_part(block_out).astype(bf16)
    member = (segment[:, :, None] == jnp.arange(SEGS)[None, None, :]).astype(f32)
    counts = jnp.sum(member, axis=1)
    pooled_rows = (
        jnp.einsum("rsg,rsd->rgd", member, block_out, precision=lax.Precision.HIGHEST)
        / counts[:, :, None]
    )
    pooled_back = lax.all_to_all(
        pack_rows(pooled_rows, back_pos, back_fill).astype(jnp.bfloat16),
        "dp",
        split_axis=0,
        concat_axis=0,
        tiled=True,
    ).astype(jnp.float32)
    pooled = jnp.take(pooled_back, own_slots, axis=0)
    pool_arrived = lax.all_to_all(
        pack_rows(pool_grad, send_pos, send_fill), "dp", split_axis=0, concat_axis=0, tiled=True
    )
    pool_rows = jnp.take(pool_arrived, recv_pos, axis=0)
    grad_final = out_grad.astype(f32) + jnp.einsum(
        "rsg,rgd->rsd", member, pool_rows / counts[:, :, None], precision=lax.Precision.HIGHEST
    )
    grad_mix = norm_back(grad_final * gain_ffn, hat_ffn, inv_ffn)
    grad_gain_ffn = jnp.sum(grad_final * hat_ffn, axis=(0, 1))
    grad_bias_ffn = jnp.sum(grad_final, axis=(0, 1))
    grad_b_down = jnp.sum(grad_mix, axis=(0, 1))
    mix_low = grad_mix.astype(bf16)
    grad_w_down = jnp.einsum("rsf,rsd->fd", active_low, mix_low, preferred_element_type=f32)
    grad_active = jnp.einsum("rsd,fd->rsf", mix_low, w_down, preferred_element_type=f32)
    grad_hidden = gelu_back(grad_active)[0].astype(bf16)
    grad_w_in = jnp.einsum("rsd,rsf->df", normed_all, grad_hidden, preferred_element_type=f32)
    grad_b_in = jnp.sum(grad_hidden.astype(f32), axis=(0, 1))
    normed_part = jnp.einsum("rsf,df->rsd", grad_hidden, w_in, preferred_element_type=f32)
    grad_normed = lax.psum_scatter(normed_part, "mp", scatter_dimension=1, tiled=True) + own_part(
        grad_mix
    )
    gain_attn_part = jnp.sum(grad_normed * hat_attn, axis=(0, 1))
    bias_attn_part = jnp.sum(grad_normed, axis=(0, 1))
    grad_inner = norm_back(grad_normed * gain_attn, hat_attn, inv_attn)
    stat_terms = jnp.stack([jnp.sum(grad_inner, axis=(0, 1)), gain_attn_part, bias_attn_part])[None]
    inner_all, stats_all = (
        lax.all_gather(grad_inner.astype(jnp.bfloat16), "mp", axis=1, tiled=True).astype(
            grad_inner.dtype
        ),
        lax.all_gather(stat_terms.astype(jnp.bfloat16), "mp", axis=0, tiled=True).astype(
            stat_terms.dtype
        ),
    )
    stat_sums = jnp.sum(stats_all, axis=0)
    inner_low = inner_all.astype(bf16)
    grad_w_out = jnp.einsum("rsf,rsd->fd", attended, inner_low, preferred_element_type=f32)
    grad_attended = (
        jnp.einsum("rsd,fd->rsf", inner_low, w_out, preferred_element_type=f32)
        .astype(bf16)
        .reshape(head_shape)
    )
    again = jnp.exp(scores_of() - log_total)
    grad_prob = jnp.einsum(
        "rqhe,rkhe->rhqk", grad_attended, value_heads, preferred_element_type=f32
    )
    grad_values = jnp.einsum(
        "rhqk,rqhe->rkhe", again.astype(bf16), grad_attended, preferred_element_type=f32
    )
    grad_scores = (again * (grad_prob - jnp.sum(grad_prob * again, axis=-1, keepdims=True))).astype(
        bf16
    )
    grad_query = (
        jnp.einsum("rhqk,rkhe->rqhe", grad_scores, key_heads, preferred_element_type=f32) * factor
    ).astype(bf16)
    grad_keys = (
        jnp.einsum("rhqk,rqhe->rkhe", grad_scores, query_heads, preferred_element_type=f32) * factor
    ).astype(bf16)
    flat_shape = (row_local, full_len, head_width)
    grad_mixed = jnp.stack(
        [
            grad_query.reshape(flat_shape),
            grad_keys.reshape(flat_shape),
            grad_values.astype(bf16).reshape(flat_shape),
        ],
        axis=2,
    )
    grad_w_qkv = jnp.einsum("rsd,rscf->dcf", gathered, grad_mixed, preferred_element_type=f32)
    grad_b_qv = jnp.stack(
        [
            jnp.sum(grad_mixed[:, :, 0].astype(f32), axis=(0, 1)),
            jnp.sum(grad_mixed[:, :, 2].astype(f32), axis=(0, 1)),
        ]
    )
    input_part = jnp.einsum("rscf,dcf->rsd", grad_mixed, w_qkv, preferred_element_type=f32)
    grad_rows = (
        lax.psum_scatter(input_part, "mp", scatter_dimension=1, tiled=True) + grad_inner
    ).astype(bf16)
    grad_home = lax.all_to_all(
        pack_rows(grad_rows, back_pos, back_fill), "dp", split_axis=0, concat_axis=0, tiled=True
    )
    grad_input = jnp.take(grad_home, own_slots, axis=0)
    vector_grads = jnp.stack(
        [stat_sums[0], stat_sums[1], stat_sums[2], grad_b_down, grad_gain_ffn, grad_bias_ffn]
    )
    totals = lax.psum(
        (grad_w_qkv, grad_b_qv, grad_w_out, grad_w_in, grad_b_in, grad_w_down, vector_grads), "dp"
    )
    return (
        output_rows,
        pooled,
        grad_input,
        totals[0],
        totals[1],
        totals[2],
        totals[6][0],
        totals[6][1],
        totals[6][2],
        totals[3],
        totals[4],
        totals[5],
        totals[6][3],
        totals[6][4],
        totals[6][5],
    )


VM = pl.BlockSpec(memory_space=pltpu.VMEM)
SM = pl.BlockSpec(memory_space=pltpu.SMEM)
HB = pl.BlockSpec(memory_space=pl.ANY)
HM = pl.BlockSpec(memory_space=pltpu.HBM)
MIB = 1024 * 1024
PACE = 2e9


def shape_of(shape, dtype=bf16):
    return jax.ShapeDtypeStruct(shape, dtype)


def call(
    body, outs, out_specs, in_specs, scratch=(), us=2, room=16, name=None, after=()
):
    made = pl.pallas_call(
        body,
        out_shape=outs,
        in_specs=in_specs,
        out_specs=out_specs,
        scratch_shapes=list(scratch),
        compiler_params=pltpu.CompilerParams(vmem_limit_bytes=room * MIB),
        cost_estimate=pl.CostEstimate(flops=int(us * PACE), bytes_accessed=0, transcendentals=0),
        name=name,
    )

    def run(*args):
        if after:
            args = list(args)
            at = min(range(len(args)), key=lambda n: args[n].size)
            args[at] = lax.optimization_barrier((args[at], *after))[0]
        return made(*args)

    return run


def mm(a, b):
    return lax.dot_general(a, b, (((1,), (0,)), ((), ())), preferred_element_type=f32)


def mm_nt(a, b):
    return lax.dot_general(a, b, (((1,), (1,)), ((), ())), preferred_element_type=f32)


def mm_tn(a, b):
    return lax.dot_general(a, b, (((0,), (0,)), ((), ())), preferred_element_type=f32)


def split3(values):
    high = values.astype(bf16)
    rest = values - high.astype(f32)
    middle = rest.astype(bf16)
    low = (rest - middle.astype(f32)).astype(bf16)
    return high, middle, low


def piece_places(refs, size):
    return [(refs[0], 0), (refs[1], 0), (refs[2], 0), (refs[3], size)]


def exchange(own, near, far, before=()):
    near = swap(near, "mp", 1)
    crossed = swap(far, "mp", 2)
    if before:
        crossed = lax.optimization_barrier((crossed, near, *before))[0]
    return [own, near, crossed, swap(crossed, "mp", 1)]


def prep_rows(route, seg, tokens, b_qv, b_in, weights, dims):
    devices, count, rows, quarter, full, width = dims
    here, cap = rows // count, rows // devices
    head_width = b_qv.shape[1]
    tile = here * quarter
    total = devices * rows
    halves = [w.shape[0] // 2 for w in weights]

    def body(
        route_ref, seg_ref, tok, bqv_ref, bin_ref, wq, wo, x0, x1, far, segr, sent_ref, spots_ref,
        ids_ref, lists, sems,
    ):
        my, mi = lax.axis_index("dp"), lax.axis_index("mp")
        crossing = []
        base = 2 * (tile + 16)
        for n, (src, half) in enumerate(zip((wq, wo), halves)):
            crossing.append(
                pltpu.make_async_copy(
                    src.at[pl.ds(pl.multiple_of(lax.rem(my, 2) * half, 16), half)],
                    far.at[pl.ds(base, half)],
                    sems.at[rows + 2 + n],
                )
            )
            crossing[n].start()
            base += half
        ids_ref[0] = my
        ids_ref[1] = mi
        ids_ref[2] = lax.rem(my, 2)
        places = piece_places((x0, x1, far, far), tile + 16)
        across = jnp.broadcast_to(route_ref[...].reshape(1, total), (total, total)).astype(f32)
        down = across.T.astype(jnp.int32)
        across = across.astype(jnp.int32)
        r = lax.broadcasted_iota(jnp.int32, (total, total), 0)
        c = lax.broadcasted_iota(jnp.int32, (total, total), 1)
        key_down = lax.div(down, rows) * total + r
        key_across = lax.div(across, rows) * total + c
        before = (lax.div(r, rows) == lax.div(c, rows)) & (key_across < key_down)
        rank = jnp.sum(jnp.where(before, 1.0, 0.0), axis=1, keepdims=True).astype(jnp.int32)
        at = lax.rem(c, rows)
        partner = my ^ ((mi ^ lax.div(at, here)) + count * lax.rem(lax.div(at, cap), here // cap))
        copy_at = lax.rem(at, cap)
        source = lax.div(r, rows)
        going = (source == my) & (rank == partner * cap + copy_at)
        coming = (source == partner) & (rank == my * cap + copy_at)
        lists[0:1, :] = jnp.sum(
            jnp.where(going, lax.rem(r, rows), 0).astype(f32), axis=0, keepdims=True
        ).astype(jnp.int32)
        lists[1:2, :] = jnp.sum(
            jnp.where(coming, down - my * rows, 0).astype(f32), axis=0, keepdims=True
        ).astype(jnp.int32)
        moves = [
            pltpu.make_async_copy(lists.at[0], sent_ref, sems.at[rows]),
            pltpu.make_async_copy(lists.at[1], spots_ref, sems.at[rows + 1]),
        ]
        for move in moves:
            move.start()
        zero = jnp.zeros((16, width), bf16)
        tail = x0.at[pl.ds(tile, 16)]
        tail[...] = zero
        for n, term in enumerate(split3(bqv_ref[...])):
            tail[n : n + 1, 0:head_width] = term[0:1]
            tail[n : n + 1, 256 : 256 + head_width] = term[1:2]
        for n, term in enumerate(split3(bin_ref[...].reshape(1, width))):
            tail[3 + n : 4 + n, :] = term
        for ref, base in places[1:]:
            ref[base + tile : base + tile + 16, :] = tail[...]
        for move in moves:
            move.wait()
        copies = []
        for kk in reversed(range(count)):
            for n in range(here):
                k = kk * here + n
                copies.append(
                    pltpu.make_async_copy(
                        tok.at[sent_ref[k]],
                        places[kk][0].at[pl.ds(places[kk][1] + n * quarter, quarter)],
                        sems.at[k],
                    )
                )
        for copy in copies:
            copy.start()
        for n in range(here):
            segr[n : n + 1, :] = seg_ref[pl.ds(my * rows + sent_ref[n], 1), :]
        segr[here:8, :] = jnp.zeros((8 - here, full), jnp.int32)
        lane = lax.broadcasted_iota(jnp.int32, (8, full), 1)
        lines = segr[...]
        bit = 1
        while bit < count:
            step = bit * quarter
            swapped = jnp.where(
                lax.rem(lax.div(lane, step), 2) == 0,
                pltpu.roll(lines, full - step, 1),
                pltpu.roll(lines, step, 1),
            )
            lines = jnp.where(lax.rem(lax.div(mi, bit), 2) == 1, swapped, lines)
            bit *= 2
        segr[...] = lines
        for copy in copies + crossing:
            copy.wait()

    return call(
        body,
        [
            shape_of((tile + 16, width)),
            shape_of((tile + 16, width)),
            shape_of((2 * (tile + 16) + sum(halves), width)),
        ]
        + [
            shape_of((8, full), jnp.int32),
            shape_of((total,), jnp.int32),
            shape_of((total,), jnp.int32),
            shape_of((3,), jnp.int32),
        ],
        [VM] * 4 + [SM] * 3,
        [VM, VM, HM, VM, VM, HM, HM],
        [pltpu.VMEM((8, total), jnp.int32), pltpu.SemaphoreType.DMA((rows + 4,))],
        us=2,
        name="prep_rows",
        room=60,
    )(route, seg, tokens, b_qv, b_in, *weights)


def prep_halves(weights, bit, after=()):
    width = weights[0].shape[1]
    halves = [w.shape[0] // 2 for w in weights]
    n = len(weights)

    def body(*refs):
        out, sems = refs[n:]
        parity = lax.rem(lax.div(lax.axis_index("dp"), bit), 2)
        copies = []
        base = 0
        for at, half in enumerate(halves):
            copies.append(
                pltpu.make_async_copy(
                    refs[at].at[pl.ds(pl.multiple_of(parity * half, 16), half)],
                    out.at[pl.ds(base, half)],
                    sems.at[at],
                )
            )
            base += half
        for copy in copies:
            copy.start()
        for copy in copies:
            copy.wait()

    return call(
        body,
        shape_of((sum(halves), width)),
        VM,
        [HM] * n,
        [pltpu.SemaphoreType.DMA((n,))],
        us=0.1,
        name="prep_halves",
        room=4,
        after=after,
    )(*weights)


def prep_cot(asked, out_grad, dims, after):
    devices, count, rows, quarter, full, width = dims
    cap, reach = rows // devices, devices // count

    def body(asked_ref, og, *refs):
        outs, sems = refs[:reach], refs[reach]
        copies = []
        for k in range(reach):
            for c in range(cap):
                at = k * cap + c
                copies.append(
                    pltpu.make_async_copy(og.at[asked_ref[at]], outs[k].at[c], sems.at[at])
                )
        for copy in copies:
            copy.start()
        for copy in copies:
            copy.wait()

    return call(
        body,
        [shape_of((cap, full, width))] * reach,
        [VM] * reach,
        [SM, HM],
        [pltpu.SemaphoreType.DMA((reach * cap,))],
        us=0.1,
        name="prep_cot",
        room=6,
        after=after,
    )(asked, out_grad)


def bias_rows(piece, at, count):
    terms = piece[at : at + 16, :].astype(f32)
    first = 0 if count == 0 else 3
    return terms[first : first + 1] + terms[first + 1 : first + 2] + terms[first + 2 : first + 3]


def head_masks(head_width):
    lane = lax.broadcasted_iota(jnp.int32, (1, head_width), 1)
    return [(lane >= h * HD) & (lane < (h + 1) * HD) for h in range(head_width // HD)]


def stack_heads(values, masks):
    zero = jnp.zeros_like(values)
    return jnp.concatenate([jnp.where(mask, values, zero) for mask in masks], axis=0)


def pick_heads(stacked, masks):
    size = stacked.shape[0] // len(masks)
    out = stacked[:size]
    for h in range(1, len(masks)):
        out = jnp.where(masks[h], stacked[h * size : (h + 1) * size], out)
    return out


def parity_of(ids_ref, bit):
    return lax.rem(lax.div(ids_ref[0], bit), 2)


def whole_block(refs, bases, parity, half, dst, row=0):
    if len(refs) == 1:
        return refs[0]
    for ref, base, place in zip(refs, bases, (parity, 1 - parity)):
        dst[pl.ds(pl.multiple_of(place * half, 16), half), :] = ref[
            base + row : base + row + half, :
        ]
    return dst


def bases_of(part):
    return [base for _, base in part]


def attend(ids, segr, pieces, parts, pair, inner, dims, keep_x, after=()):
    devices, count, rows, quarter, full, width = dims
    here = rows // count
    tokens = here * full
    tile = here * quarter
    head_width = inner // 3
    n_heads = head_width // HD
    n_parts = [len(p) for p in parts]
    flat = [ref for p in parts for ref, _ in p]

    def body(ids_ref, segr_ref, *refs):
        places = piece_places(refs[:count], tile + 16)
        w_refs = refs[count : count + len(flat)]
        out = list(refs[count + len(flat) :])
        if keep_x:
            x_out = out.pop(0)
        ol_out, qkv_out, p_out, x_ref, w_ref = out
        blocks = []
        at = 0
        for b, n in enumerate(n_parts):
            blocks.append(
                whole_block(w_refs[at : at + n], bases_of(parts[b]), ids_ref[2], inner // 2, w_ref.at[b])
            )
            at += n
        for r in range(here):
            for kk in range(count):
                ref, base = places[kk]
                x_ref[r * full + kk * quarter : r * full + (kk + 1) * quarter, :] = ref[
                    base + r * quarter : base + (r + 1) * quarter, :
                ]
        if keep_x:
            x_out[...] = x_ref[...]
        masks = head_masks(head_width)
        for b in range(2):
            ref, base = places[pair[b]]
            bias = bias_rows(ref, base + tile, 0)
            bias_q, bias_v = bias[:, 0:head_width], bias[:, 256 : 256 + head_width]

            @pl.loop(0, here)
            def _(r):
                start = pl.multiple_of(r * full, full)
                projected = mm_nt(x_ref[pl.ds(start, full), :], blocks[b][...])
                query = (projected[:, 0:head_width] + bias_q).astype(bf16)
                key = projected[:, head_width : 2 * head_width].astype(bf16)
                value = (projected[:, 2 * head_width :] + bias_v).astype(bf16)
                line = segr_ref[pl.ds(r, 1), :].astype(f32)
                wide = jnp.broadcast_to(line, (full, full))
                allowed = wide == wide.T
                stacked = stack_heads(query, masks)
                raw = mm_nt(stacked, key) * (HD ** -0.5)
                allowed3 = jnp.concatenate([allowed] * n_heads, axis=0)
                scores = jnp.where(allowed3, raw, MASKED)
                raised = jnp.exp(scores - jnp.max(scores, axis=1, keepdims=True))
                prob = raised / jnp.sum(raised, axis=1, keepdims=True)
                low = prob.astype(bf16)
                attended = pick_heads(mm(low, value), masks).astype(bf16)
                ol_out[b, pl.ds(start, full), :] = attended
                qkv_out[b, 0, pl.ds(start, full), :] = query
                qkv_out[b, 1, pl.ds(start, full), :] = key
                qkv_out[b, 2, pl.ds(start, full), :] = value
                p_out[b, r] = low

    outs = [
        shape_of((2, tokens, head_width)),
        shape_of((2, 3, tokens, head_width)),
        shape_of((2, here, n_heads * full, full)),
    ]
    if keep_x:
        outs = [shape_of((tokens, width))] + outs
    return call(
        body,
        outs,
        [VM] * len(outs),
        [SM, VM] + [VM] * (count + len(flat)),
        [
            pltpu.VMEM((tokens, width), bf16),
            pltpu.VMEM((2, inner, width), bf16),
        ],
        us=10,
        name="attend",
        room=18,
        after=after,
    )(ids, segr, *pieces, *flat)


def gelu_pair(u):
    z = jnp.abs(u) * (0.5 ** 0.5)
    t = 1.0 / (1.0 + 0.3275911 * z)
    poly = t * (
        0.254829592
        + t * (-0.284496736 + t * (1.421413741 + t * (-1.453152027 + t * 1.061405429)))
    )
    bell = jnp.exp(-0.5 * u * u)
    tail = 0.5 * poly * bell
    cdf = jnp.where(u >= 0, 1.0 - tail, tail)
    return u * cdf, cdf + u * bell * 0.3989422804014327


def norm_rows(values):
    centre = values - jnp.mean(values, axis=1, keepdims=True)
    inverse = lax.rsqrt(jnp.mean(centre * centre, axis=1, keepdims=True) + EPSILON)
    return centre * inverse, inverse


def ffn_near(ids, x, ols, pieces, vecs, out_parts, near_in, near_down, inner, dims, after=()):
    devices, count, rows, quarter, full, width = dims
    here = rows // count
    tokens = here * full
    tile = here * quarter
    head_width = ols[0].shape[2]
    hidden = width
    flat = [ref for p in out_parts for ref, _ in p]
    n = len(flat)

    def body(ids_ref, x_ref, ol_a, ol_b, *refs):
        refs = list(refs)
        places = piece_places([refs.pop(0) for _ in range(count)], tile + 16)
        vec_refs = [refs.pop(0) for _ in range(3)]
        wo_refs = [refs.pop(0) for _ in range(n)]
        wi_refs = [refs.pop(0) for _ in range(2)]
        wd_refs = [refs.pop(0) for _ in range(2)]
        al_out, hat_out, inv_out, acc_out, hl0, hl1, gp0, gp1, wo = refs
        hl_out, gp_out = (hl0, hl1), (gp0, gp1)
        w_out = []
        at = 0
        for kk in range(count):
            m = len(out_parts[kk])
            w_out.append(
                whole_block(
                    wo_refs[at : at + m], bases_of(out_parts[kk]), ids_ref[2], head_width // 2,
                    wo.at[kk], inner // 2,
                )
            )
            at += m
        b_out, gain_a, bias_a = (v[...].reshape(1, width) for v in vec_refs)
        for r in range(here):
            span = slice(r * full, (r + 1) * full)
            total = x_ref[span, :].astype(f32) + b_out
            for kk in range(count):
                ol = (ol_a, ol_b)[kk // 2]
                total = total + mm(ol[kk % 2, span, :], w_out[kk][...])
            hat, inverse = norm_rows(total)
            hat_out[span, :] = hat
            inv_out[span, :] = jnp.broadcast_to(inverse, (full, 128))
            al_out[span, :] = (hat * gain_a + bias_a).astype(bf16)
        half = tokens // 2
        for b in range(2):
            ref, base = places[b]
            bias = bias_rows(ref, base + tile, 3)
            for m in range(2):
                span = slice(m * half, (m + 1) * half)
                u = mm(al_out[span, :], wi_refs[b][...]) + bias
                active, slope = gelu_pair(u)
                active = active.astype(bf16)
                hl_out[b][span, :] = active
                gp_out[b][span, :] = slope.astype(bf16)
                part = mm(active, wd_refs[b][...])
                if b == 0:
                    acc_out[span, :] = part
                else:
                    acc_out[span, :] += part

    wide = (tokens, width)
    return call(
        body,
        [
            shape_of(wide), shape_of(wide, f32), shape_of((tokens, 128), f32), shape_of(wide, f32),
            *[shape_of(wide)] * 4,
        ],
        [VM] * 8,
        [SM, VM, VM, VM] + [VM] * (count + n + 7),
        [
            pltpu.VMEM((count, head_width, width), bf16),
        ],
        us=11,
        name="ffn_near",
        room=26,
        after=after,
    )(ids, x, ols[0], ols[1], *pieces, *vecs, *flat, *near_in, *near_down)


def ffn_far(ids, al, pieces, parts, dims, after=()):
    devices, count, rows, quarter, full, width = dims
    here = rows // count
    tokens = here * full
    tile = here * quarter
    hidden = width
    flat = [ref for p in parts for ref, _ in p]
    n = len(flat)

    def body(ids_ref, al_ref, *refs):
        places = piece_places(refs[:count], tile + 16)
        w_refs = refs[count : count + n]
        hl2, hl3, gp2, gp3, wi = refs[count + n :]
        hl_out, gp_out = (hl2, hl3), (gp2, gp3)
        blocks = []
        at = 0
        for b in range(2):
            m = len(parts[b])
            blocks.append(
                whole_block(w_refs[at : at + m], bases_of(parts[b]), ids_ref[2], width // 2, wi.at[b])
            )
            at += m
        half = tokens // 2
        for b in range(2):
            ref, base = places[2 + b]
            bias = bias_rows(ref, base + tile, 3)
            for m in range(2):
                span = slice(m * half, (m + 1) * half)
                active, slope = gelu_pair(mm(al_ref[span, :], blocks[b][...]) + bias)
                hl_out[b][span, :] = active.astype(bf16)
                gp_out[b][span, :] = slope.astype(bf16)

    wide = (tokens, width)
    return call(
        body,
        [shape_of(wide)] * 4,
        [VM] * 4,
        [SM, VM] + [VM] * (count + n),
        [pltpu.VMEM((2, width, hidden), bf16)],
        us=6,
        name="ffn_far",
        room=14,
        after=after,
    )(ids, al, *pieces, *flat)


def ffn_down(ids, sent, segr, al, acc, hls, vecs, ogs, pool_grad, parts, dims):
    devices, count, rows, quarter, full, width = dims
    here, cap, reach = rows // count, rows // devices, devices // count
    tokens = here * full
    hidden = width
    flat = [ref for p in parts for ref, _ in p]
    n = len(flat)

    def body(ids_ref, sent_ref, segr_ref, al_ref, near_ref, hl1, hl2, hl3, *refs):
        hl_far = (hl2, hl3)
        refs = list(refs)
        vec_refs = [refs.pop(0) for _ in range(3)]
        og_refs = [refs.pop(0) for _ in range(reach)]
        pool_ref = refs.pop(0)
        w_refs = [refs.pop(0) for _ in range(n)]
        tk0, tk1, pooled_out, dz_out, low_out, sums_out, down_out, wd, og_buf, acc_ref, sems = refs
        mi, parity = ids_ref[1], parity_of(ids_ref, 2)
        blocks = []
        at = 0
        for b in range(2):
            m = len(parts[b])
            blocks.append(
                whole_block(w_refs[at : at + m], bases_of(parts[b]), parity, width // 2, wd.at[b])
            )
            at += m
        cots = []
        for k in range(reach):
            for c in range(cap):
                r = k * cap + c
                for kk in range(count):
                    cots.append(
                        pltpu.make_async_copy(
                            og_refs[k].at[c, pl.ds(pl.multiple_of((mi ^ kk) * quarter, quarter), quarter)],
                            og_buf.at[pl.ds(r * full + kk * quarter, quarter)],
                            sems.at[r * count + kk],
                        )
                    )
        for copy in cots:
            copy.start()
        b_down, gain_f, bias_f = (v[...].reshape(1, width) for v in vec_refs)
        half = tokens // 2
        for b in range(2):
            for m in range(2):
                span = slice(m * half, (m + 1) * half)
                part = mm(hl_far[b][span, :], blocks[b][...])
                if b == 0:
                    acc_ref[span, :] = part + near_ref[span, :]
                else:
                    acc_ref[span, :] += part
        for copy in cots:
            copy.wait()
        sums_out[...] = jnp.zeros_like(sums_out)
        for r in range(here):
            span = slice(r * full, (r + 1) * full)
            hat, inverse = norm_rows(al_ref[span, :].astype(f32) + acc_ref[span, :] + b_down)
            final = hat * gain_f + bias_f
            final_low = final.astype(bf16)
            for kk in range(count):
                (tk0, tk1)[r // cap][
                    kk, (r % cap) * quarter : (r % cap + 1) * quarter, :
                ] = final_low[kk * quarter : (kk + 1) * quarter, :]
            line = jnp.broadcast_to(segr_ref[r : r + 1, :].astype(f32), (full, full)).T[:, 0:1]
            cot = og_buf[span, :].astype(f32)
            row = sent_ref[r]
            for g in range(SEGS):
                inside = line == float(g)
                number = jnp.sum(jnp.where(inside, 1.0, 0.0), axis=0, keepdims=True)
                share = 1.0 / number
                pooled_out[r * SEGS + g : r * SEGS + g + 1, :] = (
                    jnp.sum(jnp.where(inside, final, 0.0), axis=0, keepdims=True) * share
                )
                cot = cot + jnp.where(inside, pool_ref[row, g : g + 1, :] * share, 0.0)
            e = cot * gain_f
            mean_e = jnp.mean(e, axis=1, keepdims=True)
            mean_p = jnp.mean(e * hat, axis=1, keepdims=True)
            dz = inverse * (e - mean_e - hat * mean_p)
            dz_out[span, :] = dz
            low_out[span, :] = dz.astype(bf16)
            sums_out[0:1, :] += jnp.sum(dz, axis=0, keepdims=True)
            sums_out[1:2, :] += jnp.sum(cot * hat, axis=0, keepdims=True)
            sums_out[2:3, :] += jnp.sum(cot, axis=0, keepdims=True)
        for b in range(2):
            for c in range(hidden // 256):
                cols = slice(c * 256, (c + 1) * 256)
                left = (hl1, hl3)[b][:, cols]
                down_out[b, cols, :] = mm_tn(left, low_out[...]).astype(bf16)

    wide = (tokens, width)
    return call(
        body,
        [
            shape_of((count, cap * quarter, width)), shape_of((count, cap * quarter, width)),
            shape_of((here * SEGS, width), f32), shape_of(wide, f32), shape_of(wide),
            shape_of((8, width), f32), shape_of((2, hidden, width)),
        ],
        [VM] * 7,
        [SM, SM] + [VM] * 9 + [HB] * reach + [VM] * (1 + n),
        [
            pltpu.VMEM((2, hidden, width), bf16),
            pltpu.VMEM(wide, bf16),
            pltpu.VMEM(wide, f32),
            pltpu.SemaphoreType.DMA((here * count,)),
        ],
        us=9,
        name="ffn_down",
        room=26,
    )(ids, sent, segr, al, acc, *hls, *vecs, *ogs, pool_grad, *flat)


def ffn_back(ids, low, gps, parts, dims):
    devices, count, rows, quarter, full, width = dims
    tokens = low.shape[0]
    hidden = width
    flat = [ref for p in parts for ref, _ in p]
    n = len(flat)

    def body(ids_ref, low_ref, *refs):
        gp_refs, dn_refs = refs[:count], refs[count : count + n]
        du_outs = refs[count + n : 2 * count + n]
        bin_out, wd = refs[2 * count + n :]
        parity = parity_of(ids_ref, 2)
        blocks = []
        at = 0
        for kk in range(count):
            m = len(parts[kk])
            blocks.append(
                whole_block(
                    dn_refs[at : at + m], bases_of(parts[kk]), parity, width // 2, wd.at[kk % 2],
                )
            )
            at += m
        half = tokens // 2
        for kk in (1, 3, 2, 0):
            total = jnp.zeros((1, hidden), f32)
            for m in range(2):
                span = slice(m * half, (m + 1) * half)
                part = (
                    mm_nt(low_ref[span, :], blocks[kk][...]) * gp_refs[kk][span, :].astype(f32)
                ).astype(bf16)
                du_outs[kk][span, :] = part
                total = total + jnp.sum(part.astype(f32), axis=0, keepdims=True)
            bin_out[kk : kk + 1, :] = total

    return call(
        body,
        [shape_of((tokens, hidden))] * count + [shape_of((count, hidden), f32)],
        [VM] * (count + 1),
        [SM, VM] + [VM] * (count + n),
        [pltpu.VMEM((2, hidden, width), bf16)],
        us=5,
        name="ffn_back",
        room=22,
    )(ids, low, *gps, *flat)


def norm_back_attn(ids, dus, al, dz, hat, inv, gain, parts, dims, after=()):
    devices, count, rows, quarter, full, width = dims
    tokens = al.shape[0]
    hidden = width
    flat = [ref for p in parts for ref, _ in p]
    n = len(flat)

    def body(ids_ref, al_ref, dz_ref, hat_ref, inv_ref, vec_ref, *refs):
        du_refs, refs = refs[:count], refs[count:]
        oi_refs = refs[:n]
        dz1_out, low_out, sums_out, in_out, wi, acc = refs[n:]
        blocks = []
        at = 0
        for kk in range(count):
            m = len(parts[kk])
            blocks.append(
                whole_block(
                    oi_refs[at : at + m], bases_of(parts[kk]), ids_ref[2], width // 2, wi.at[kk % 2]
                )
            )
            at += m
        half = tokens // 2
        for kk in range(count):
            for m in range(2):
                span = slice(m * half, (m + 1) * half)
                part = mm_nt(du_refs[kk][span, :], blocks[kk][...])
                if kk == 0:
                    acc[span, :] = part + dz_ref[span, :]
                else:
                    acc[span, :] += part
        gain_a = vec_ref[...].reshape(1, width)
        sums_out[...] = jnp.zeros_like(sums_out)

        @pl.loop(0, tokens // full)
        def _(r):
            span = pl.ds(pl.multiple_of(r * full, full), full)
            da = acc[span, :]
            hat_r = hat_ref[span, :]
            e = da * gain_a
            mean_e = jnp.mean(e, axis=1, keepdims=True)
            mean_p = jnp.mean(e * hat_r, axis=1, keepdims=True)
            dz1 = inv_ref[span, 0:1] * (e - mean_e - hat_r * mean_p)
            dz1_out[span, :] = dz1
            low_out[span, :] = dz1.astype(bf16)
            sums_out[0:1, :] += jnp.sum(dz1, axis=0, keepdims=True)
            sums_out[1:2, :] += jnp.sum(da * hat_r, axis=0, keepdims=True)
            sums_out[2:3, :] += jnp.sum(da, axis=0, keepdims=True)

        for b, kk in enumerate((1, 3)):
            for c in range(width // 256):
                cols = slice(c * 256, (c + 1) * 256)
                in_out[b, cols, :] = mm_tn(al_ref[:, cols], du_refs[kk][...]).astype(bf16)

    wide = (tokens, width)
    return call(
        body,
        [
            shape_of(wide, f32), shape_of(wide), shape_of((8, width), f32),
            shape_of((2, width, hidden)),
        ],
        [VM] * 4,
        [SM] + [VM] * (5 + count + n),
        [
            pltpu.VMEM((2, width, hidden), bf16),
            pltpu.VMEM(wide, f32),
        ],
        us=8,
        name="norm_back",
        room=26,
        after=after,
    )(ids, al, dz, hat, inv, gain, *dus, *flat)


def attend_back(ids, low, x, blocks, extras, dims, after=()):
    devices, count, rows, quarter, full, width = dims
    here = rows // count
    tokens = x.shape[0]
    head_width = blocks[0][2].shape[2]
    inner = 3 * head_width
    flat = [ref for b in blocks for ref, _ in b[5]]
    n = len(flat)
    half_out = head_width // 2
    nb = len(blocks)

    def body(ids_ref, low_ref, x_ref, bin_ref, ffn_ref, norm_ref, *refs):
        data = refs[: 3 * nb]
        w_refs = refs[3 * nb : 3 * nb + n]
        mix_out, grad_out, wo, sums = refs[3 * nb + n :]
        w_out = []
        at = 0
        for b in range(nb):
            m = len(blocks[b][5])
            w_out.append(
                whole_block(
                    w_refs[at : at + m], bases_of(blocks[b][5]), ids_ref[2], half_out, wo.at[b],
                    inner // 2,
                )
            )
            at += m
        masks = head_masks(head_width)
        sums[...] = jnp.zeros_like(sums)
        for b in range(nb):
            kk, place = blocks[b][:2]
            ol_ref, qkv_ref, p_ref = data[3 * b : 3 * b + 3]

            @pl.loop(0, here)
            def _(r):
                span = pl.ds(pl.multiple_of(r * full, full), full)
                dol = mm_nt(low_ref[span, :], w_out[b][...]).astype(bf16)
                query, key, value = (qkv_ref[place, i, span, :] for i in range(3))
                low_p = p_ref[place, r]
                prob = low_p.astype(f32)
                dos = stack_heads(dol, masks)
                dp = mm_nt(dos, value)
                ds = (prob * (dp - jnp.sum(dp * prob, axis=1, keepdims=True))).astype(bf16)
                dv = mm_tn(low_p, dos).astype(bf16)
                dq = (pick_heads(mm(ds, key), masks) * (HD ** -0.5)).astype(bf16)
                dk = (mm_tn(ds, stack_heads(query, masks)) * (HD ** -0.5)).astype(bf16)
                mix_out[b, span, 0:head_width] = dq
                mix_out[b, span, head_width : 2 * head_width] = dk
                mix_out[b, span, 2 * head_width :] = dv
                sums[b : b + 1, 0:head_width] += jnp.sum(dq.astype(f32), axis=0, keepdims=True)
                sums[b : b + 1, 256 : 256 + head_width] += jnp.sum(
                    dv.astype(f32), axis=0, keepdims=True
                )

            for c in range(3):
                part = slice(c * head_width, (c + 1) * head_width)
                grad_out[b, part, :] = mm_tn(mix_out[b, :, part], x_ref[...]).astype(bf16)
            grad_out[b, inner:width, :] = mm_tn(ol_ref[place], low_ref[...]).astype(bf16)
            lines = jnp.concatenate(
                [sums[b : b + 1], bin_ref[kk : kk + 1], norm_ref[0:3], ffn_ref[0:3]], axis=0
            )
            grad_out[b, width : width + 16, :] = two_terms(lines)

    return call(
        body,
        [shape_of((nb, tokens, inner)), shape_of((nb, width + 16, width))],
        [VM] * 2,
        [SM] + [VM] * (5 + 3 * nb + n),
        [
            pltpu.VMEM((nb, head_width, width), bf16),
            pltpu.VMEM((8, width), f32),
        ],
        us=13,
        name="attend_back",
        room=26,
        after=after,
    )(ids, low, x, *extras, *[v for b in blocks for v in b[2:5]], *flat)


def two_terms(lines):
    high = lines.astype(bf16)
    return jnp.concatenate([high, (lines - high.astype(f32)).astype(bf16)], axis=0)


def one_term(lines):
    return lines[0:8].astype(f32) + lines[8:16].astype(f32)


def peer_grad(lhs, rhs, got, after=()):
    tokens, width = rhs.shape
    rows = lhs.shape[1]

    def body(lhs_ref, rhs_ref, got_ref, out):
        for c in range(rows // 256):
            cols = slice(c * 256, (c + 1) * 256)
            out[cols, :] = (
                mm_tn(lhs_ref[:, cols], rhs_ref[...]) + got_ref[1, cols, :].astype(f32)
            ).astype(bf16)

    return call(
        body,
        shape_of((rows, width)),
        VM,
        [VM, VM, VM],
        us=0.2,
        name="peer_grad",
        room=10,
        after=after,
    )(lhs, rhs, got)


def shards(acc, ids_ref, devices, bits, size, send, keep):
    for p in range(devices):
        mirror = sum(((p >> j) & 1) << (bits - 1 - j) for j in range(bits))
        rows = acc[pl.ds(pl.multiple_of((ids_ref[0] ^ mirror) * size, 16), size), :]
        if p < devices // 2:
            keep[p * size : (p + 1) * size, :] = rows
        else:
            q = p - devices // 2
            send[q * size : (q + 1) * size, :] = rows.astype(bf16)


def own_grad(ids, lhs, rhs, got, crossed, devices, after=()):
    tokens, width = rhs.shape
    rows = lhs.shape[1]
    bits = devices.bit_length() - 1
    size = rows // devices

    def body(ids_ref, lhs_ref, rhs_ref, got_ref, cross_ref, send, keep, acc):
        for c in range(rows // 256):
            cols = slice(c * 256, (c + 1) * 256)
            acc[cols, :] = (
                mm_tn(lhs_ref[:, cols], rhs_ref[...])
                + got_ref[0, cols, :].astype(f32)
                + cross_ref[cols, :].astype(f32)
            )
        shards(acc, ids_ref, devices, bits, size, send, keep)

    return call(
        body,
        [shape_of((rows // 2, width)), shape_of((rows // 2, width), f32)],
        [VM, VM],
        [SM, VM, VM, VM, VM],
        [pltpu.VMEM((rows, width), f32)],
        us=0.2,
        name="own_grad",
        room=14,
        after=after,
    )(ids, lhs, rhs, got, crossed)


def peer_last(grads, got, at, after=()):
    _, high, width = grads.shape

    def body(a_ref, g_ref, out):
        out[0 : high - 16, :] = (
            a_ref[at, 0 : high - 16, :].astype(f32) + g_ref[1, 0 : high - 16, :].astype(f32)
        ).astype(bf16)
        out[high - 16 :, :] = two_terms(
            one_term(a_ref[at, high - 16 :, :]) + one_term(g_ref[1, high - 16 :, :])
        )

    return call(
        body, shape_of((high, width)), VM, [VM, VM], us=0.2, name="peer_last",
        room=12,
        after=after,
    )(grads, got)


def own_last(ids, grads, got, crossed, at, devices, after=()):
    _, high, width = grads.shape
    body_rows = high - 16
    bits = devices.bit_length() - 1
    size = body_rows // devices

    def body(ids_ref, a_ref, g_ref, c_ref, send, keep, vec, acc):
        acc[...] = (
            a_ref[at, 0:body_rows, :].astype(f32)
            + g_ref[0, 0:body_rows, :].astype(f32)
            + c_ref[0:body_rows, :].astype(f32)
        )
        shards(acc, ids_ref, devices, bits, size, send, keep)
        lines = (
            one_term(a_ref[at, body_rows:, :])
            + one_term(g_ref[0, body_rows:, :])
            + one_term(c_ref[body_rows:, :])
        )
        send[body_rows // 2 :, :] = two_terms(lines)
        vec[...] = lines

    return call(
        body,
        [
            shape_of((body_rows // 2 + 16, width)),
            shape_of((body_rows // 2, width), f32),
            shape_of((8, width), f32),
        ],
        [VM] * 3,
        [SM, VM, VM, VM],
        [pltpu.VMEM((body_rows, width), f32)],
        us=0.2,
        name="own_last",
        room=16,
        after=after,
    )(ids, grads, got, crossed)


def cut(keep, got, vec, after=()):
    high, width = keep.shape
    last = vec is not None
    tail = 16 if last else 0
    size = high // 4

    def body(*refs):
        keep_ref, got_ref = refs[:2]
        rest = refs[2:]
        if last:
            vec_ref, rest = rest[0], rest[1:]
            lines = vec_ref[...] + one_term(got_ref[high:, :])
            rest[4][...] = lines
        for p in range(4):
            span = slice(p * size, (p + 1) * size)
            total = keep_ref[span, :] + got_ref[span, :].astype(f32)
            if p == 0:
                rest[3][...] = total
            else:
                rest[p - 1][0:size, :] = total.astype(bf16)
                if last:
                    rest[p - 1][size:, :] = two_terms(lines)

    outs = [shape_of((size + tail, width))] * 3 + [shape_of((size, width), f32)]
    args = [keep, got]
    if last:
        outs.append(shape_of((8, width), f32))
        args.append(vec)
    return call(
        body, outs, [VM] * len(outs), [VM] * len(args), us=0.1, name="cut", room=8, after=after
    )(*args)


def gather_sum(keep, gots, vec, after=()):
    high, width = keep.shape
    last = vec is not None
    n = len(gots)

    def body(*refs):
        keep_ref, got_refs, rest = refs[0], refs[1 : 1 + n], refs[1 + n :]
        if last:
            vec_ref, rest = rest[0], rest[1:]
            lines = vec_ref[...]
            for got in got_refs:
                lines = lines + one_term(got[high:, :])
            rest[1][...] = lines
        total = keep_ref[...]
        for got in got_refs:
            total = total + got[0:high, :].astype(f32)
        rest[0][...] = total.astype(bf16)

    outs = [shape_of((high, width))]
    args = [keep, *gots]
    if last:
        outs.append(shape_of((8, width), f32))
        args.append(vec)
    return call(
        body, outs, [VM] * len(outs), [VM] * len(args), us=0.1, name="gather_sum", room=8, after=after
    )(*args)


def join(pieces, after=()):
    size, width = pieces[0].shape
    n = len(pieces)

    def body(*refs):
        for p in range(n):
            refs[n][p * size : (p + 1) * size, :] = refs[p][...]

    return call(
        body, shape_of((n * size, width)), VM, [VM] * n, us=0.1, name="join", room=4, after=after
    )(*pieces)


MASKS = (4, 2, 6)


def place_shards(ids_ref, pieces, devices, size, put):
    bits = devices.bit_length() - 1
    p = 0
    for piece in pieces:
        for q in range(piece.shape[0] // size):
            mirror = sum(((p >> j) & 1) << (bits - 1 - j) for j in range(bits))
            at = pl.multiple_of((ids_ref[0] ^ mirror) * size, 8)
            put(at, piece[q * size : (q + 1) * size, :].astype(f32))
            p += 1


def whole_grad(ids, pieces, devices, cuts, after=()):
    size, width = pieces[0].shape
    n = len(pieces)

    def body(ids_ref, *refs):
        outs = refs[n : n + len(cuts)]
        acc = refs[n + len(cuts)] if len(cuts) > 1 else outs[0]

        def put(at, rows):
            acc[pl.ds(at, size), :] = rows

        place_shards(ids_ref, refs[:n], devices, size, put)
        if len(cuts) > 1:
            base = 0
            for out, rows in zip(outs, cuts):
                out[...] = acc[base : base + rows, :]
                base += rows

    return call(
        body,
        [shape_of((rows, width), f32) for rows in cuts],
        [VM] * len(cuts),
        [SM] + [VM] * n,
        [pltpu.VMEM((size * devices, width), f32)] if len(cuts) > 1 else [],
        us=0.5,
        name="whole_grad",
        room=12,
        after=after,
    )(ids, *pieces)


def grad_input_rows(ids, dz1, mixes, parts, pooled, dims, after=()):
    devices, count, rows, quarter, full, width = dims
    here = rows // count
    tokens = here * full
    tile = here * quarter
    inner = mixes[0].shape[2]
    flat = [ref for p in parts for ref, _ in p]
    n = len(flat)
    turn = (1, 3, 2, 0)

    def body(ids_ref, dz_ref, m_a, m_b, pool_ref, *refs):
        w_refs = refs[:n]
        own, near, far = refs[n : n + 3]
        wq, acc = refs[n + 3 :]
        blocks = []
        at = 0
        for kk in range(count):
            m = len(parts[kk])
            blocks.append(
                whole_block(
                    w_refs[at : at + m], bases_of(parts[kk]), ids_ref[2], inner // 2, wq.at[kk % 2]
                )
            )
            at += m
        half = tokens // 2
        for i, kk in enumerate(turn):
            mix = (m_a, m_b)[i // 2]
            for m in range(2):
                span = slice(m * half, (m + 1) * half)
                part = mm(mix[i % 2, span, :], blocks[kk][...])
                if i == 0:
                    acc[span, :] = part + dz_ref[span, :]
                else:
                    acc[span, :] += part
        size = tile + here * SEGS
        for kk, (ref, base) in enumerate(piece_places((own, near, far, far), size)):
            for r in range(here):
                ref[base + r * quarter : base + (r + 1) * quarter, :] = acc[
                    r * full + kk * quarter : r * full + (kk + 1) * quarter, :
                ].astype(bf16)
            ref[base + tile : base + size, :] = pool_ref[...].astype(bf16)

    return call(
        body,
        [shape_of((m * (tile + here * SEGS), width)) for m in (1, 1, 2)],
        [VM] * 3,
        [SM] + [VM] * (4 + n),
        [
            pltpu.VMEM((2, inner, width), bf16),
            pltpu.VMEM((tokens, width), f32),
        ],
        us=6,
        name="grad_input_rows",
        room=22,
        after=after,
    )(ids, dz1, *mixes, pooled, *flat)


def land_grad(sent, pieces, dims, after=()):
    devices, count, rows, quarter, full, width = dims
    here = rows // count
    tile = here * quarter
    size = tile + here * SEGS

    def body(sent_ref, *refs):
        places = piece_places(refs[:count], size)
        out, pooled, sems = refs[count:]
        copies = []
        for kk, (ref, base) in enumerate(places):
            for j in range(here):
                at = kk * here + j
                copy = pltpu.make_async_copy(
                    ref.at[pl.ds(base + j * quarter, quarter)], out.at[sent_ref[at]], sems.at[at]
                )
                copy.start()
                copies.append(copy)
        for kk, (ref, base) in enumerate(places):
            lines = ref[base + tile : base + size, :].astype(f32)
            for j in range(here):
                pooled[sent_ref[kk * here + j]] = lines[j * SEGS : (j + 1) * SEGS]
        for copy in copies:
            copy.wait()

    return call(
        body,
        [shape_of((rows, quarter, width)), shape_of((rows, SEGS, width), f32)],
        [HB, VM],
        [SM] + [VM] * count,
        [pltpu.SemaphoreType.DMA((rows,))],
        us=0.5,
        name="land_grad",
        room=8,
        after=after,
    )(sent, *pieces)


def turn_output(hops, dims, after=()):
    devices, count, rows, quarter, full, width = dims
    cap, reach = rows // devices, devices // count
    part = cap * quarter
    tile = reach * part

    def body(*refs):
        hop_refs = refs[:reach]
        near, far, sems = refs[reach:]
        copies = []
        for kk, (ref, base) in enumerate(((near, 0), (far, 0), (far, tile))):
            for k in range(reach):
                copies.append(
                    pltpu.make_async_copy(
                        hop_refs[k].at[kk + 1],
                        ref.at[pl.ds(base + k * part, part)],
                        sems.at[kk * reach + k],
                    )
                )
        for copy in copies:
            copy.start()
        for copy in copies:
            copy.wait()

    return call(
        body,
        [shape_of((tile, width)), shape_of((2 * tile, width))],
        [VM, VM],
        [HB] * reach,
        [pltpu.SemaphoreType.DMA((3 * reach,))],
        us=0.1,
        name="turn_output",
        room=8,
        after=after,
    )(*hops)


def land_output(spots, hops, pieces, dims, after=()):
    devices, count, rows, quarter, full, width = dims
    here, cap, reach = rows // count, rows // devices, devices // count
    tile = here * quarter

    def body(spots_ref, *refs):
        hop_refs = refs[:reach]
        places = piece_places((None,) + refs[reach : reach + count - 1], tile)
        out, sems = refs[reach + count - 1 :]
        copies = []
        for kk in range(count):
            for j in range(here):
                at = kk * here + j
                if kk == 0:
                    src = hop_refs[j // cap].at[0, pl.ds((j % cap) * quarter, quarter)]
                else:
                    ref, base = places[kk]
                    src = ref.at[pl.ds(base + j * quarter, quarter)]
                copies.append(pltpu.make_async_copy(src, out.at[spots_ref[at]], sems.at[at]))
        for copy in copies:
            copy.start()
        for copy in copies:
            copy.wait()

    return call(
        body,
        shape_of((rows, quarter, width)),
        HB,
        [SM] + [VM] * (reach + count - 1),
        [pltpu.SemaphoreType.DMA((rows,))],
        us=0.5,
        name="land_output",
        room=8,
        after=after,
    )(spots, *hops, *pieces)


def swap(values, axis, bit):
    return lax.ppermute(values, axis, [(i, i ^ bit) for i in range(lax.axis_size(axis))])


def per_device(
    tokens_in, seg, route, w_qkv, b_qv, w_out, b_out, gain_attn, bias_attn, w_in, b_in, w_down,
    b_down, gain_ffn, bias_ffn, out_grad, pool_grad,
):
    devices, count = lax.axis_size("dp"), lax.axis_size("mp")
    rows, quarter, width = tokens_in.shape
    full = seg.shape[1]
    dims = (devices, count, rows, quarter, full, width)
    reach = devices // count
    head_width = w_qkv.shape[2]
    inner = 3 * head_width

    def hop(values, k):
        return lax.ppermute(
            values,
            ("dp", "mp"),
            [
                (s * count + f, (s ^ (f + count * k)) * count + f)
                for s in range(devices)
                for f in range(count)
            ],
        )

    wq = w_qkv.transpose(1, 2, 0).reshape(inner, width)
    half_rows = (inner + head_width) // 2
    *sends, segr, sent, spots, ids = prep_rows(
        route, seg, tokens_in, b_qv, b_in, (wq, w_out), dims
    )
    near_q, near_o, near_i, near_d = (swap(v, "mp", 1) for v in (wq, w_out, w_in, w_down))
    og_sends = prep_cot(spots, out_grad, dims, (near_q,))
    ogs = [hop(og_sends[k], k) for k in range(reach)]
    pieces = exchange(*sends, before=(near_q, near_o, near_i, near_d, *ogs))

    def later(values, after):
        return lax.optimization_barrier((values, after))[0]

    def crossed(half, bit, first, second):
        direct = later(swap(half, "mp", 2), first)
        relayed = swap(direct, "dp", bit)
        far = (direct, relayed)
        return [
            [(v, 0) for v in far],
            [(swap(direct, "mp", 1), 0), (swap(later(relayed, second), "mp", 1), 0)],
        ]

    below = sends[2].shape[0] - half_rows
    relay_q = swap(pieces[2][below:], "dp", 1)
    half_in = prep_halves((w_in,), 1, (pieces[2],))
    x, ol_a, qkv_a, p_a = attend(
        ids, segr, pieces, [[(wq, 0)], [(near_q, 0)]], (0, 1), inner, dims, True,
        (half_in,),
    )
    relay_q3 = swap(later(relay_q, x), "mp", 1)
    far_q = [(pieces[2], below), (relay_q, 0)]
    far_q3 = [(pieces[3], below), (relay_q3, 0)]
    half_dn = prep_halves((w_down,), 2, (x,))
    ol_b, qkv_b, p_b = attend(
        ids, segr, pieces, [far_q, far_q3], (2, 3), inner, dims, False, (half_dn,)
    )
    q_parts = [[(wq, 0)], [(near_q, 0)], far_q, far_q3]
    wo_parts = [[(w_out, 0)], [(near_o, 0)], far_q, far_q3]
    al, hat, inv, acc, hl0, hl1, gp0, gp1 = ffn_near(
        ids, x, (ol_a, ol_b), pieces, (b_out, gain_attn, bias_attn), wo_parts, (w_in, near_i),
        (w_down, near_d), inner, dims,
    )
    in_parts = [[(w_in, 0)], [(near_i, 0)], *crossed(half_in, 1, x, ol_b)]
    hl2, hl3, gp2, gp3 = ffn_far(ids, al, pieces, in_parts[2:], dims)
    dn_parts = [[(w_down, 0)], [(near_d, 0)], *crossed(half_dn, 2, ol_b, hl2)]
    tk0, tk1, pooled, dz, low, ffn_sums, down_pair = ffn_down(
        ids, sent, segr, al, acc, (hl1, hl2, hl3), (b_down, gain_ffn, bias_ffn), ogs, pool_grad,
        dn_parts[2:], dims,
    )
    got_down = swap(down_pair, "mp", 1)
    *dus, bin_sums = ffn_back(ids, low, (gp0, gp1, gp2, gp3), dn_parts, dims)
    down_far = peer_grad(hl2, low, got_down, (bin_sums,))
    hops = [hop(t, k) for k, t in enumerate(lax.optimization_barrier((tk0, tk1, down_far))[:2])]
    crossed_down = swap(down_far, "mp", 2)
    dz1, low1, norm_sums, in_pair = norm_back_attn(
        ids, dus, al, dz, hat, inv, gain_attn, in_parts, dims, (down_far,)
    )
    got_in = swap(in_pair, "mp", 1)
    extras = (bin_sums, ffn_sums, norm_sums)
    mix_a, grads_a = attend_back(
        ids, low1, x,
        [(1, 1, ol_a, qkv_a, p_a, wo_parts[1]), (3, 1, ol_b, qkv_b, p_b, wo_parts[3])],
        extras, dims,
    )
    got_last = swap(grads_a, "mp", 1)
    in_far = peer_grad(al, dus[2], got_in, (grads_a,))
    crossed_in = swap(in_far, "mp", 2)
    turned = turn_output(hops, dims, (in_far,))
    send_down, keep_down = own_grad(
        ids, hl0, low, got_down, crossed_down, devices, (turned[0],)
    )
    mix_b, grads_b = attend_back(
        ids, low1, x,
        [(2, 0, ol_b, qkv_b, p_b, wo_parts[2]), (0, 0, ol_a, qkv_a, p_a, wo_parts[0])],
        extras, dims, (send_down,),
    )
    last_far = peer_last(grads_b, got_last, 0)
    crossed_last = swap(last_far, "mp", 2)

    def places_of(parts):
        return [swap(part, "dp", mask) for part, mask in zip(parts, MASKS)]

    cut_down = cut(keep_down, swap(send_down, "dp", 1), None, (last_far,))
    down_places = places_of(cut_down[:3])
    gx = grad_input_rows(ids, dz1, (mix_a, mix_b), q_parts, pooled, dims, (cut_down[0],))
    (shard_down,) = gather_sum(cut_down[3], down_places, None, (gx[0],))
    down_spread = [shard_down] + places_of([shard_down] * 3)
    send_in, keep_in = own_grad(
        ids, al, dus[0], got_in, crossed_in, devices, (shard_down,)
    )
    in_half = swap(send_in, "dp", 1)
    cut_in = cut(keep_in, in_half, None, (send_in,))
    in_places = places_of(cut_in[:3])
    half_down = join(down_spread, (cut_in[0],))
    down_spread.append(swap(half_down, "dp", 1))
    (shard_in,) = gather_sum(cut_in[3], in_places, None, (half_down,))
    in_spread = [shard_in] + places_of([shard_in] * 3)
    send, keep, vec = own_last(
        ids, grads_b, got_last, crossed_last, 1, devices, (shard_in,)
    )
    last_half = swap(send, "dp", 1)
    *gx, turned_near, turned_far, _ = lax.optimization_barrier((*gx, *turned, send))
    landed = exchange(None, turned_near, turned_far)[1:]
    gx_landed = exchange(*gx)
    half_in = join(in_spread, (send,))
    in_spread.append(swap(half_in, "dp", 1))
    cut_last = cut(keep, last_half, vec, (half_in,))
    last_places = places_of(cut_last[:3])
    shard_last, vec = gather_sum(cut_last[3], last_places, cut_last[4])
    last_spread = [shard_last] + places_of([shard_last] * 3)
    half_last = join(last_spread, (shard_last,))
    last_spread.append(swap(half_last, "dp", 1))
    (g_down,) = whole_grad(ids, down_spread, devices, (width,), (half_last,))
    (g_in,) = whole_grad(ids, in_spread, devices, (width,), (half_last,))
    tokens_out = land_output(spots, hops, landed, dims, (half_last,))
    grad_input, pooled_out = land_grad(sent, gx_landed, dims, (half_last,))
    g_qkv, g_out = whole_grad(ids, last_spread, devices, (inner, head_width))
    g_qkv = g_qkv.reshape(3, head_width, width).transpose(2, 0, 1)
    g_bqv = jnp.stack([vec[0, :head_width], vec[0, 256 : 256 + head_width]])
    return (
        tokens_out, pooled_out, grad_input, g_qkv, g_bqv, g_out,
        vec[2], vec[3], vec[4], g_in, vec[1], g_down, vec[5], vec[6], vec[7],
    )


def solution(mesh):
    devices, count = mesh.shape["dp"], mesh.shape["mp"]

    def body(*args):
        rows = args[0].shape[0]
        even = rows % devices == 0 and devices % count == 0 and count == 4
        even = even and devices & (devices - 1) == 0 and rows // count == 2 * (rows // devices)
        return (per_device if even else per_device_general)(*args)

    return jax.shard_map(
        body,
        mesh=mesh,
        in_specs=(
            P("dp", "mp", None),
            P(),
            P(),
            P(None, None, "mp"),
            P(None, "mp"),
            P("mp", None),
            P(),
            P(),
            P(),
            P(None, "mp"),
            P("mp"),
            P("mp", None),
            P(),
            P(),
            P(),
            P("dp", None, None),
            P("dp", None, None),
        ),
        out_specs=(
            P("dp", "mp", None),
            P("dp", None, None),
            P("dp", "mp", None),
            P(None, None, "mp"),
            P(None, "mp"),
            P("mp", None),
            P(),
            P(),
            P(),
            P(None, "mp"),
            P("mp"),
            P("mp", None),
            P(),
            P(),
            P(),
        ),
        check_vma=False,
    )
```

```python
import jax
import jax.numpy as jnp
from jax import lax
from jax.experimental import pallas as pl
from jax.experimental.pallas import tpu as pltpu
from jax.sharding import PartitionSpec as P

HD = 64
SEGS = 4


EPSILON = 1e-12
MASKED = -1e30
f32 = jnp.float32
bf16 = jnp.bfloat16


def normalize(values):
    centre = values - jnp.mean(values, axis=-1, keepdims=True)
    scale_inv = lax.rsqrt(jnp.mean(centre * centre, axis=-1, keepdims=True) + EPSILON)
    return (centre * scale_inv, scale_inv[..., 0])


def norm_back(grad_hat, normed_hat, inverse):
    mean_grad = jnp.mean(grad_hat, axis=-1, keepdims=True)
    mean_proj = jnp.mean(grad_hat * normed_hat, axis=-1, keepdims=True)
    return inverse[..., None] * (grad_hat - mean_grad - normed_hat * mean_proj)


def pack_rows(values, position, filled):
    picked = jnp.take(values, position, axis=0)
    shape_mask = filled.reshape((-1,) + (1,) * (values.ndim - 1))
    return jnp.where(shape_mask, picked, jnp.zeros_like(picked))


def per_device_general(
    tokens_in,
    seg,
    route,
    w_qkv,
    b_qv,
    w_out,
    b_out,
    gain_attn,
    bias_attn,
    w_in,
    b_in,
    w_down,
    b_down,
    gain_ffn,
    bias_ffn,
    out_grad,
    pool_grad,
):
    f32 = jnp.float32
    bf16 = jnp.bfloat16
    devices = lax.axis_size("dp")
    row_local = tokens_in.shape[0]
    quarter = tokens_in.shape[1]
    all_rows = route.shape[0]
    capacity = max(1, row_local // devices)
    buffer_len = devices * capacity
    my_index = lax.axis_index("dp")
    target_dev = route // row_local
    dest_grid = target_dev.reshape(devices, row_local)
    before = jnp.arange(row_local)[None, :] < jnp.arange(row_local)[:, None]
    same_dest = dest_grid[:, :, None] == dest_grid[:, None, :]
    earlier_count = (
        jnp.sum(jnp.where(same_dest & before[None], 1, 0), axis=2).reshape(-1).astype(jnp.int32)
    )
    slot_out = target_dev * capacity + earlier_count
    slot_in = jnp.arange(all_rows, dtype=jnp.int32) // row_local * capacity + earlier_count
    own_slots = lax.dynamic_slice_in_dim(slot_out, my_index * row_local, row_local)
    local_rows = jnp.arange(row_local, dtype=jnp.int32)
    send_pos = jnp.zeros(buffer_len, jnp.int32).at[own_slots].set(local_rows)
    send_fill = jnp.zeros(buffer_len, jnp.bool_).at[own_slots].set(True)
    arrive = jnp.where(target_dev == my_index, route - my_index * row_local, row_local)
    recv_pos = jnp.zeros(row_local, jnp.int32).at[arrive].set(slot_in, mode="drop")
    anchor = (
        jnp.zeros(row_local, jnp.int32)
        .at[arrive]
        .set(jnp.arange(all_rows, dtype=jnp.int32), mode="drop")
    )
    back_pos = jnp.zeros(buffer_len, jnp.int32).at[recv_pos].set(local_rows)
    back_fill = jnp.zeros(buffer_len, jnp.bool_).at[recv_pos].set(True)
    arrived = lax.all_to_all(
        pack_rows(tokens_in, send_pos, send_fill), "dp", split_axis=0, concat_axis=0, tiled=True
    )
    rows_x = jnp.take(arrived, recv_pos, axis=0)
    segment = jnp.take(seg, anchor, axis=0)
    full_len = segment.shape[1]
    mp_index = lax.axis_index("mp")

    def own_part(values):
        return lax.dynamic_slice_in_dim(values, mp_index * quarter, quarter, 1)

    gathered = lax.all_gather(rows_x, "mp", axis=1, tiled=True)
    head_width = w_qkv.shape[2]
    local_heads = head_width // HD
    head_shape = (row_local, full_len, local_heads, HD)
    projected = jnp.einsum("rsd,dcf->rscf", gathered, w_qkv, preferred_element_type=f32)
    query_heads = (projected[:, :, 0] + b_qv[0]).astype(bf16).reshape(head_shape)
    key_heads = projected[:, :, 1].astype(bf16).reshape(head_shape)
    value_heads = (projected[:, :, 2] + b_qv[1]).astype(bf16).reshape(head_shape)
    allowed = (segment[:, :, None] == segment[:, None, :])[:, None]
    factor = HD ** (-0.5)

    def scores_of():
        raw_scores = (
            jnp.einsum("rqhe,rkhe->rhqk", query_heads, key_heads, preferred_element_type=f32)
            * factor
        )
        return jnp.where(allowed, raw_scores, MASKED)

    scores = scores_of()
    row_peak = jnp.max(scores, axis=-1, keepdims=True)
    raised = jnp.exp(scores - row_peak)
    weight_total = jnp.sum(raised, axis=-1, keepdims=True)
    log_total = row_peak + jnp.log(weight_total)
    attention = raised / weight_total
    attended = jnp.einsum(
        "rhqk,rkhe->rqhe", attention.astype(bf16), value_heads, preferred_element_type=f32
    )
    attended = attended.astype(bf16).reshape(row_local, full_len, head_width)
    branch = jnp.einsum("rsf,fd->rsd", attended, w_out, preferred_element_type=f32)
    summed_branch = lax.psum_scatter(branch, "mp", scatter_dimension=1, tiled=True)
    hat_attn, inv_attn = normalize(rows_x.astype(f32) + summed_branch + b_out)
    normed_low = (hat_attn * gain_attn + bias_attn).astype(bf16)
    normed_all = lax.all_gather(normed_low, "mp", axis=1, tiled=True)
    hidden = jnp.einsum("rsd,df->rsf", normed_all, w_in, preferred_element_type=f32) + b_in
    active, gelu_back = jax.vjp(lambda values: jax.nn.gelu(values, approximate=False), hidden)
    active_low = active.astype(bf16)
    ffn_part = jnp.einsum("rsf,fd->rsd", active_low, w_down, preferred_element_type=f32)
    ffn_total = lax.psum(ffn_part, "mp")
    hat_ffn, inv_ffn = normalize(normed_all.astype(f32) + ffn_total + b_down)
    block_out = hat_ffn * gain_ffn + bias_ffn
    output_rows = own_part(block_out).astype(bf16)
    member = (segment[:, :, None] == jnp.arange(SEGS)[None, None, :]).astype(f32)
    counts = jnp.sum(member, axis=1)
    pooled_rows = (
        jnp.einsum("rsg,rsd->rgd", member, block_out, precision=lax.Precision.HIGHEST)
        / counts[:, :, None]
    )
    pooled_back = lax.all_to_all(
        pack_rows(pooled_rows, back_pos, back_fill).astype(jnp.bfloat16),
        "dp",
        split_axis=0,
        concat_axis=0,
        tiled=True,
    ).astype(jnp.float32)
    pooled = jnp.take(pooled_back, own_slots, axis=0)
    pool_arrived = lax.all_to_all(
        pack_rows(pool_grad, send_pos, send_fill), "dp", split_axis=0, concat_axis=0, tiled=True
    )
    pool_rows = jnp.take(pool_arrived, recv_pos, axis=0)
    grad_final = out_grad.astype(f32) + jnp.einsum(
        "rsg,rgd->rsd", member, pool_rows / counts[:, :, None], precision=lax.Precision.HIGHEST
    )
    grad_mix = norm_back(grad_final * gain_ffn, hat_ffn, inv_ffn)
    grad_gain_ffn = jnp.sum(grad_final * hat_ffn, axis=(0, 1))
    grad_bias_ffn = jnp.sum(grad_final, axis=(0, 1))
    grad_b_down = jnp.sum(grad_mix, axis=(0, 1))
    mix_low = grad_mix.astype(bf16)
    grad_w_down = jnp.einsum("rsf,rsd->fd", active_low, mix_low, preferred_element_type=f32)
    grad_active = jnp.einsum("rsd,fd->rsf", mix_low, w_down, preferred_element_type=f32)
    grad_hidden = gelu_back(grad_active)[0].astype(bf16)
    grad_w_in = jnp.einsum("rsd,rsf->df", normed_all, grad_hidden, preferred_element_type=f32)
    grad_b_in = jnp.sum(grad_hidden.astype(f32), axis=(0, 1))
    normed_part = jnp.einsum("rsf,df->rsd", grad_hidden, w_in, preferred_element_type=f32)
    grad_normed = lax.psum_scatter(normed_part, "mp", scatter_dimension=1, tiled=True) + own_part(
        grad_mix
    )
    gain_attn_part = jnp.sum(grad_normed * hat_attn, axis=(0, 1))
    bias_attn_part = jnp.sum(grad_normed, axis=(0, 1))
    grad_inner = norm_back(grad_normed * gain_attn, hat_attn, inv_attn)
    stat_terms = jnp.stack([jnp.sum(grad_inner, axis=(0, 1)), gain_attn_part, bias_attn_part])[None]
    inner_all, stats_all = (
        lax.all_gather(grad_inner.astype(jnp.bfloat16), "mp", axis=1, tiled=True).astype(
            grad_inner.dtype
        ),
        lax.all_gather(stat_terms.astype(jnp.bfloat16), "mp", axis=0, tiled=True).astype(
            stat_terms.dtype
        ),
    )
    stat_sums = jnp.sum(stats_all, axis=0)
    inner_low = inner_all.astype(bf16)
    grad_w_out = jnp.einsum("rsf,rsd->fd", attended, inner_low, preferred_element_type=f32)
    grad_attended = (
        jnp.einsum("rsd,fd->rsf", inner_low, w_out, preferred_element_type=f32)
        .astype(bf16)
        .reshape(head_shape)
    )
    again = jnp.exp(scores_of() - log_total)
    grad_prob = jnp.einsum(
        "rqhe,rkhe->rhqk", grad_attended, value_heads, preferred_element_type=f32
    )
    grad_values = jnp.einsum(
        "rhqk,rqhe->rkhe", again.astype(bf16), grad_attended, preferred_element_type=f32
    )
    grad_scores = (again * (grad_prob - jnp.sum(grad_prob * again, axis=-1, keepdims=True))).astype(
        bf16
    )
    grad_query = (
        jnp.einsum("rhqk,rkhe->rqhe", grad_scores, key_heads, preferred_element_type=f32) * factor
    ).astype(bf16)
    grad_keys = (
        jnp.einsum("rhqk,rqhe->rkhe", grad_scores, query_heads, preferred_element_type=f32) * factor
    ).astype(bf16)
    flat_shape = (row_local, full_len, head_width)
    grad_mixed = jnp.stack(
        [
            grad_query.reshape(flat_shape),
            grad_keys.reshape(flat_shape),
            grad_values.astype(bf16).reshape(flat_shape),
        ],
        axis=2,
    )
    grad_w_qkv = jnp.einsum("rsd,rscf->dcf", gathered, grad_mixed, preferred_element_type=f32)
    grad_b_qv = jnp.stack(
        [
            jnp.sum(grad_mixed[:, :, 0].astype(f32), axis=(0, 1)),
            jnp.sum(grad_mixed[:, :, 2].astype(f32), axis=(0, 1)),
        ]
    )
    input_part = jnp.einsum("rscf,dcf->rsd", grad_mixed, w_qkv, preferred_element_type=f32)
    grad_rows = (
        lax.psum_scatter(input_part, "mp", scatter_dimension=1, tiled=True) + grad_inner
    ).astype(bf16)
    grad_home = lax.all_to_all(
        pack_rows(grad_rows, back_pos, back_fill), "dp", split_axis=0, concat_axis=0, tiled=True
    )
    grad_input = jnp.take(grad_home, own_slots, axis=0)
    vector_grads = jnp.stack(
        [stat_sums[0], stat_sums[1], stat_sums[2], grad_b_down, grad_gain_ffn, grad_bias_ffn]
    )
    totals = lax.psum(
        (grad_w_qkv, grad_b_qv, grad_w_out, grad_w_in, grad_b_in, grad_w_down, vector_grads), "dp"
    )
    return (
        output_rows,
        pooled,
        grad_input,
        totals[0],
        totals[1],
        totals[2],
        totals[6][0],
        totals[6][1],
        totals[6][2],
        totals[3],
        totals[4],
        totals[5],
        totals[6][3],
        totals[6][4],
        totals[6][5],
    )


VM = pl.BlockSpec(memory_space=pltpu.VMEM)
SM = pl.BlockSpec(memory_space=pltpu.SMEM)
HB = pl.BlockSpec(memory_space=pl.ANY)
HM = pl.BlockSpec(memory_space=pltpu.HBM)
MIB = 1024 * 1024
PACE = 2e9


def shape_of(shape, dtype=bf16):
    return jax.ShapeDtypeStruct(shape, dtype)


def call(
    body, outs, out_specs, in_specs, scratch=(), us=2, room=16, name=None, after=()
):
    made = pl.pallas_call(
        body,
        out_shape=outs,
        in_specs=in_specs,
        out_specs=out_specs,
        scratch_shapes=list(scratch),
        compiler_params=pltpu.CompilerParams(vmem_limit_bytes=room * MIB),
        cost_estimate=pl.CostEstimate(flops=int(us * PACE), bytes_accessed=0, transcendentals=0),
        name=name,
    )

    def run(*args):
        if after:
            args = list(args)
            at = min(range(len(args)), key=lambda n: args[n].size)
            args[at] = lax.optimization_barrier((args[at], *after))[0]
        return made(*args)

    return run


def mm(a, b):
    return lax.dot_general(a, b, (((1,), (0,)), ((), ())), preferred_element_type=f32)


def mm_nt(a, b):
    return lax.dot_general(a, b, (((1,), (1,)), ((), ())), preferred_element_type=f32)


def mm_tn(a, b):
    return lax.dot_general(a, b, (((0,), (0,)), ((), ())), preferred_element_type=f32)


def split3(values):
    high = values.astype(bf16)
    rest = values - high.astype(f32)
    middle = rest.astype(bf16)
    low = (rest - middle.astype(f32)).astype(bf16)
    return high, middle, low


def piece_places(refs, size):
    return [(refs[0], 0), (refs[1], 0), (refs[2], 0), (refs[3], size)]


def exchange(own, near, far, before=()):
    near = swap(near, "mp", 1)
    crossed = swap(far, "mp", 2)
    if before:
        crossed = lax.optimization_barrier((crossed, near, *before))[0]
    return [own, near, crossed, swap(crossed, "mp", 1)]


def prep_rows(route, seg, tokens, b_qv, b_in, weights, dims):
    devices, count, rows, quarter, full, width = dims
    here, cap = rows // count, rows // devices
    head_width = b_qv.shape[1]
    tile = here * quarter
    total = devices * rows
    halves = [w.shape[0] // 2 for w in weights]

    def body(
        route_ref, seg_ref, tok, bqv_ref, bin_ref, wq, wo, x0, x1, far, segr, sent_ref, spots_ref,
        ids_ref, lists, sems,
    ):
        my, mi = lax.axis_index("dp"), lax.axis_index("mp")
        crossing = []
        base = 2 * (tile + 16)
        for n, (src, half) in enumerate(zip((wq, wo), halves)):
            crossing.append(
                pltpu.make_async_copy(
                    src.at[pl.ds(pl.multiple_of(lax.rem(my, 2) * half, 16), half)],
                    far.at[pl.ds(base, half)],
                    sems.at[rows + 2 + n],
                )
            )
            crossing[n].start()
            base += half
        ids_ref[0] = my
        ids_ref[1] = mi
        ids_ref[2] = lax.rem(my, 2)
        places = piece_places((x0, x1, far, far), tile + 16)
        across = jnp.broadcast_to(route_ref[...].reshape(1, total), (total, total)).astype(f32)
        down = across.T.astype(jnp.int32)
        across = across.astype(jnp.int32)
        r = lax.broadcasted_iota(jnp.int32, (total, total), 0)
        c = lax.broadcasted_iota(jnp.int32, (total, total), 1)
        key_down = lax.div(down, rows) * total + r
        key_across = lax.div(across, rows) * total + c
        before = (lax.div(r, rows) == lax.div(c, rows)) & (key_across < key_down)
        rank = jnp.sum(jnp.where(before, 1.0, 0.0), axis=1, keepdims=True).astype(jnp.int32)
        at = lax.rem(c, rows)
        partner = my ^ ((mi ^ lax.div(at, here)) + count * lax.rem(lax.div(at, cap), here // cap))
        copy_at = lax.rem(at, cap)
        source = lax.div(r, rows)
        going = (source == my) & (rank == partner * cap + copy_at)
        coming = (source == partner) & (rank == my * cap + copy_at)
        lists[0:1, :] = jnp.sum(
            jnp.where(going, lax.rem(r, rows), 0).astype(f32), axis=0, keepdims=True
        ).astype(jnp.int32)
        lists[1:2, :] = jnp.sum(
            jnp.where(coming, down - my * rows, 0).astype(f32), axis=0, keepdims=True
        ).astype(jnp.int32)
        moves = [
            pltpu.make_async_copy(lists.at[0], sent_ref, sems.at[rows]),
            pltpu.make_async_copy(lists.at[1], spots_ref, sems.at[rows + 1]),
        ]
        for move in moves:
            move.start()
        zero = jnp.zeros((16, width), bf16)
        tail = x0.at[pl.ds(tile, 16)]
        tail[...] = zero
        for n, term in enumerate(split3(bqv_ref[...])):
            tail[n : n + 1, 0:head_width] = term[0:1]
            tail[n : n + 1, 256 : 256 + head_width] = term[1:2]
        for n, term in enumerate(split3(bin_ref[...].reshape(1, width))):
            tail[3 + n : 4 + n, :] = term
        for ref, base in places[1:]:
            ref[base + tile : base + tile + 16, :] = tail[...]
        for move in moves:
            move.wait()
        copies = []
        for kk in reversed(range(count)):
            for n in range(here):
                k = kk * here + n
                copies.append(
                    pltpu.make_async_copy(
                        tok.at[sent_ref[k]],
                        places[kk][0].at[pl.ds(places[kk][1] + n * quarter, quarter)],
                        sems.at[k],
                    )
                )
        for copy in copies:
            copy.start()
        for n in range(here):
            segr[n : n + 1, :] = seg_ref[pl.ds(my * rows + sent_ref[n], 1), :]
        segr[here:8, :] = jnp.zeros((8 - here, full), jnp.int32)
        lane = lax.broadcasted_iota(jnp.int32, (8, full), 1)
        lines = segr[...]
        bit = 1
        while bit < count:
            step = bit * quarter
            swapped = jnp.where(
                lax.rem(lax.div(lane, step), 2) == 0,
                pltpu.roll(lines, full - step, 1),
                pltpu.roll(lines, step, 1),
            )
            lines = jnp.where(lax.rem(lax.div(mi, bit), 2) == 1, swapped, lines)
            bit *= 2
        segr[...] = lines
        for copy in copies + crossing:
            copy.wait()

    return call(
        body,
        [
            shape_of((tile + 16, width)),
            shape_of((tile + 16, width)),
            shape_of((2 * (tile + 16) + sum(halves), width)),
        ]
        + [
            shape_of((8, full), jnp.int32),
            shape_of((total,), jnp.int32),
            shape_of((total,), jnp.int32),
            shape_of((3,), jnp.int32),
        ],
        [VM] * 4 + [SM] * 3,
        [VM, VM, HM, VM, VM, HM, HM],
        [pltpu.VMEM((8, total), jnp.int32), pltpu.SemaphoreType.DMA((rows + 4,))],
        us=2,
        name="prep_rows",
        room=60,
    )(route, seg, tokens, b_qv, b_in, *weights)


def prep_halves(weights, bit, after=()):
    width = weights[0].shape[1]
    halves = [w.shape[0] // 2 for w in weights]
    n = len(weights)

    def body(*refs):
        out, sems = refs[n:]
        parity = lax.rem(lax.div(lax.axis_index("dp"), bit), 2)
        copies = []
        base = 0
        for at, half in enumerate(halves):
            copies.append(
                pltpu.make_async_copy(
                    refs[at].at[pl.ds(pl.multiple_of(parity * half, 16), half)],
                    out.at[pl.ds(base, half)],
                    sems.at[at],
                )
            )
            base += half
        for copy in copies:
            copy.start()
        for copy in copies:
            copy.wait()

    return call(
        body,
        shape_of((sum(halves), width)),
        VM,
        [HM] * n,
        [pltpu.SemaphoreType.DMA((n,))],
        us=0.1,
        name="prep_halves",
        room=4,
        after=after,
    )(*weights)


def prep_cot(asked, out_grad, dims, after):
    devices, count, rows, quarter, full, width = dims
    cap, reach = rows // devices, devices // count

    def body(asked_ref, og, *refs):
        outs, sems = refs[:reach], refs[reach]
        copies = []
        for k in range(reach):
            for c in range(cap):
                at = k * cap + c
                copies.append(
                    pltpu.make_async_copy(og.at[asked_ref[at]], outs[k].at[c], sems.at[at])
                )
        for copy in copies:
            copy.start()
        for copy in copies:
            copy.wait()

    return call(
        body,
        [shape_of((cap, full, width))] * reach,
        [VM] * reach,
        [SM, HM],
        [pltpu.SemaphoreType.DMA((reach * cap,))],
        us=0.1,
        name="prep_cot",
        room=6,
        after=after,
    )(asked, out_grad)


def bias_rows(piece, at, count):
    terms = piece[at : at + 16, :].astype(f32)
    first = 0 if count == 0 else 3
    return terms[first : first + 1] + terms[first + 1 : first + 2] + terms[first + 2 : first + 3]


def head_masks(head_width):
    lane = lax.broadcasted_iota(jnp.int32, (1, head_width), 1)
    return [(lane >= h * HD) & (lane < (h + 1) * HD) for h in range(head_width // HD)]


def stack_heads(values, masks):
    zero = jnp.zeros_like(values)
    return jnp.concatenate([jnp.where(mask, values, zero) for mask in masks], axis=0)


def pick_heads(stacked, masks):
    size = stacked.shape[0] // len(masks)
    out = stacked[:size]
    for h in range(1, len(masks)):
        out = jnp.where(masks[h], stacked[h * size : (h + 1) * size], out)
    return out


def parity_of(ids_ref, bit):
    return lax.rem(lax.div(ids_ref[0], bit), 2)


def whole_block(refs, bases, parity, half, dst, row=0):
    if len(refs) == 1:
        return refs[0]
    for ref, base, place in zip(refs, bases, (parity, 1 - parity)):
        dst[pl.ds(pl.multiple_of(place * half, 16), half), :] = ref[
            base + row : base + row + half, :
        ]
    return dst


def bases_of(part):
    return [base for _, base in part]


def attend(ids, segr, pieces, parts, pair, inner, dims, keep_x, after=()):
    devices, count, rows, quarter, full, width = dims
    here = rows // count
    tokens = here * full
    tile = here * quarter
    head_width = inner // 3
    n_heads = head_width // HD
    n_parts = [len(p) for p in parts]
    flat = [ref for p in parts for ref, _ in p]

    def body(ids_ref, segr_ref, *refs):
        places = piece_places(refs[:count], tile + 16)
        w_refs = refs[count : count + len(flat)]
        out = list(refs[count + len(flat) :])
        if keep_x:
            x_out = out.pop(0)
        ol_out, qkv_out, p_out, x_ref, w_ref = out
        blocks = []
        at = 0
        for b, n in enumerate(n_parts):
            blocks.append(
                whole_block(w_refs[at : at + n], bases_of(parts[b]), ids_ref[2], inner // 2, w_ref.at[b])
            )
            at += n
        for r in range(here):
            for kk in range(count):
                ref, base = places[kk]
                x_ref[r * full + kk * quarter : r * full + (kk + 1) * quarter, :] = ref[
                    base + r * quarter : base + (r + 1) * quarter, :
                ]
        if keep_x:
            x_out[...] = x_ref[...]
        masks = head_masks(head_width)
        for b in range(2):
            ref, base = places[pair[b]]
            bias = bias_rows(ref, base + tile, 0)
            bias_q, bias_v = bias[:, 0:head_width], bias[:, 256 : 256 + head_width]

            @pl.loop(0, here, unroll=True)
            def _(r):
                start = pl.multiple_of(r * full, full)
                projected = mm_nt(x_ref[pl.ds(start, full), :], blocks[b][...])
                query = (projected[:, 0:head_width] + bias_q).astype(bf16)
                key = projected[:, head_width : 2 * head_width].astype(bf16)
                value = (projected[:, 2 * head_width :] + bias_v).astype(bf16)
                line = segr_ref[pl.ds(r, 1), :].astype(f32)
                wide = jnp.broadcast_to(line, (full, full))
                allowed = wide == wide.T
                stacked = stack_heads(query, masks)
                raw = mm_nt(stacked, key) * (HD ** -0.5)
                allowed3 = jnp.concatenate([allowed] * n_heads, axis=0)
                scores = jnp.where(allowed3, raw, MASKED)
                raised = jnp.exp(scores - jnp.max(scores, axis=1, keepdims=True))
                prob = raised / jnp.sum(raised, axis=1, keepdims=True)
                low = prob.astype(bf16)
                attended = pick_heads(mm(low, value), masks).astype(bf16)
                ol_out[b, pl.ds(start, full), :] = attended
                qkv_out[b, 0, pl.ds(start, full), :] = query
                qkv_out[b, 1, pl.ds(start, full), :] = key
                qkv_out[b, 2, pl.ds(start, full), :] = value
                p_out[b, r] = low

    outs = [
        shape_of((2, tokens, head_width)),
        shape_of((2, 3, tokens, head_width)),
        shape_of((2, here, n_heads * full, full)),
    ]
    if keep_x:
        outs = [shape_of((tokens, width))] + outs
    return call(
        body,
        outs,
        [VM] * len(outs),
        [SM, VM] + [VM] * (count + len(flat)),
        [
            pltpu.VMEM((tokens, width), bf16),
            pltpu.VMEM((2, inner, width), bf16),
        ],
        us=10,
        name="attend",
        room=18,
        after=after,
    )(ids, segr, *pieces, *flat)


def gelu_pair(u):
    z = jnp.abs(u) * (0.5 ** 0.5)
    t = 1.0 / (1.0 + 0.3275911 * z)
    poly = t * (
        0.254829592
        + t * (-0.284496736 + t * (1.421413741 + t * (-1.453152027 + t * 1.061405429)))
    )
    bell = jnp.exp(-0.5 * u * u)
    tail = 0.5 * poly * bell
    cdf = jnp.where(u >= 0, 1.0 - tail, tail)
    return u * cdf, cdf + u * bell * 0.3989422804014327


def norm_rows(values):
    centre = values - jnp.mean(values, axis=1, keepdims=True)
    inverse = lax.rsqrt(jnp.mean(centre * centre, axis=1, keepdims=True) + EPSILON)
    return centre * inverse, inverse


def ffn_near(ids, x, ols, pieces, vecs, out_parts, near_in, near_down, inner, dims, after=()):
    devices, count, rows, quarter, full, width = dims
    here = rows // count
    tokens = here * full
    tile = here * quarter
    head_width = ols[0].shape[2]
    hidden = width
    flat = [ref for p in out_parts for ref, _ in p]
    n = len(flat)

    def body(ids_ref, x_ref, ol_a, ol_b, *refs):
        refs = list(refs)
        places = piece_places([refs.pop(0) for _ in range(count)], tile + 16)
        vec_refs = [refs.pop(0) for _ in range(3)]
        wo_refs = [refs.pop(0) for _ in range(n)]
        wi_refs = [refs.pop(0) for _ in range(2)]
        wd_refs = [refs.pop(0) for _ in range(2)]
        al_out, hat_out, inv_out, acc_out, hl0, hl1, gp0, gp1, wo = refs
        hl_out, gp_out = (hl0, hl1), (gp0, gp1)
        w_out = []
        at = 0
        for kk in range(count):
            m = len(out_parts[kk])
            w_out.append(
                whole_block(
                    wo_refs[at : at + m], bases_of(out_parts[kk]), ids_ref[2], head_width // 2,
                    wo.at[kk], inner // 2,
                )
            )
            at += m
        b_out, gain_a, bias_a = (v[...].reshape(1, width) for v in vec_refs)
        for r in range(here):
            span = slice(r * full, (r + 1) * full)
            total = x_ref[span, :].astype(f32) + b_out
            for kk in range(count):
                ol = (ol_a, ol_b)[kk // 2]
                total = total + mm(ol[kk % 2, span, :], w_out[kk][...])
            hat, inverse = norm_rows(total)
            hat_out[span, :] = hat
            inv_out[span, :] = jnp.broadcast_to(inverse, (full, 128))
            al_out[span, :] = (hat * gain_a + bias_a).astype(bf16)
        half = tokens // 2
        for b in range(2):
            ref, base = places[b]
            bias = bias_rows(ref, base + tile, 3)
            for m in range(2):
                span = slice(m * half, (m + 1) * half)
                u = mm(al_out[span, :], wi_refs[b][...]) + bias
                active, slope = gelu_pair(u)
                active = active.astype(bf16)
                hl_out[b][span, :] = active
                gp_out[b][span, :] = slope.astype(bf16)
                part = mm(active, wd_refs[b][...])
                if b == 0:
                    acc_out[span, :] = part
                else:
                    acc_out[span, :] += part

    wide = (tokens, width)
    return call(
        body,
        [
            shape_of(wide), shape_of(wide, f32), shape_of((tokens, 128), f32), shape_of(wide, f32),
            *[shape_of(wide)] * 4,
        ],
        [VM] * 8,
        [SM, VM, VM, VM] + [VM] * (count + n + 7),
        [
            pltpu.VMEM((count, head_width, width), bf16),
        ],
        us=11,
        name="ffn_near",
        room=26,
        after=after,
    )(ids, x, ols[0], ols[1], *pieces, *vecs, *flat, *near_in, *near_down)


def ffn_far(ids, al, pieces, parts, dims, after=()):
    devices, count, rows, quarter, full, width = dims
    here = rows // count
    tokens = here * full
    tile = here * quarter
    hidden = width
    flat = [ref for p in parts for ref, _ in p]
    n = len(flat)

    def body(ids_ref, al_ref, *refs):
        places = piece_places(refs[:count], tile + 16)
        w_refs = refs[count : count + n]
        hl2, hl3, gp2, gp3, wi = refs[count + n :]
        hl_out, gp_out = (hl2, hl3), (gp2, gp3)
        blocks = []
        at = 0
        for b in range(2):
            m = len(parts[b])
            blocks.append(
                whole_block(w_refs[at : at + m], bases_of(parts[b]), ids_ref[2], width // 2, wi.at[b])
            )
            at += m
        half = tokens // 2
        for b in range(2):
            ref, base = places[2 + b]
            bias = bias_rows(ref, base + tile, 3)
            for m in range(2):
                span = slice(m * half, (m + 1) * half)
                active, slope = gelu_pair(mm(al_ref[span, :], blocks[b][...]) + bias)
                hl_out[b][span, :] = active.astype(bf16)
                gp_out[b][span, :] = slope.astype(bf16)

    wide = (tokens, width)
    return call(
        body,
        [shape_of(wide)] * 4,
        [VM] * 4,
        [SM, VM] + [VM] * (count + n),
        [pltpu.VMEM((2, width, hidden), bf16)],
        us=6,
        name="ffn_far",
        room=14,
        after=after,
    )(ids, al, *pieces, *flat)


def ffn_down(ids, sent, segr, al, acc, hls, vecs, ogs, pool_grad, parts, dims):
    devices, count, rows, quarter, full, width = dims
    here, cap, reach = rows // count, rows // devices, devices // count
    tokens = here * full
    hidden = width
    flat = [ref for p in parts for ref, _ in p]
    n = len(flat)

    def body(ids_ref, sent_ref, segr_ref, al_ref, near_ref, hl1, hl2, hl3, *refs):
        hl_far = (hl2, hl3)
        refs = list(refs)
        vec_refs = [refs.pop(0) for _ in range(3)]
        og_refs = [refs.pop(0) for _ in range(reach)]
        pool_ref = refs.pop(0)
        w_refs = [refs.pop(0) for _ in range(n)]
        tk0, tk1, pooled_out, dz_out, low_out, sums_out, down_out, wd, og_buf, acc_ref, sems = refs
        mi, parity = ids_ref[1], parity_of(ids_ref, 2)
        blocks = []
        at = 0
        for b in range(2):
            m = len(parts[b])
            blocks.append(
                whole_block(w_refs[at : at + m], bases_of(parts[b]), parity, width // 2, wd.at[b])
            )
            at += m
        cots = []
        for k in range(reach):
            for c in range(cap):
                r = k * cap + c
                for kk in range(count):
                    cots.append(
                        pltpu.make_async_copy(
                            og_refs[k].at[c, pl.ds(pl.multiple_of((mi ^ kk) * quarter, quarter), quarter)],
                            og_buf.at[pl.ds(r * full + kk * quarter, quarter)],
                            sems.at[r * count + kk],
                        )
                    )
        for copy in cots:
            copy.start()
        b_down, gain_f, bias_f = (v[...].reshape(1, width) for v in vec_refs)
        half = tokens // 2
        for b in range(2):
            for m in range(2):
                span = slice(m * half, (m + 1) * half)
                part = mm(hl_far[b][span, :], blocks[b][...])
                if b == 0:
                    acc_ref[span, :] = part + near_ref[span, :]
                else:
                    acc_ref[span, :] += part
        for copy in cots:
            copy.wait()
        sums_out[...] = jnp.zeros_like(sums_out)
        for r in range(here):
            span = slice(r * full, (r + 1) * full)
            hat, inverse = norm_rows(al_ref[span, :].astype(f32) + acc_ref[span, :] + b_down)
            final = hat * gain_f + bias_f
            final_low = final.astype(bf16)
            for kk in range(count):
                (tk0, tk1)[r // cap][
                    kk, (r % cap) * quarter : (r % cap + 1) * quarter, :
                ] = final_low[kk * quarter : (kk + 1) * quarter, :]
            line = jnp.broadcast_to(segr_ref[r : r + 1, :].astype(f32), (full, full)).T[:, 0:1]
            cot = og_buf[span, :].astype(f32)
            row = sent_ref[r]
            for g in range(SEGS):
                inside = line == float(g)
                number = jnp.sum(jnp.where(inside, 1.0, 0.0), axis=0, keepdims=True)
                share = 1.0 / number
                pooled_out[r * SEGS + g : r * SEGS + g + 1, :] = (
                    jnp.sum(jnp.where(inside, final, 0.0), axis=0, keepdims=True) * share
                )
                cot = cot + jnp.where(inside, pool_ref[row, g : g + 1, :] * share, 0.0)
            e = cot * gain_f
            mean_e = jnp.mean(e, axis=1, keepdims=True)
            mean_p = jnp.mean(e * hat, axis=1, keepdims=True)
            dz = inverse * (e - mean_e - hat * mean_p)
            dz_out[span, :] = dz
            low_out[span, :] = dz.astype(bf16)
            sums_out[0:1, :] += jnp.sum(dz, axis=0, keepdims=True)
            sums_out[1:2, :] += jnp.sum(cot * hat, axis=0, keepdims=True)
            sums_out[2:3, :] += jnp.sum(cot, axis=0, keepdims=True)
        for b in range(2):
            for c in range(hidden // 256):
                cols = slice(c * 256, (c + 1) * 256)
                left = (hl1, hl3)[b][:, cols]
                down_out[b, cols, :] = mm_tn(left, low_out[...]).astype(bf16)

    wide = (tokens, width)
    return call(
        body,
        [
            shape_of((count, cap * quarter, width)), shape_of((count, cap * quarter, width)),
            shape_of((here * SEGS, width), f32), shape_of(wide, f32), shape_of(wide),
            shape_of((8, width), f32), shape_of((2, hidden, width)),
        ],
        [VM] * 7,
        [SM, SM] + [VM] * 9 + [HB] * reach + [VM] * (1 + n),
        [
            pltpu.VMEM((2, hidden, width), bf16),
            pltpu.VMEM(wide, bf16),
            pltpu.VMEM(wide, f32),
            pltpu.SemaphoreType.DMA((here * count,)),
        ],
        us=9,
        name="ffn_down",
        room=26,
    )(ids, sent, segr, al, acc, *hls, *vecs, *ogs, pool_grad, *flat)


def ffn_back(ids, low, gps, parts, dims):
    devices, count, rows, quarter, full, width = dims
    tokens = low.shape[0]
    hidden = width
    flat = [ref for p in parts for ref, _ in p]
    n = len(flat)

    def body(ids_ref, low_ref, *refs):
        gp_refs, dn_refs = refs[:count], refs[count : count + n]
        du_outs = refs[count + n : 2 * count + n]
        bin_out, wd = refs[2 * count + n :]
        parity = parity_of(ids_ref, 2)
        blocks = []
        at = 0
        for kk in range(count):
            m = len(parts[kk])
            blocks.append(
                whole_block(
                    dn_refs[at : at + m], bases_of(parts[kk]), parity, width // 2, wd.at[kk % 2],
                )
            )
            at += m
        half = tokens // 2
        for kk in (1, 3, 2, 0):
            total = jnp.zeros((1, hidden), f32)
            for m in range(2):
                span = slice(m * half, (m + 1) * half)
                part = (
                    mm_nt(low_ref[span, :], blocks[kk][...]) * gp_refs[kk][span, :].astype(f32)
                ).astype(bf16)
                du_outs[kk][span, :] = part
                total = total + jnp.sum(part.astype(f32), axis=0, keepdims=True)
            bin_out[kk : kk + 1, :] = total

    return call(
        body,
        [shape_of((tokens, hidden))] * count + [shape_of((count, hidden), f32)],
        [VM] * (count + 1),
        [SM, VM] + [VM] * (count + n),
        [pltpu.VMEM((2, hidden, width), bf16)],
        us=5,
        name="ffn_back",
        room=22,
    )(ids, low, *gps, *flat)


def norm_back_attn(ids, dus, al, dz, hat, inv, gain, parts, dims, after=()):
    devices, count, rows, quarter, full, width = dims
    tokens = al.shape[0]
    hidden = width
    flat = [ref for p in parts for ref, _ in p]
    n = len(flat)

    def body(ids_ref, al_ref, dz_ref, hat_ref, inv_ref, vec_ref, *refs):
        du_refs, refs = refs[:count], refs[count:]
        oi_refs = refs[:n]
        dz1_out, low_out, sums_out, in_out, wi, acc = refs[n:]
        blocks = []
        at = 0
        for kk in range(count):
            m = len(parts[kk])
            blocks.append(
                whole_block(
                    oi_refs[at : at + m], bases_of(parts[kk]), ids_ref[2], width // 2, wi.at[kk % 2]
                )
            )
            at += m
        half = tokens // 2
        for kk in range(count):
            for m in range(2):
                span = slice(m * half, (m + 1) * half)
                part = mm_nt(du_refs[kk][span, :], blocks[kk][...])
                if kk == 0:
                    acc[span, :] = part + dz_ref[span, :]
                else:
                    acc[span, :] += part
        gain_a = vec_ref[...].reshape(1, width)
        sums_out[...] = jnp.zeros_like(sums_out)

        @pl.loop(0, tokens // full)
        def _(r):
            span = pl.ds(pl.multiple_of(r * full, full), full)
            da = acc[span, :]
            hat_r = hat_ref[span, :]
            e = da * gain_a
            mean_e = jnp.mean(e, axis=1, keepdims=True)
            mean_p = jnp.mean(e * hat_r, axis=1, keepdims=True)
            dz1 = inv_ref[span, 0:1] * (e - mean_e - hat_r * mean_p)
            dz1_out[span, :] = dz1
            low_out[span, :] = dz1.astype(bf16)
            sums_out[0:1, :] += jnp.sum(dz1, axis=0, keepdims=True)
            sums_out[1:2, :] += jnp.sum(da * hat_r, axis=0, keepdims=True)
            sums_out[2:3, :] += jnp.sum(da, axis=0, keepdims=True)

        for b, kk in enumerate((1, 3)):
            for c in range(width // 256):
                cols = slice(c * 256, (c + 1) * 256)
                in_out[b, cols, :] = mm_tn(al_ref[:, cols], du_refs[kk][...]).astype(bf16)

    wide = (tokens, width)
    return call(
        body,
        [
            shape_of(wide, f32), shape_of(wide), shape_of((8, width), f32),
            shape_of((2, width, hidden)),
        ],
        [VM] * 4,
        [SM] + [VM] * (5 + count + n),
        [
            pltpu.VMEM((2, width, hidden), bf16),
            pltpu.VMEM(wide, f32),
        ],
        us=8,
        name="norm_back",
        room=26,
        after=after,
    )(ids, al, dz, hat, inv, gain, *dus, *flat)


def attend_back(ids, low, x, blocks, extras, dims, after=()):
    devices, count, rows, quarter, full, width = dims
    here = rows // count
    tokens = x.shape[0]
    head_width = blocks[0][2].shape[2]
    inner = 3 * head_width
    flat = [ref for b in blocks for ref, _ in b[5]]
    n = len(flat)
    half_out = head_width // 2
    nb = len(blocks)

    def body(ids_ref, low_ref, x_ref, bin_ref, ffn_ref, norm_ref, *refs):
        data = refs[: 3 * nb]
        w_refs = refs[3 * nb : 3 * nb + n]
        mix_out, grad_out, wo, sums = refs[3 * nb + n :]
        w_out = []
        at = 0
        for b in range(nb):
            m = len(blocks[b][5])
            w_out.append(
                whole_block(
                    w_refs[at : at + m], bases_of(blocks[b][5]), ids_ref[2], half_out, wo.at[b],
                    inner // 2,
                )
            )
            at += m
        masks = head_masks(head_width)
        sums[...] = jnp.zeros_like(sums)
        for b in range(nb):
            kk, place = blocks[b][:2]
            ol_ref, qkv_ref, p_ref = data[3 * b : 3 * b + 3]

            @pl.loop(0, here, unroll=True)
            def _(r):
                span = pl.ds(pl.multiple_of(r * full, full), full)
                dol = mm_nt(low_ref[span, :], w_out[b][...]).astype(bf16)
                query, key, value = (qkv_ref[place, i, span, :] for i in range(3))
                low_p = p_ref[place, r]
                prob = low_p.astype(f32)
                dos = stack_heads(dol, masks)
                dp = mm_nt(dos, value)
                ds = (prob * (dp - jnp.sum(dp * prob, axis=1, keepdims=True))).astype(bf16)
                dv = mm_tn(low_p, dos).astype(bf16)
                dq = (pick_heads(mm(ds, key), masks) * (HD ** -0.5)).astype(bf16)
                dk = (mm_tn(ds, stack_heads(query, masks)) * (HD ** -0.5)).astype(bf16)
                mix_out[b, span, 0:head_width] = dq
                mix_out[b, span, head_width : 2 * head_width] = dk
                mix_out[b, span, 2 * head_width :] = dv
                sums[b : b + 1, 0:head_width] += jnp.sum(dq.astype(f32), axis=0, keepdims=True)
                sums[b : b + 1, 256 : 256 + head_width] += jnp.sum(
                    dv.astype(f32), axis=0, keepdims=True
                )

            for c in range(3):
                part = slice(c * head_width, (c + 1) * head_width)
                grad_out[b, part, :] = mm_tn(mix_out[b, :, part], x_ref[...]).astype(bf16)
            grad_out[b, inner:width, :] = mm_tn(ol_ref[place], low_ref[...]).astype(bf16)
            lines = jnp.concatenate(
                [sums[b : b + 1], bin_ref[kk : kk + 1], norm_ref[0:3], ffn_ref[0:3]], axis=0
            )
            grad_out[b, width : width + 16, :] = two_terms(lines)

    return call(
        body,
        [shape_of((nb, tokens, inner)), shape_of((nb, width + 16, width))],
        [VM] * 2,
        [SM] + [VM] * (5 + 3 * nb + n),
        [
            pltpu.VMEM((nb, head_width, width), bf16),
            pltpu.VMEM((8, width), f32),
        ],
        us=13,
        name="attend_back",
        room=26,
        after=after,
    )(ids, low, x, *extras, *[v for b in blocks for v in b[2:5]], *flat)


def two_terms(lines):
    high = lines.astype(bf16)
    return jnp.concatenate([high, (lines - high.astype(f32)).astype(bf16)], axis=0)


def one_term(lines):
    return lines[0:8].astype(f32) + lines[8:16].astype(f32)


def peer_grad(lhs, rhs, got, after=()):
    tokens, width = rhs.shape
    rows = lhs.shape[1]

    def body(lhs_ref, rhs_ref, got_ref, out):
        for c in range(rows // 256):
            cols = slice(c * 256, (c + 1) * 256)
            out[cols, :] = (
                mm_tn(lhs_ref[:, cols], rhs_ref[...]) + got_ref[1, cols, :].astype(f32)
            ).astype(bf16)

    return call(
        body,
        shape_of((rows, width)),
        VM,
        [VM, VM, VM],
        us=0.2,
        name="peer_grad",
        room=10,
        after=after,
    )(lhs, rhs, got)


def shards(acc, ids_ref, devices, bits, size, send, keep):
    for p in range(devices):
        mirror = sum(((p >> j) & 1) << (bits - 1 - j) for j in range(bits))
        rows = acc[pl.ds(pl.multiple_of((ids_ref[0] ^ mirror) * size, 16), size), :]
        if p < devices // 2:
            keep[p * size : (p + 1) * size, :] = rows
        else:
            q = p - devices // 2
            send[q * size : (q + 1) * size, :] = rows.astype(bf16)


def own_grad(ids, lhs, rhs, got, crossed, devices, after=()):
    tokens, width = rhs.shape
    rows = lhs.shape[1]
    bits = devices.bit_length() - 1
    size = rows // devices

    def body(ids_ref, lhs_ref, rhs_ref, got_ref, cross_ref, send, keep, acc):
        for c in range(rows // 256):
            cols = slice(c * 256, (c + 1) * 256)
            acc[cols, :] = (
                mm_tn(lhs_ref[:, cols], rhs_ref[...])
                + got_ref[0, cols, :].astype(f32)
                + cross_ref[cols, :].astype(f32)
            )
        shards(acc, ids_ref, devices, bits, size, send, keep)

    return call(
        body,
        [shape_of((rows // 2, width)), shape_of((rows // 2, width), f32)],
        [VM, VM],
        [SM, VM, VM, VM, VM],
        [pltpu.VMEM((rows, width), f32)],
        us=0.2,
        name="own_grad",
        room=14,
        after=after,
    )(ids, lhs, rhs, got, crossed)


def peer_last(grads, got, at, after=()):
    _, high, width = grads.shape

    def body(a_ref, g_ref, out):
        out[0 : high - 16, :] = (
            a_ref[at, 0 : high - 16, :].astype(f32) + g_ref[1, 0 : high - 16, :].astype(f32)
        ).astype(bf16)
        out[high - 16 :, :] = two_terms(
            one_term(a_ref[at, high - 16 :, :]) + one_term(g_ref[1, high - 16 :, :])
        )

    return call(
        body, shape_of((high, width)), VM, [VM, VM], us=0.2, name="peer_last",
        room=12,
        after=after,
    )(grads, got)


def own_last(ids, grads, got, crossed, at, devices, after=()):
    _, high, width = grads.shape
    body_rows = high - 16
    bits = devices.bit_length() - 1
    size = body_rows // devices

    def body(ids_ref, a_ref, g_ref, c_ref, send, keep, vec, acc):
        acc[...] = (
            a_ref[at, 0:body_rows, :].astype(f32)
            + g_ref[0, 0:body_rows, :].astype(f32)
            + c_ref[0:body_rows, :].astype(f32)
        )
        shards(acc, ids_ref, devices, bits, size, send, keep)
        lines = (
            one_term(a_ref[at, body_rows:, :])
            + one_term(g_ref[0, body_rows:, :])
            + one_term(c_ref[body_rows:, :])
        )
        send[body_rows // 2 :, :] = two_terms(lines)
        vec[...] = lines

    return call(
        body,
        [
            shape_of((body_rows // 2 + 16, width)),
            shape_of((body_rows // 2, width), f32),
            shape_of((8, width), f32),
        ],
        [VM] * 3,
        [SM, VM, VM, VM],
        [pltpu.VMEM((body_rows, width), f32)],
        us=0.2,
        name="own_last",
        room=16,
        after=after,
    )(ids, grads, got, crossed)


def cut(keep, got, vec, after=()):
    high, width = keep.shape
    last = vec is not None
    tail = 16 if last else 0
    size = high // 4

    def body(*refs):
        keep_ref, got_ref = refs[:2]
        rest = refs[2:]
        if last:
            vec_ref, rest = rest[0], rest[1:]
            lines = vec_ref[...] + one_term(got_ref[high:, :])
            rest[4][...] = lines
        for p in range(4):
            span = slice(p * size, (p + 1) * size)
            total = keep_ref[span, :] + got_ref[span, :].astype(f32)
            if p == 0:
                rest[3][...] = total
            else:
                rest[p - 1][0:size, :] = total.astype(bf16)
                if last:
                    rest[p - 1][size:, :] = two_terms(lines)

    outs = [shape_of((size + tail, width))] * 3 + [shape_of((size, width), f32)]
    args = [keep, got]
    if last:
        outs.append(shape_of((8, width), f32))
        args.append(vec)
    return call(
        body, outs, [VM] * len(outs), [VM] * len(args), us=0.1, name="cut", room=8, after=after
    )(*args)


def gather_sum(keep, gots, vec, after=()):
    high, width = keep.shape
    last = vec is not None
    n = len(gots)

    def body(*refs):
        keep_ref, got_refs, rest = refs[0], refs[1 : 1 + n], refs[1 + n :]
        if last:
            vec_ref, rest = rest[0], rest[1:]
            lines = vec_ref[...]
            for got in got_refs:
                lines = lines + one_term(got[high:, :])
            rest[1][...] = lines
        total = keep_ref[...]
        for got in got_refs:
            total = total + got[0:high, :].astype(f32)
        rest[0][...] = total.astype(bf16)

    outs = [shape_of((high, width))]
    args = [keep, *gots]
    if last:
        outs.append(shape_of((8, width), f32))
        args.append(vec)
    return call(
        body, outs, [VM] * len(outs), [VM] * len(args), us=0.1, name="gather_sum", room=8, after=after
    )(*args)


def join(pieces, after=()):
    size, width = pieces[0].shape
    n = len(pieces)

    def body(*refs):
        for p in range(n):
            refs[n][p * size : (p + 1) * size, :] = refs[p][...]

    return call(
        body, shape_of((n * size, width)), VM, [VM] * n, us=0.1, name="join", room=4, after=after
    )(*pieces)


MASKS = (4, 2, 6)


def place_shards(ids_ref, pieces, devices, size, put):
    bits = devices.bit_length() - 1
    p = 0
    for piece in pieces:
        for q in range(piece.shape[0] // size):
            mirror = sum(((p >> j) & 1) << (bits - 1 - j) for j in range(bits))
            at = pl.multiple_of((ids_ref[0] ^ mirror) * size, 8)
            put(at, piece[q * size : (q + 1) * size, :].astype(f32))
            p += 1


def whole_grad(ids, pieces, devices, cuts, after=()):
    size, width = pieces[0].shape
    n = len(pieces)

    def body(ids_ref, *refs):
        outs = refs[n : n + len(cuts)]
        acc = refs[n + len(cuts)] if len(cuts) > 1 else outs[0]

        def put(at, rows):
            acc[pl.ds(at, size), :] = rows

        place_shards(ids_ref, refs[:n], devices, size, put)
        if len(cuts) > 1:
            base = 0
            for out, rows in zip(outs, cuts):
                out[...] = acc[base : base + rows, :]
                base += rows

    return call(
        body,
        [shape_of((rows, width), f32) for rows in cuts],
        [VM] * len(cuts),
        [SM] + [VM] * n,
        [pltpu.VMEM((size * devices, width), f32)] if len(cuts) > 1 else [],
        us=0.5,
        name="whole_grad",
        room=12,
        after=after,
    )(ids, *pieces)


def grad_input_rows(ids, dz1, mixes, parts, pooled, dims, after=()):
    devices, count, rows, quarter, full, width = dims
    here = rows // count
    tokens = here * full
    tile = here * quarter
    inner = mixes[0].shape[2]
    flat = [ref for p in parts for ref, _ in p]
    n = len(flat)
    turn = (1, 3, 2, 0)

    def body(ids_ref, dz_ref, m_a, m_b, pool_ref, *refs):
        w_refs = refs[:n]
        own, near, far = refs[n : n + 3]
        wq, acc = refs[n + 3 :]
        blocks = []
        at = 0
        for kk in range(count):
            m = len(parts[kk])
            blocks.append(
                whole_block(
                    w_refs[at : at + m], bases_of(parts[kk]), ids_ref[2], inner // 2, wq.at[kk % 2]
                )
            )
            at += m
        half = tokens // 2
        for i, kk in enumerate(turn):
            mix = (m_a, m_b)[i // 2]
            for m in range(2):
                span = slice(m * half, (m + 1) * half)
                part = mm(mix[i % 2, span, :], blocks[kk][...])
                if i == 0:
                    acc[span, :] = part + dz_ref[span, :]
                else:
                    acc[span, :] += part
        size = tile + here * SEGS
        for kk, (ref, base) in enumerate(piece_places((own, near, far, far), size)):
            for r in range(here):
                ref[base + r * quarter : base + (r + 1) * quarter, :] = acc[
                    r * full + kk * quarter : r * full + (kk + 1) * quarter, :
                ].astype(bf16)
            ref[base + tile : base + size, :] = pool_ref[...].astype(bf16)

    return call(
        body,
        [shape_of((m * (tile + here * SEGS), width)) for m in (1, 1, 2)],
        [VM] * 3,
        [SM] + [VM] * (4 + n),
        [
            pltpu.VMEM((2, inner, width), bf16),
            pltpu.VMEM((tokens, width), f32),
        ],
        us=6,
        name="grad_input_rows",
        room=22,
        after=after,
    )(ids, dz1, *mixes, pooled, *flat)


def land_grad(sent, pieces, dims, after=()):
    devices, count, rows, quarter, full, width = dims
    here = rows // count
    tile = here * quarter
    size = tile + here * SEGS

    def body(sent_ref, *refs):
        places = piece_places(refs[:count], size)
        out, pooled, sems = refs[count:]
        copies = []
        for kk, (ref, base) in enumerate(places):
            for j in range(here):
                at = kk * here + j
                copy = pltpu.make_async_copy(
                    ref.at[pl.ds(base + j * quarter, quarter)], out.at[sent_ref[at]], sems.at[at]
                )
                copy.start()
                copies.append(copy)
        for kk, (ref, base) in enumerate(places):
            lines = ref[base + tile : base + size, :].astype(f32)
            for j in range(here):
                pooled[sent_ref[kk * here + j]] = lines[j * SEGS : (j + 1) * SEGS]
        for copy in copies:
            copy.wait()

    return call(
        body,
        [shape_of((rows, quarter, width)), shape_of((rows, SEGS, width), f32)],
        [HB, VM],
        [SM] + [VM] * count,
        [pltpu.SemaphoreType.DMA((rows,))],
        us=0.5,
        name="land_grad",
        room=8,
        after=after,
    )(sent, *pieces)


def turn_output(hops, dims, after=()):
    devices, count, rows, quarter, full, width = dims
    cap, reach = rows // devices, devices // count
    part = cap * quarter
    tile = reach * part

    def body(*refs):
        hop_refs = refs[:reach]
        near, far, sems = refs[reach:]
        copies = []
        for kk, (ref, base) in enumerate(((near, 0), (far, 0), (far, tile))):
            for k in range(reach):
                copies.append(
                    pltpu.make_async_copy(
                        hop_refs[k].at[kk + 1],
                        ref.at[pl.ds(base + k * part, part)],
                        sems.at[kk * reach + k],
                    )
                )
        for copy in copies:
            copy.start()
        for copy in copies:
            copy.wait()

    return call(
        body,
        [shape_of((tile, width)), shape_of((2 * tile, width))],
        [VM, VM],
        [HB] * reach,
        [pltpu.SemaphoreType.DMA((3 * reach,))],
        us=0.1,
        name="turn_output",
        room=8,
        after=after,
    )(*hops)


def land_output(spots, hops, pieces, dims, after=()):
    devices, count, rows, quarter, full, width = dims
    here, cap, reach = rows // count, rows // devices, devices // count
    tile = here * quarter

    def body(spots_ref, *refs):
        hop_refs = refs[:reach]
        places = piece_places((None,) + refs[reach : reach + count - 1], tile)
        out, sems = refs[reach + count - 1 :]
        copies = []
        for kk in range(count):
            for j in range(here):
                at = kk * here + j
                if kk == 0:
                    src = hop_refs[j // cap].at[0, pl.ds((j % cap) * quarter, quarter)]
                else:
                    ref, base = places[kk]
                    src = ref.at[pl.ds(base + j * quarter, quarter)]
                copies.append(pltpu.make_async_copy(src, out.at[spots_ref[at]], sems.at[at]))
        for copy in copies:
            copy.start()
        for copy in copies:
            copy.wait()

    return call(
        body,
        shape_of((rows, quarter, width)),
        HB,
        [SM] + [VM] * (reach + count - 1),
        [pltpu.SemaphoreType.DMA((rows,))],
        us=0.5,
        name="land_output",
        room=8,
        after=after,
    )(spots, *hops, *pieces)


def swap(values, axis, bit):
    return lax.ppermute(values, axis, [(i, i ^ bit) for i in range(lax.axis_size(axis))])


def per_device(
    tokens_in, seg, route, w_qkv, b_qv, w_out, b_out, gain_attn, bias_attn, w_in, b_in, w_down,
    b_down, gain_ffn, bias_ffn, out_grad, pool_grad,
):
    devices, count = lax.axis_size("dp"), lax.axis_size("mp")
    rows, quarter, width = tokens_in.shape
    full = seg.shape[1]
    dims = (devices, count, rows, quarter, full, width)
    reach = devices // count
    head_width = w_qkv.shape[2]
    inner = 3 * head_width

    def hop(values, k):
        return lax.ppermute(
            values,
            ("dp", "mp"),
            [
                (s * count + f, (s ^ (f + count * k)) * count + f)
                for s in range(devices)
                for f in range(count)
            ],
        )

    wq = w_qkv.transpose(1, 2, 0).reshape(inner, width)
    half_rows = (inner + head_width) // 2
    *sends, segr, sent, spots, ids = prep_rows(
        route, seg, tokens_in, b_qv, b_in, (wq, w_out), dims
    )
    near_q, near_o, near_i, near_d = (swap(v, "mp", 1) for v in (wq, w_out, w_in, w_down))
    og_sends = prep_cot(spots, out_grad, dims, (near_q,))
    ogs = [hop(og_sends[k], k) for k in range(reach)]
    pieces = exchange(*sends, before=(near_q, near_o, near_i, near_d, *ogs))

    def later(values, after):
        return lax.optimization_barrier((values, after))[0]

    def crossed(half, bit, first, second):
        direct = later(swap(half, "mp", 2), first)
        relayed = swap(direct, "dp", bit)
        far = (direct, relayed)
        return [
            [(v, 0) for v in far],
            [(swap(direct, "mp", 1), 0), (swap(later(relayed, second), "mp", 1), 0)],
        ]

    below = sends[2].shape[0] - half_rows
    relay_q = swap(pieces[2][below:], "dp", 1)
    half_in = prep_halves((w_in,), 1, (pieces[2],))
    x, ol_a, qkv_a, p_a = attend(
        ids, segr, pieces, [[(wq, 0)], [(near_q, 0)]], (0, 1), inner, dims, True,
        (half_in,),
    )
    relay_q3 = swap(later(relay_q, x), "mp", 1)
    far_q = [(pieces[2], below), (relay_q, 0)]
    far_q3 = [(pieces[3], below), (relay_q3, 0)]
    half_dn = prep_halves((w_down,), 2, (x,))
    ol_b, qkv_b, p_b = attend(
        ids, segr, pieces, [far_q, far_q3], (2, 3), inner, dims, False, (half_dn,)
    )
    q_parts = [[(wq, 0)], [(near_q, 0)], far_q, far_q3]
    wo_parts = [[(w_out, 0)], [(near_o, 0)], far_q, far_q3]
    al, hat, inv, acc, hl0, hl1, gp0, gp1 = ffn_near(
        ids, x, (ol_a, ol_b), pieces, (b_out, gain_attn, bias_attn), wo_parts, (w_in, near_i),
        (w_down, near_d), inner, dims,
    )
    in_parts = [[(w_in, 0)], [(near_i, 0)], *crossed(half_in, 1, x, ol_b)]
    hl2, hl3, gp2, gp3 = ffn_far(ids, al, pieces, in_parts[2:], dims)
    dn_parts = [[(w_down, 0)], [(near_d, 0)], *crossed(half_dn, 2, x, al)]
    tk0, tk1, pooled, dz, low, ffn_sums, down_pair = ffn_down(
        ids, sent, segr, al, acc, (hl1, hl2, hl3), (b_down, gain_ffn, bias_ffn), ogs, pool_grad,
        dn_parts[2:], dims,
    )
    got_down = swap(down_pair, "mp", 1)
    *dus, bin_sums = ffn_back(ids, low, (gp0, gp1, gp2, gp3), dn_parts, dims)
    down_far = peer_grad(hl2, low, got_down, (bin_sums,))
    hops = [hop(t, k) for k, t in enumerate(lax.optimization_barrier((tk0, tk1, down_far))[:2])]
    crossed_down = swap(down_far, "mp", 2)
    dz1, low1, norm_sums, in_pair = norm_back_attn(
        ids, dus, al, dz, hat, inv, gain_attn, in_parts, dims, (down_far,)
    )
    got_in = swap(in_pair, "mp", 1)
    extras = (bin_sums, ffn_sums, norm_sums)
    mix_a, grads_a = attend_back(
        ids, low1, x,
        [(1, 1, ol_a, qkv_a, p_a, wo_parts[1]), (3, 1, ol_b, qkv_b, p_b, wo_parts[3])],
        extras, dims,
    )
    got_last = swap(grads_a, "mp", 1)
    in_far = peer_grad(al, dus[2], got_in, (grads_a,))
    crossed_in = swap(in_far, "mp", 2)
    turned = turn_output(hops, dims, (in_far,))
    send_down, keep_down = own_grad(
        ids, hl0, low, got_down, crossed_down, devices, (turned[0],)
    )
    mix_b, grads_b = attend_back(
        ids, low1, x,
        [(2, 0, ol_b, qkv_b, p_b, wo_parts[2]), (0, 0, ol_a, qkv_a, p_a, wo_parts[0])],
        extras, dims, (send_down,),
    )
    last_far = peer_last(grads_b, got_last, 0)
    crossed_last = swap(last_far, "mp", 2)

    def places_of(parts):
        return [swap(part, "dp", mask) for part, mask in zip(parts, MASKS)]

    cut_down = cut(keep_down, swap(send_down, "dp", 1), None, (last_far,))
    down_places = places_of(cut_down[:3])
    gx = grad_input_rows(ids, dz1, (mix_a, mix_b), q_parts, pooled, dims, (cut_down[0],))
    (shard_down,) = gather_sum(cut_down[3], down_places, None, (gx[0],))
    down_spread = [shard_down] + places_of([shard_down] * 3)
    send_in, keep_in = own_grad(
        ids, al, dus[0], got_in, crossed_in, devices, (shard_down,)
    )
    in_half = swap(send_in, "dp", 1)
    cut_in = cut(keep_in, in_half, None, (send_in,))
    in_places = places_of(cut_in[:3])
    half_down = join(down_spread, (cut_in[0],))
    down_spread.append(swap(half_down, "dp", 1))
    (shard_in,) = gather_sum(cut_in[3], in_places, None, (half_down,))
    in_spread = [shard_in] + places_of([shard_in] * 3)
    send, keep, vec = own_last(
        ids, grads_b, got_last, crossed_last, 1, devices, (shard_in,)
    )
    last_half = swap(send, "dp", 1)
    *gx, turned_near, turned_far, _ = lax.optimization_barrier((*gx, *turned, send))
    landed = exchange(None, turned_near, turned_far)[1:]
    gx_landed = exchange(*gx)
    half_in = join(in_spread, (send,))
    in_spread.append(swap(half_in, "dp", 1))
    cut_last = cut(keep, last_half, vec, (half_in,))
    last_places = places_of(cut_last[:3])
    shard_last, vec = gather_sum(cut_last[3], last_places, cut_last[4])
    last_spread = [shard_last] + places_of([shard_last] * 3)
    half_last = join(last_spread, (shard_last,))
    last_spread.append(swap(half_last, "dp", 1))
    (g_down,) = whole_grad(ids, down_spread, devices, (width,), (half_last,))
    (g_in,) = whole_grad(ids, in_spread, devices, (width,), (half_last,))
    tokens_out = land_output(spots, hops, landed, dims, (half_last,))
    grad_input, pooled_out = land_grad(sent, gx_landed, dims, (half_last,))
    g_qkv, g_out = whole_grad(ids, last_spread, devices, (inner, head_width))
    g_qkv = g_qkv.reshape(3, head_width, width).transpose(2, 0, 1)
    g_bqv = jnp.stack([vec[0, :head_width], vec[0, 256 : 256 + head_width]])
    return (
        tokens_out, pooled_out, grad_input, g_qkv, g_bqv, g_out,
        vec[2], vec[3], vec[4], g_in, vec[1], g_down, vec[5], vec[6], vec[7],
    )


def solution(mesh):
    devices, count = mesh.shape["dp"], mesh.shape["mp"]

    def body(*args):
        rows = args[0].shape[0]
        even = rows % devices == 0 and devices % count == 0 and count == 4
        even = even and devices & (devices - 1) == 0 and rows // count == 2 * (rows // devices)
        return (per_device if even else per_device_general)(*args)

    return jax.shard_map(
        body,
        mesh=mesh,
        in_specs=(
            P("dp", "mp", None),
            P(),
            P(),
            P(None, None, "mp"),
            P(None, "mp"),
            P("mp", None),
            P(),
            P(),
            P(),
            P(None, "mp"),
            P("mp"),
            P("mp", None),
            P(),
            P(),
            P(),
            P("dp", None, None),
            P("dp", None, None),
        ),
        out_specs=(
            P("dp", "mp", None),
            P("dp", None, None),
            P("dp", "mp", None),
            P(None, None, "mp"),
            P(None, "mp"),
            P("mp", None),
            P(),
            P(),
            P(),
            P(None, "mp"),
            P("mp"),
            P("mp", None),
            P(),
            P(),
            P(),
        ),
        check_vma=False,
    )
```

```python
import jax
import jax.numpy as jnp
from jax import lax
from jax.experimental import pallas as pl
from jax.experimental.pallas import tpu as pltpu
from jax.sharding import PartitionSpec as P

HD = 64
SEGS = 4


EPSILON = 1e-12
MASKED = -1e30
f32 = jnp.float32
bf16 = jnp.bfloat16


def normalize(values):
    centre = values - jnp.mean(values, axis=-1, keepdims=True)
    scale_inv = lax.rsqrt(jnp.mean(centre * centre, axis=-1, keepdims=True) + EPSILON)
    return (centre * scale_inv, scale_inv[..., 0])


def norm_back(grad_hat, normed_hat, inverse):
    mean_grad = jnp.mean(grad_hat, axis=-1, keepdims=True)
    mean_proj = jnp.mean(grad_hat * normed_hat, axis=-1, keepdims=True)
    return inverse[..., None] * (grad_hat - mean_grad - normed_hat * mean_proj)


def pack_rows(values, position, filled):
    picked = jnp.take(values, position, axis=0)
    shape_mask = filled.reshape((-1,) + (1,) * (values.ndim - 1))
    return jnp.where(shape_mask, picked, jnp.zeros_like(picked))


def per_device_general(
    tokens_in,
    seg,
    route,
    w_qkv,
    b_qv,
    w_out,
    b_out,
    gain_attn,
    bias_attn,
    w_in,
    b_in,
    w_down,
    b_down,
    gain_ffn,
    bias_ffn,
    out_grad,
    pool_grad,
):
    f32 = jnp.float32
    bf16 = jnp.bfloat16
    devices = lax.axis_size("dp")
    row_local = tokens_in.shape[0]
    quarter = tokens_in.shape[1]
    all_rows = route.shape[0]
    capacity = max(1, row_local // devices)
    buffer_len = devices * capacity
    my_index = lax.axis_index("dp")
    target_dev = route // row_local
    dest_grid = target_dev.reshape(devices, row_local)
    before = jnp.arange(row_local)[None, :] < jnp.arange(row_local)[:, None]
    same_dest = dest_grid[:, :, None] == dest_grid[:, None, :]
    earlier_count = (
        jnp.sum(jnp.where(same_dest & before[None], 1, 0), axis=2).reshape(-1).astype(jnp.int32)
    )
    slot_out = target_dev * capacity + earlier_count
    slot_in = jnp.arange(all_rows, dtype=jnp.int32) // row_local * capacity + earlier_count
    own_slots = lax.dynamic_slice_in_dim(slot_out, my_index * row_local, row_local)
    local_rows = jnp.arange(row_local, dtype=jnp.int32)
    send_pos = jnp.zeros(buffer_len, jnp.int32).at[own_slots].set(local_rows)
    send_fill = jnp.zeros(buffer_len, jnp.bool_).at[own_slots].set(True)
    arrive = jnp.where(target_dev == my_index, route - my_index * row_local, row_local)
    recv_pos = jnp.zeros(row_local, jnp.int32).at[arrive].set(slot_in, mode="drop")
    anchor = (
        jnp.zeros(row_local, jnp.int32)
        .at[arrive]
        .set(jnp.arange(all_rows, dtype=jnp.int32), mode="drop")
    )
    back_pos = jnp.zeros(buffer_len, jnp.int32).at[recv_pos].set(local_rows)
    back_fill = jnp.zeros(buffer_len, jnp.bool_).at[recv_pos].set(True)
    arrived = lax.all_to_all(
        pack_rows(tokens_in, send_pos, send_fill), "dp", split_axis=0, concat_axis=0, tiled=True
    )
    rows_x = jnp.take(arrived, recv_pos, axis=0)
    segment = jnp.take(seg, anchor, axis=0)
    full_len = segment.shape[1]
    mp_index = lax.axis_index("mp")

    def own_part(values):
        return lax.dynamic_slice_in_dim(values, mp_index * quarter, quarter, 1)

    gathered = lax.all_gather(rows_x, "mp", axis=1, tiled=True)
    head_width = w_qkv.shape[2]
    local_heads = head_width // HD
    head_shape = (row_local, full_len, local_heads, HD)
    projected = jnp.einsum("rsd,dcf->rscf", gathered, w_qkv, preferred_element_type=f32)
    query_heads = (projected[:, :, 0] + b_qv[0]).astype(bf16).reshape(head_shape)
    key_heads = projected[:, :, 1].astype(bf16).reshape(head_shape)
    value_heads = (projected[:, :, 2] + b_qv[1]).astype(bf16).reshape(head_shape)
    allowed = (segment[:, :, None] == segment[:, None, :])[:, None]
    factor = HD ** (-0.5)

    def scores_of():
        raw_scores = (
            jnp.einsum("rqhe,rkhe->rhqk", query_heads, key_heads, preferred_element_type=f32)
            * factor
        )
        return jnp.where(allowed, raw_scores, MASKED)

    scores = scores_of()
    row_peak = jnp.max(scores, axis=-1, keepdims=True)
    raised = jnp.exp(scores - row_peak)
    weight_total = jnp.sum(raised, axis=-1, keepdims=True)
    log_total = row_peak + jnp.log(weight_total)
    attention = raised / weight_total
    attended = jnp.einsum(
        "rhqk,rkhe->rqhe", attention.astype(bf16), value_heads, preferred_element_type=f32
    )
    attended = attended.astype(bf16).reshape(row_local, full_len, head_width)
    branch = jnp.einsum("rsf,fd->rsd", attended, w_out, preferred_element_type=f32)
    summed_branch = lax.psum_scatter(branch, "mp", scatter_dimension=1, tiled=True)
    hat_attn, inv_attn = normalize(rows_x.astype(f32) + summed_branch + b_out)
    normed_low = (hat_attn * gain_attn + bias_attn).astype(bf16)
    normed_all = lax.all_gather(normed_low, "mp", axis=1, tiled=True)
    hidden = jnp.einsum("rsd,df->rsf", normed_all, w_in, preferred_element_type=f32) + b_in
    active, gelu_back = jax.vjp(lambda values: jax.nn.gelu(values, approximate=False), hidden)
    active_low = active.astype(bf16)
    ffn_part = jnp.einsum("rsf,fd->rsd", active_low, w_down, preferred_element_type=f32)
    ffn_total = lax.psum(ffn_part, "mp")
    hat_ffn, inv_ffn = normalize(normed_all.astype(f32) + ffn_total + b_down)
    block_out = hat_ffn * gain_ffn + bias_ffn
    output_rows = own_part(block_out).astype(bf16)
    member = (segment[:, :, None] == jnp.arange(SEGS)[None, None, :]).astype(f32)
    counts = jnp.sum(member, axis=1)
    pooled_rows = (
        jnp.einsum("rsg,rsd->rgd", member, block_out, precision=lax.Precision.HIGHEST)
        / counts[:, :, None]
    )
    pooled_back = lax.all_to_all(
        pack_rows(pooled_rows, back_pos, back_fill).astype(jnp.bfloat16),
        "dp",
        split_axis=0,
        concat_axis=0,
        tiled=True,
    ).astype(jnp.float32)
    pooled = jnp.take(pooled_back, own_slots, axis=0)
    pool_arrived = lax.all_to_all(
        pack_rows(pool_grad, send_pos, send_fill), "dp", split_axis=0, concat_axis=0, tiled=True
    )
    pool_rows = jnp.take(pool_arrived, recv_pos, axis=0)
    grad_final = out_grad.astype(f32) + jnp.einsum(
        "rsg,rgd->rsd", member, pool_rows / counts[:, :, None], precision=lax.Precision.HIGHEST
    )
    grad_mix = norm_back(grad_final * gain_ffn, hat_ffn, inv_ffn)
    grad_gain_ffn = jnp.sum(grad_final * hat_ffn, axis=(0, 1))
    grad_bias_ffn = jnp.sum(grad_final, axis=(0, 1))
    grad_b_down = jnp.sum(grad_mix, axis=(0, 1))
    mix_low = grad_mix.astype(bf16)
    grad_w_down = jnp.einsum("rsf,rsd->fd", active_low, mix_low, preferred_element_type=f32)
    grad_active = jnp.einsum("rsd,fd->rsf", mix_low, w_down, preferred_element_type=f32)
    grad_hidden = gelu_back(grad_active)[0].astype(bf16)
    grad_w_in = jnp.einsum("rsd,rsf->df", normed_all, grad_hidden, preferred_element_type=f32)
    grad_b_in = jnp.sum(grad_hidden.astype(f32), axis=(0, 1))
    normed_part = jnp.einsum("rsf,df->rsd", grad_hidden, w_in, preferred_element_type=f32)
    grad_normed = lax.psum_scatter(normed_part, "mp", scatter_dimension=1, tiled=True) + own_part(
        grad_mix
    )
    gain_attn_part = jnp.sum(grad_normed * hat_attn, axis=(0, 1))
    bias_attn_part = jnp.sum(grad_normed, axis=(0, 1))
    grad_inner = norm_back(grad_normed * gain_attn, hat_attn, inv_attn)
    stat_terms = jnp.stack([jnp.sum(grad_inner, axis=(0, 1)), gain_attn_part, bias_attn_part])[None]
    inner_all, stats_all = (
        lax.all_gather(grad_inner.astype(jnp.bfloat16), "mp", axis=1, tiled=True).astype(
            grad_inner.dtype
        ),
        lax.all_gather(stat_terms.astype(jnp.bfloat16), "mp", axis=0, tiled=True).astype(
            stat_terms.dtype
        ),
    )
    stat_sums = jnp.sum(stats_all, axis=0)
    inner_low = inner_all.astype(bf16)
    grad_w_out = jnp.einsum("rsf,rsd->fd", attended, inner_low, preferred_element_type=f32)
    grad_attended = (
        jnp.einsum("rsd,fd->rsf", inner_low, w_out, preferred_element_type=f32)
        .astype(bf16)
        .reshape(head_shape)
    )
    again = jnp.exp(scores_of() - log_total)
    grad_prob = jnp.einsum(
        "rqhe,rkhe->rhqk", grad_attended, value_heads, preferred_element_type=f32
    )
    grad_values = jnp.einsum(
        "rhqk,rqhe->rkhe", again.astype(bf16), grad_attended, preferred_element_type=f32
    )
    grad_scores = (again * (grad_prob - jnp.sum(grad_prob * again, axis=-1, keepdims=True))).astype(
        bf16
    )
    grad_query = (
        jnp.einsum("rhqk,rkhe->rqhe", grad_scores, key_heads, preferred_element_type=f32) * factor
    ).astype(bf16)
    grad_keys = (
        jnp.einsum("rhqk,rqhe->rkhe", grad_scores, query_heads, preferred_element_type=f32) * factor
    ).astype(bf16)
    flat_shape = (row_local, full_len, head_width)
    grad_mixed = jnp.stack(
        [
            grad_query.reshape(flat_shape),
            grad_keys.reshape(flat_shape),
            grad_values.astype(bf16).reshape(flat_shape),
        ],
        axis=2,
    )
    grad_w_qkv = jnp.einsum("rsd,rscf->dcf", gathered, grad_mixed, preferred_element_type=f32)
    grad_b_qv = jnp.stack(
        [
            jnp.sum(grad_mixed[:, :, 0].astype(f32), axis=(0, 1)),
            jnp.sum(grad_mixed[:, :, 2].astype(f32), axis=(0, 1)),
        ]
    )
    input_part = jnp.einsum("rscf,dcf->rsd", grad_mixed, w_qkv, preferred_element_type=f32)
    grad_rows = (
        lax.psum_scatter(input_part, "mp", scatter_dimension=1, tiled=True) + grad_inner
    ).astype(bf16)
    grad_home = lax.all_to_all(
        pack_rows(grad_rows, back_pos, back_fill), "dp", split_axis=0, concat_axis=0, tiled=True
    )
    grad_input = jnp.take(grad_home, own_slots, axis=0)
    vector_grads = jnp.stack(
        [stat_sums[0], stat_sums[1], stat_sums[2], grad_b_down, grad_gain_ffn, grad_bias_ffn]
    )
    totals = lax.psum(
        (grad_w_qkv, grad_b_qv, grad_w_out, grad_w_in, grad_b_in, grad_w_down, vector_grads), "dp"
    )
    return (
        output_rows,
        pooled,
        grad_input,
        totals[0],
        totals[1],
        totals[2],
        totals[6][0],
        totals[6][1],
        totals[6][2],
        totals[3],
        totals[4],
        totals[5],
        totals[6][3],
        totals[6][4],
        totals[6][5],
    )


VM = pl.BlockSpec(memory_space=pltpu.VMEM)
SM = pl.BlockSpec(memory_space=pltpu.SMEM)
HB = pl.BlockSpec(memory_space=pl.ANY)
HM = pl.BlockSpec(memory_space=pltpu.HBM)
MIB = 1024 * 1024
PACE = 2e9


def shape_of(shape, dtype=bf16):
    return jax.ShapeDtypeStruct(shape, dtype)


def call(
    body, outs, out_specs, in_specs, scratch=(), us=2, room=16, name=None, after=()
):
    made = pl.pallas_call(
        body,
        out_shape=outs,
        in_specs=in_specs,
        out_specs=out_specs,
        scratch_shapes=list(scratch),
        compiler_params=pltpu.CompilerParams(vmem_limit_bytes=room * MIB),
        cost_estimate=pl.CostEstimate(flops=int(us * PACE), bytes_accessed=0, transcendentals=0),
        name=name,
    )

    def run(*args):
        if after:
            args = list(args)
            at = min(range(len(args)), key=lambda n: args[n].size)
            args[at] = lax.optimization_barrier((args[at], *after))[0]
        return made(*args)

    return run


def mm(a, b):
    return lax.dot_general(a, b, (((1,), (0,)), ((), ())), preferred_element_type=f32)


def mm_nt(a, b):
    return lax.dot_general(a, b, (((1,), (1,)), ((), ())), preferred_element_type=f32)


def mm_tn(a, b):
    return lax.dot_general(a, b, (((0,), (0,)), ((), ())), preferred_element_type=f32)


def split3(values):
    high = values.astype(bf16)
    rest = values - high.astype(f32)
    middle = rest.astype(bf16)
    low = (rest - middle.astype(f32)).astype(bf16)
    return high, middle, low


def piece_places(refs, size):
    return [(refs[0], 0), (refs[1], 0), (refs[2], 0), (refs[3], size)]


def exchange(own, near, far, before=()):
    near = swap(near, "mp", 1)
    crossed = swap(far, "mp", 2)
    if before:
        crossed = lax.optimization_barrier((crossed, near, *before))[0]
    return [own, near, crossed, swap(crossed, "mp", 1)]


def prep_rows(route, seg, tokens, b_qv, b_in, weights, dims):
    devices, count, rows, quarter, full, width = dims
    here, cap = rows // count, rows // devices
    head_width = b_qv.shape[1]
    tile = here * quarter
    total = devices * rows
    halves = [w.shape[0] // 2 for w in weights]

    def body(
        route_ref, seg_ref, tok, bqv_ref, bin_ref, wq, wo, x0, x1, far, segr, sent_ref, spots_ref,
        ids_ref, lists, sems,
    ):
        my, mi = lax.axis_index("dp"), lax.axis_index("mp")
        crossing = []
        base = 2 * (tile + 16)
        for n, (src, half) in enumerate(zip((wq, wo), halves)):
            crossing.append(
                pltpu.make_async_copy(
                    src.at[pl.ds(pl.multiple_of(lax.rem(my, 2) * half, 16), half)],
                    far.at[pl.ds(base, half)],
                    sems.at[rows + 2 + n],
                )
            )
            crossing[n].start()
            base += half
        ids_ref[0] = my
        ids_ref[1] = mi
        ids_ref[2] = lax.rem(my, 2)
        places = piece_places((x0, x1, far, far), tile + 16)
        across = jnp.broadcast_to(route_ref[...].reshape(1, total), (total, total)).astype(f32)
        down = across.T.astype(jnp.int32)
        across = across.astype(jnp.int32)
        r = lax.broadcasted_iota(jnp.int32, (total, total), 0)
        c = lax.broadcasted_iota(jnp.int32, (total, total), 1)
        key_down = lax.div(down, rows) * total + r
        key_across = lax.div(across, rows) * total + c
        before = (lax.div(r, rows) == lax.div(c, rows)) & (key_across < key_down)
        rank = jnp.sum(jnp.where(before, 1.0, 0.0), axis=1, keepdims=True).astype(jnp.int32)
        at = lax.rem(c, rows)
        partner = my ^ ((mi ^ lax.div(at, here)) + count * lax.rem(lax.div(at, cap), here // cap))
        copy_at = lax.rem(at, cap)
        source = lax.div(r, rows)
        going = (source == my) & (rank == partner * cap + copy_at)
        coming = (source == partner) & (rank == my * cap + copy_at)
        lists[0:1, :] = jnp.sum(
            jnp.where(going, lax.rem(r, rows), 0).astype(f32), axis=0, keepdims=True
        ).astype(jnp.int32)
        lists[1:2, :] = jnp.sum(
            jnp.where(coming, down - my * rows, 0).astype(f32), axis=0, keepdims=True
        ).astype(jnp.int32)
        moves = [
            pltpu.make_async_copy(lists.at[0], sent_ref, sems.at[rows]),
            pltpu.make_async_copy(lists.at[1], spots_ref, sems.at[rows + 1]),
        ]
        for move in moves:
            move.start()
        zero = jnp.zeros((16, width), bf16)
        tail = x0.at[pl.ds(tile, 16)]
        tail[...] = zero
        for n, term in enumerate(split3(bqv_ref[...])):
            tail[n : n + 1, 0:head_width] = term[0:1]
            tail[n : n + 1, 256 : 256 + head_width] = term[1:2]
        for n, term in enumerate(split3(bin_ref[...].reshape(1, width))):
            tail[3 + n : 4 + n, :] = term
        for ref, base in places[1:]:
            ref[base + tile : base + tile + 16, :] = tail[...]
        for move in moves:
            move.wait()
        copies = []
        for kk in reversed(range(count)):
            for n in range(here):
                k = kk * here + n
                copies.append(
                    pltpu.make_async_copy(
                        tok.at[sent_ref[k]],
                        places[kk][0].at[pl.ds(places[kk][1] + n * quarter, quarter)],
                        sems.at[k],
                    )
                )
        for copy in copies:
            copy.start()
        for n in range(here):
            segr[n : n + 1, :] = seg_ref[pl.ds(my * rows + sent_ref[n], 1), :]
        segr[here:8, :] = jnp.zeros((8 - here, full), jnp.int32)
        lane = lax.broadcasted_iota(jnp.int32, (8, full), 1)
        lines = segr[...]
        bit = 1
        while bit < count:
            step = bit * quarter
            swapped = jnp.where(
                lax.rem(lax.div(lane, step), 2) == 0,
                pltpu.roll(lines, full - step, 1),
                pltpu.roll(lines, step, 1),
            )
            lines = jnp.where(lax.rem(lax.div(mi, bit), 2) == 1, swapped, lines)
            bit *= 2
        segr[...] = lines
        for copy in copies + crossing:
            copy.wait()

    return call(
        body,
        [
            shape_of((tile + 16, width)),
            shape_of((tile + 16, width)),
            shape_of((2 * (tile + 16) + sum(halves), width)),
        ]
        + [
            shape_of((8, full), jnp.int32),
            shape_of((total,), jnp.int32),
            shape_of((total,), jnp.int32),
            shape_of((3,), jnp.int32),
        ],
        [VM] * 4 + [SM] * 3,
        [VM, VM, HM, VM, VM, HM, HM],
        [pltpu.VMEM((8, total), jnp.int32), pltpu.SemaphoreType.DMA((rows + 4,))],
        us=2,
        name="prep_rows",
        room=60,
    )(route, seg, tokens, b_qv, b_in, *weights)


def prep_halves(weights, bit, after=()):
    width = weights[0].shape[1]
    halves = [w.shape[0] // 2 for w in weights]
    n = len(weights)

    def body(*refs):
        out, sems = refs[n:]
        parity = lax.rem(lax.div(lax.axis_index("dp"), bit), 2)
        copies = []
        base = 0
        for at, half in enumerate(halves):
            copies.append(
                pltpu.make_async_copy(
                    refs[at].at[pl.ds(pl.multiple_of(parity * half, 16), half)],
                    out.at[pl.ds(base, half)],
                    sems.at[at],
                )
            )
            base += half
        for copy in copies:
            copy.start()
        for copy in copies:
            copy.wait()

    return call(
        body,
        shape_of((sum(halves), width)),
        VM,
        [HM] * n,
        [pltpu.SemaphoreType.DMA((n,))],
        us=0.1,
        name="prep_halves",
        room=4,
        after=after,
    )(*weights)


def prep_cot(asked, out_grad, dims, after):
    devices, count, rows, quarter, full, width = dims
    cap, reach = rows // devices, devices // count

    def body(asked_ref, og, *refs):
        outs, sems = refs[:reach], refs[reach]
        copies = []
        for k in range(reach):
            for c in range(cap):
                at = k * cap + c
                copies.append(
                    pltpu.make_async_copy(og.at[asked_ref[at]], outs[k].at[c], sems.at[at])
                )
        for copy in copies:
            copy.start()
        for copy in copies:
            copy.wait()

    return call(
        body,
        [shape_of((cap, full, width))] * reach,
        [VM] * reach,
        [SM, HM],
        [pltpu.SemaphoreType.DMA((reach * cap,))],
        us=0.1,
        name="prep_cot",
        room=6,
        after=after,
    )(asked, out_grad)


def bias_rows(piece, at, count):
    terms = piece[at : at + 16, :].astype(f32)
    first = 0 if count == 0 else 3
    return terms[first : first + 1] + terms[first + 1 : first + 2] + terms[first + 2 : first + 3]


def head_masks(head_width):
    lane = lax.broadcasted_iota(jnp.int32, (1, head_width), 1)
    return [(lane >= h * HD) & (lane < (h + 1) * HD) for h in range(head_width // HD)]


def stack_heads(values, masks):
    zero = jnp.zeros_like(values)
    return jnp.concatenate([jnp.where(mask, values, zero) for mask in masks], axis=0)


def pick_heads(stacked, masks):
    size = stacked.shape[0] // len(masks)
    out = stacked[:size]
    for h in range(1, len(masks)):
        out = jnp.where(masks[h], stacked[h * size : (h + 1) * size], out)
    return out


def parity_of(ids_ref, bit):
    return lax.rem(lax.div(ids_ref[0], bit), 2)


def whole_block(refs, bases, parity, half, dst, row=0):
    if len(refs) == 1:
        return refs[0]
    for ref, base, place in zip(refs, bases, (parity, 1 - parity)):
        dst[pl.ds(pl.multiple_of(place * half, 16), half), :] = ref[
            base + row : base + row + half, :
        ]
    return dst


def bases_of(part):
    return [base for _, base in part]


def attend(ids, segr, pieces, parts, pair, inner, dims, keep_x, after=()):
    devices, count, rows, quarter, full, width = dims
    here = rows // count
    tokens = here * full
    tile = here * quarter
    head_width = inner // 3
    n_heads = head_width // HD
    n_parts = [len(p) for p in parts]
    flat = [ref for p in parts for ref, _ in p]

    def body(ids_ref, segr_ref, *refs):
        places = piece_places(refs[:count], tile + 16)
        w_refs = refs[count : count + len(flat)]
        out = list(refs[count + len(flat) :])
        if keep_x:
            x_out = out.pop(0)
        ol_out, qkv_out, p_out, x_ref, w_ref = out
        blocks = []
        at = 0
        for b, n in enumerate(n_parts):
            blocks.append(
                whole_block(w_refs[at : at + n], bases_of(parts[b]), ids_ref[2], inner // 2, w_ref.at[b])
            )
            at += n
        for r in range(here):
            for kk in range(count):
                ref, base = places[kk]
                x_ref[r * full + kk * quarter : r * full + (kk + 1) * quarter, :] = ref[
                    base + r * quarter : base + (r + 1) * quarter, :
                ]
        if keep_x:
            x_out[...] = x_ref[...]
        masks = head_masks(head_width)
        for b in range(2):
            ref, base = places[pair[b]]
            bias = bias_rows(ref, base + tile, 0)
            bias_q, bias_v = bias[:, 0:head_width], bias[:, 256 : 256 + head_width]

            @pl.loop(0, here, unroll=True)
            def _(r):
                start = pl.multiple_of(r * full, full)
                projected = mm_nt(x_ref[pl.ds(start, full), :], blocks[b][...])
                query = (projected[:, 0:head_width] + bias_q).astype(bf16)
                key = projected[:, head_width : 2 * head_width].astype(bf16)
                value = (projected[:, 2 * head_width :] + bias_v).astype(bf16)
                line = segr_ref[pl.ds(r, 1), :].astype(f32)
                wide = jnp.broadcast_to(line, (full, full))
                allowed = wide == wide.T
                stacked = stack_heads(query, masks)
                raw = mm_nt(stacked, key) * (HD ** -0.5)
                allowed3 = jnp.concatenate([allowed] * n_heads, axis=0)
                scores = jnp.where(allowed3, raw, MASKED)
                raised = jnp.exp(scores - jnp.max(scores, axis=1, keepdims=True))
                prob = raised / jnp.sum(raised, axis=1, keepdims=True)
                low = prob.astype(bf16)
                attended = pick_heads(mm(low, value), masks).astype(bf16)
                ol_out[b, pl.ds(start, full), :] = attended
                qkv_out[b, 0, pl.ds(start, full), :] = query
                qkv_out[b, 1, pl.ds(start, full), :] = key
                qkv_out[b, 2, pl.ds(start, full), :] = value
                p_out[b, r] = low

    outs = [
        shape_of((2, tokens, head_width)),
        shape_of((2, 3, tokens, head_width)),
        shape_of((2, here, n_heads * full, full)),
    ]
    if keep_x:
        outs = [shape_of((tokens, width))] + outs
    return call(
        body,
        outs,
        [VM] * len(outs),
        [SM, VM] + [VM] * (count + len(flat)),
        [
            pltpu.VMEM((tokens, width), bf16),
            pltpu.VMEM((2, inner, width), bf16),
        ],
        us=10,
        name="attend",
        room=18,
        after=after,
    )(ids, segr, *pieces, *flat)


def gelu_pair(u):
    z = jnp.abs(u) * (0.5 ** 0.5)
    t = 1.0 / (1.0 + 0.3275911 * z)
    poly = t * (
        0.254829592
        + t * (-0.284496736 + t * (1.421413741 + t * (-1.453152027 + t * 1.061405429)))
    )
    bell = jnp.exp(-0.5 * u * u)
    tail = 0.5 * poly * bell
    cdf = jnp.where(u >= 0, 1.0 - tail, tail)
    return u * cdf, cdf + u * bell * 0.3989422804014327


def norm_rows(values):
    centre = values - jnp.mean(values, axis=1, keepdims=True)
    inverse = lax.rsqrt(jnp.mean(centre * centre, axis=1, keepdims=True) + EPSILON)
    return centre * inverse, inverse


def ffn_near(ids, x, ols, pieces, vecs, out_parts, near_in, near_down, inner, dims, after=()):
    devices, count, rows, quarter, full, width = dims
    here = rows // count
    tokens = here * full
    tile = here * quarter
    head_width = ols[0].shape[2]
    hidden = width
    flat = [ref for p in out_parts for ref, _ in p]
    n = len(flat)

    def body(ids_ref, x_ref, ol_a, ol_b, *refs):
        refs = list(refs)
        places = piece_places([refs.pop(0) for _ in range(count)], tile + 16)
        vec_refs = [refs.pop(0) for _ in range(3)]
        wo_refs = [refs.pop(0) for _ in range(n)]
        wi_refs = [refs.pop(0) for _ in range(2)]
        wd_refs = [refs.pop(0) for _ in range(2)]
        al_out, hat_out, inv_out, acc_out, hl0, hl1, gp0, gp1, wo = refs
        hl_out, gp_out = (hl0, hl1), (gp0, gp1)
        w_out = []
        at = 0
        for kk in range(count):
            m = len(out_parts[kk])
            w_out.append(
                whole_block(
                    wo_refs[at : at + m], bases_of(out_parts[kk]), ids_ref[2], head_width // 2,
                    wo.at[kk], inner // 2,
                )
            )
            at += m
        b_out, gain_a, bias_a = (v[...].reshape(1, width) for v in vec_refs)
        for r in range(here):
            span = slice(r * full, (r + 1) * full)
            total = x_ref[span, :].astype(f32) + b_out
            for kk in range(count):
                ol = (ol_a, ol_b)[kk // 2]
                total = total + mm(ol[kk % 2, span, :], w_out[kk][...])
            hat, inverse = norm_rows(total)
            hat_out[span, :] = hat
            inv_out[span, :] = jnp.broadcast_to(inverse, (full, 128))
            al_out[span, :] = (hat * gain_a + bias_a).astype(bf16)
        half = tokens // 2
        for b in range(2):
            ref, base = places[b]
            bias = bias_rows(ref, base + tile, 3)
            for m in range(2):
                span = slice(m * half, (m + 1) * half)
                u = mm(al_out[span, :], wi_refs[b][...]) + bias
                active, slope = gelu_pair(u)
                active = active.astype(bf16)
                hl_out[b][span, :] = active
                gp_out[b][span, :] = slope.astype(bf16)
                part = mm(active, wd_refs[b][...])
                if b == 0:
                    acc_out[span, :] = part
                else:
                    acc_out[span, :] += part

    wide = (tokens, width)
    return call(
        body,
        [
            shape_of(wide), shape_of(wide, f32), shape_of((tokens, 128), f32), shape_of(wide, f32),
            *[shape_of(wide)] * 4,
        ],
        [VM] * 8,
        [SM, VM, VM, VM] + [VM] * (count + n + 7),
        [
            pltpu.VMEM((count, head_width, width), bf16),
        ],
        us=11,
        name="ffn_near",
        room=26,
        after=after,
    )(ids, x, ols[0], ols[1], *pieces, *vecs, *flat, *near_in, *near_down)


def ffn_far(ids, al, pieces, parts, dims, after=()):
    devices, count, rows, quarter, full, width = dims
    here = rows // count
    tokens = here * full
    tile = here * quarter
    hidden = width
    flat = [ref for p in parts for ref, _ in p]
    n = len(flat)

    def body(ids_ref, al_ref, *refs):
        places = piece_places(refs[:count], tile + 16)
        w_refs = refs[count : count + n]
        hl2, hl3, gp2, gp3, wi = refs[count + n :]
        hl_out, gp_out = (hl2, hl3), (gp2, gp3)
        blocks = []
        at = 0
        for b in range(2):
            m = len(parts[b])
            blocks.append(
                whole_block(w_refs[at : at + m], bases_of(parts[b]), ids_ref[2], width // 2, wi.at[b])
            )
            at += m
        half = tokens // 2
        for b in range(2):
            ref, base = places[2 + b]
            bias = bias_rows(ref, base + tile, 3)
            for m in range(2):
                span = slice(m * half, (m + 1) * half)
                active, slope = gelu_pair(mm(al_ref[span, :], blocks[b][...]) + bias)
                hl_out[b][span, :] = active.astype(bf16)
                gp_out[b][span, :] = slope.astype(bf16)

    wide = (tokens, width)
    return call(
        body,
        [shape_of(wide)] * 4,
        [VM] * 4,
        [SM, VM] + [VM] * (count + n),
        [pltpu.VMEM((2, width, hidden), bf16)],
        us=6,
        name="ffn_far",
        room=14,
        after=after,
    )(ids, al, *pieces, *flat)


def ffn_down(ids, sent, segr, al, acc, hls, vecs, ogs, pool_grad, parts, dims):
    devices, count, rows, quarter, full, width = dims
    here, cap, reach = rows // count, rows // devices, devices // count
    tokens = here * full
    hidden = width
    flat = [ref for p in parts for ref, _ in p]
    n = len(flat)

    def body(ids_ref, sent_ref, segr_ref, al_ref, near_ref, hl1, hl2, hl3, *refs):
        hl_far = (hl2, hl3)
        refs = list(refs)
        vec_refs = [refs.pop(0) for _ in range(3)]
        og_refs = [refs.pop(0) for _ in range(reach)]
        pool_ref = refs.pop(0)
        w_refs = [refs.pop(0) for _ in range(n)]
        tk0, tk1, pooled_out, dz_out, low_out, sums_out, down_out, wd, og_buf, acc_ref, sems = refs
        mi, parity = ids_ref[1], parity_of(ids_ref, 2)
        blocks = []
        at = 0
        for b in range(2):
            m = len(parts[b])
            blocks.append(
                whole_block(w_refs[at : at + m], bases_of(parts[b]), parity, width // 2, wd.at[b])
            )
            at += m
        cots = []
        for k in range(reach):
            for c in range(cap):
                r = k * cap + c
                for kk in range(count):
                    cots.append(
                        pltpu.make_async_copy(
                            og_refs[k].at[c, pl.ds(pl.multiple_of((mi ^ kk) * quarter, quarter), quarter)],
                            og_buf.at[pl.ds(r * full + kk * quarter, quarter)],
                            sems.at[r * count + kk],
                        )
                    )
        for copy in cots:
            copy.start()
        b_down, gain_f, bias_f = (v[...].reshape(1, width) for v in vec_refs)
        half = tokens // 2
        for b in range(2):
            for m in range(2):
                span = slice(m * half, (m + 1) * half)
                part = mm(hl_far[b][span, :], blocks[b][...])
                if b == 0:
                    acc_ref[span, :] = part + near_ref[span, :]
                else:
                    acc_ref[span, :] += part
        for copy in cots:
            copy.wait()
        sums_out[...] = jnp.zeros_like(sums_out)
        for r in range(here):
            span = slice(r * full, (r + 1) * full)
            hat, inverse = norm_rows(al_ref[span, :].astype(f32) + acc_ref[span, :] + b_down)
            final = hat * gain_f + bias_f
            final_low = final.astype(bf16)
            for kk in range(count):
                (tk0, tk1)[r // cap][
                    kk, (r % cap) * quarter : (r % cap + 1) * quarter, :
                ] = final_low[kk * quarter : (kk + 1) * quarter, :]
            lane = jnp.broadcast_to(segr_ref[r : r + 1, :], (8, full))
            member = jnp.where(lane == lax.broadcasted_iota(jnp.int32, (8, full), 0), 1.0, 0.0)
            share = 1.0 / jnp.maximum(jnp.sum(member, axis=1, keepdims=True), 1.0)
            member = member.astype(bf16)
            sums = sum(mm(member, term) for term in split3(final))
            pooled_out[r * SEGS : (r + 1) * SEGS, :] = (sums * share)[0:SEGS]
            spread = jnp.concatenate(
                [pool_ref[sent_ref[r]], jnp.zeros((8 - SEGS, width), f32)], axis=0
            ) * share
            cot = og_buf[span, :].astype(f32) + sum(mm_tn(member, term) for term in split3(spread))
            e = cot * gain_f
            mean_e = jnp.mean(e, axis=1, keepdims=True)
            mean_p = jnp.mean(e * hat, axis=1, keepdims=True)
            dz = inverse * (e - mean_e - hat * mean_p)
            dz_out[span, :] = dz
            low_out[span, :] = dz.astype(bf16)
            sums_out[0:1, :] += jnp.sum(dz, axis=0, keepdims=True)
            sums_out[1:2, :] += jnp.sum(cot * hat, axis=0, keepdims=True)
            sums_out[2:3, :] += jnp.sum(cot, axis=0, keepdims=True)
        for b in range(2):
            for c in range(hidden // 256):
                cols = slice(c * 256, (c + 1) * 256)
                left = (hl1, hl3)[b][:, cols]
                down_out[b, cols, :] = mm_tn(left, low_out[...]).astype(bf16)

    wide = (tokens, width)
    return call(
        body,
        [
            shape_of((count, cap * quarter, width)), shape_of((count, cap * quarter, width)),
            shape_of((here * SEGS, width), f32), shape_of(wide, f32), shape_of(wide),
            shape_of((8, width), f32), shape_of((2, hidden, width)),
        ],
        [VM] * 7,
        [SM, SM] + [VM] * 9 + [HB] * reach + [VM] * (1 + n),
        [
            pltpu.VMEM((2, hidden, width), bf16),
            pltpu.VMEM(wide, bf16),
            pltpu.VMEM(wide, f32),
            pltpu.SemaphoreType.DMA((here * count,)),
        ],
        us=9,
        name="ffn_down",
        room=26,
    )(ids, sent, segr, al, acc, *hls, *vecs, *ogs, pool_grad, *flat)


def ffn_back(ids, low, gps, parts, dims):
    devices, count, rows, quarter, full, width = dims
    tokens = low.shape[0]
    hidden = width
    flat = [ref for p in parts for ref, _ in p]
    n = len(flat)

    def body(ids_ref, low_ref, *refs):
        gp_refs, dn_refs = refs[:count], refs[count : count + n]
        du_outs = refs[count + n : 2 * count + n]
        bin_out, wd = refs[2 * count + n :]
        parity = parity_of(ids_ref, 2)
        blocks = []
        at = 0
        for kk in range(count):
            m = len(parts[kk])
            blocks.append(
                whole_block(
                    dn_refs[at : at + m], bases_of(parts[kk]), parity, width // 2, wd.at[kk % 2],
                )
            )
            at += m
        half = tokens // 2
        for kk in (1, 3, 2, 0):
            total = jnp.zeros((1, hidden), f32)
            for m in range(2):
                span = slice(m * half, (m + 1) * half)
                part = (
                    mm_nt(low_ref[span, :], blocks[kk][...]) * gp_refs[kk][span, :].astype(f32)
                ).astype(bf16)
                du_outs[kk][span, :] = part
                total = total + jnp.sum(part.astype(f32), axis=0, keepdims=True)
            bin_out[kk : kk + 1, :] = total

    return call(
        body,
        [shape_of((tokens, hidden))] * count + [shape_of((count, hidden), f32)],
        [VM] * (count + 1),
        [SM, VM] + [VM] * (count + n),
        [pltpu.VMEM((2, hidden, width), bf16)],
        us=5,
        name="ffn_back",
        room=22,
    )(ids, low, *gps, *flat)


def norm_back_attn(ids, dus, al, dz, hat, inv, gain, parts, dims, after=()):
    devices, count, rows, quarter, full, width = dims
    tokens = al.shape[0]
    hidden = width
    flat = [ref for p in parts for ref, _ in p]
    n = len(flat)

    def body(ids_ref, al_ref, dz_ref, hat_ref, inv_ref, vec_ref, *refs):
        du_refs, refs = refs[:count], refs[count:]
        oi_refs = refs[:n]
        dz1_out, low_out, sums_out, in_out, wi, acc = refs[n:]
        blocks = []
        at = 0
        for kk in range(count):
            m = len(parts[kk])
            blocks.append(
                whole_block(
                    oi_refs[at : at + m], bases_of(parts[kk]), ids_ref[2], width // 2, wi.at[kk % 2]
                )
            )
            at += m
        half = tokens // 2
        for kk in range(count):
            for m in range(2):
                span = slice(m * half, (m + 1) * half)
                part = mm_nt(du_refs[kk][span, :], blocks[kk][...])
                if kk == 0:
                    acc[span, :] = part + dz_ref[span, :]
                else:
                    acc[span, :] += part
        gain_a = vec_ref[...].reshape(1, width)
        sums_out[...] = jnp.zeros_like(sums_out)

        @pl.loop(0, tokens // full)
        def _(r):
            span = pl.ds(pl.multiple_of(r * full, full), full)
            da = acc[span, :]
            hat_r = hat_ref[span, :]
            e = da * gain_a
            mean_e = jnp.mean(e, axis=1, keepdims=True)
            mean_p = jnp.mean(e * hat_r, axis=1, keepdims=True)
            dz1 = inv_ref[span, 0:1] * (e - mean_e - hat_r * mean_p)
            dz1_out[span, :] = dz1
            low_out[span, :] = dz1.astype(bf16)
            sums_out[0:1, :] += jnp.sum(dz1, axis=0, keepdims=True)
            sums_out[1:2, :] += jnp.sum(da * hat_r, axis=0, keepdims=True)
            sums_out[2:3, :] += jnp.sum(da, axis=0, keepdims=True)

        for b, kk in enumerate((1, 3)):
            for c in range(width // 256):
                cols = slice(c * 256, (c + 1) * 256)
                in_out[b, cols, :] = mm_tn(al_ref[:, cols], du_refs[kk][...]).astype(bf16)

    wide = (tokens, width)
    return call(
        body,
        [
            shape_of(wide, f32), shape_of(wide), shape_of((8, width), f32),
            shape_of((2, width, hidden)),
        ],
        [VM] * 4,
        [SM] + [VM] * (5 + count + n),
        [
            pltpu.VMEM((2, width, hidden), bf16),
            pltpu.VMEM(wide, f32),
        ],
        us=8,
        name="norm_back",
        room=26,
        after=after,
    )(ids, al, dz, hat, inv, gain, *dus, *flat)


def attend_back(ids, low, x, blocks, extras, dims, after=()):
    devices, count, rows, quarter, full, width = dims
    here = rows // count
    tokens = x.shape[0]
    head_width = blocks[0][2].shape[2]
    inner = 3 * head_width
    flat = [ref for b in blocks for ref, _ in b[5]]
    n = len(flat)
    half_out = head_width // 2
    nb = len(blocks)

    def body(ids_ref, low_ref, x_ref, bin_ref, ffn_ref, norm_ref, *refs):
        data = refs[: 3 * nb]
        w_refs = refs[3 * nb : 3 * nb + n]
        mix_out, grad_out, wo, sums = refs[3 * nb + n :]
        w_out = []
        at = 0
        for b in range(nb):
            m = len(blocks[b][5])
            w_out.append(
                whole_block(
                    w_refs[at : at + m], bases_of(blocks[b][5]), ids_ref[2], half_out, wo.at[b],
                    inner // 2,
                )
            )
            at += m
        masks = head_masks(head_width)
        sums[...] = jnp.zeros_like(sums)
        for b in range(nb):
            kk, place = blocks[b][:2]
            ol_ref, qkv_ref, p_ref = data[3 * b : 3 * b + 3]

            @pl.loop(0, here, unroll=True)
            def _(r):
                span = pl.ds(pl.multiple_of(r * full, full), full)
                dol = mm_nt(low_ref[span, :], w_out[b][...]).astype(bf16)
                query, key, value = (qkv_ref[place, i, span, :] for i in range(3))
                low_p = p_ref[place, r]
                prob = low_p.astype(f32)
                dos = stack_heads(dol, masks)
                dp = mm_nt(dos, value)
                ds = (prob * (dp - jnp.sum(dp * prob, axis=1, keepdims=True))).astype(bf16)
                dv = mm_tn(low_p, dos).astype(bf16)
                dq = (pick_heads(mm(ds, key), masks) * (HD ** -0.5)).astype(bf16)
                dk = (mm_tn(ds, stack_heads(query, masks)) * (HD ** -0.5)).astype(bf16)
                mix_out[b, span, 0:head_width] = dq
                mix_out[b, span, head_width : 2 * head_width] = dk
                mix_out[b, span, 2 * head_width :] = dv
                sums[b : b + 1, 0:head_width] += jnp.sum(dq.astype(f32), axis=0, keepdims=True)
                sums[b : b + 1, 256 : 256 + head_width] += jnp.sum(
                    dv.astype(f32), axis=0, keepdims=True
                )

            for c in range(3):
                part = slice(c * head_width, (c + 1) * head_width)
                grad_out[b, part, :] = mm_tn(mix_out[b, :, part], x_ref[...]).astype(bf16)
            grad_out[b, inner:width, :] = mm_tn(ol_ref[place], low_ref[...]).astype(bf16)
            lines = jnp.concatenate(
                [sums[b : b + 1], bin_ref[kk : kk + 1], norm_ref[0:3], ffn_ref[0:3]], axis=0
            )
            grad_out[b, width : width + 16, :] = two_terms(lines)

    return call(
        body,
        [shape_of((nb, tokens, inner)), shape_of((nb, width + 16, width))],
        [VM] * 2,
        [SM] + [VM] * (5 + 3 * nb + n),
        [
            pltpu.VMEM((nb, head_width, width), bf16),
            pltpu.VMEM((8, width), f32),
        ],
        us=13,
        name="attend_back",
        room=26,
        after=after,
    )(ids, low, x, *extras, *[v for b in blocks for v in b[2:5]], *flat)


def two_terms(lines):
    high = lines.astype(bf16)
    return jnp.concatenate([high, (lines - high.astype(f32)).astype(bf16)], axis=0)


def one_term(lines):
    return lines[0:8].astype(f32) + lines[8:16].astype(f32)


def peer_grad(lhs, rhs, got, after=()):
    tokens, width = rhs.shape
    rows = lhs.shape[1]

    def body(lhs_ref, rhs_ref, got_ref, out):
        for c in range(rows // 256):
            cols = slice(c * 256, (c + 1) * 256)
            out[cols, :] = (
                mm_tn(lhs_ref[:, cols], rhs_ref[...]) + got_ref[1, cols, :].astype(f32)
            ).astype(bf16)

    return call(
        body,
        shape_of((rows, width)),
        VM,
        [VM, VM, VM],
        us=0.2,
        name="peer_grad",
        room=10,
        after=after,
    )(lhs, rhs, got)


def shards(acc, ids_ref, devices, bits, size, send, keep):
    for p in range(devices):
        mirror = sum(((p >> j) & 1) << (bits - 1 - j) for j in range(bits))
        rows = acc[pl.ds(pl.multiple_of((ids_ref[0] ^ mirror) * size, 16), size), :]
        if p < devices // 2:
            keep[p * size : (p + 1) * size, :] = rows
        else:
            q = p - devices // 2
            send[q * size : (q + 1) * size, :] = rows.astype(bf16)


def own_grad(ids, lhs, rhs, got, crossed, devices, after=()):
    tokens, width = rhs.shape
    rows = lhs.shape[1]
    bits = devices.bit_length() - 1
    size = rows // devices

    def body(ids_ref, lhs_ref, rhs_ref, got_ref, cross_ref, send, keep, acc):
        for c in range(rows // 256):
            cols = slice(c * 256, (c + 1) * 256)
            acc[cols, :] = (
                mm_tn(lhs_ref[:, cols], rhs_ref[...])
                + got_ref[0, cols, :].astype(f32)
                + cross_ref[cols, :].astype(f32)
            )
        shards(acc, ids_ref, devices, bits, size, send, keep)

    return call(
        body,
        [shape_of((rows // 2, width)), shape_of((rows // 2, width), f32)],
        [VM, VM],
        [SM, VM, VM, VM, VM],
        [pltpu.VMEM((rows, width), f32)],
        us=0.2,
        name="own_grad",
        room=14,
        after=after,
    )(ids, lhs, rhs, got, crossed)


def peer_last(grads, got, at, after=()):
    _, high, width = grads.shape

    def body(a_ref, g_ref, out):
        out[0 : high - 16, :] = (
            a_ref[at, 0 : high - 16, :].astype(f32) + g_ref[1, 0 : high - 16, :].astype(f32)
        ).astype(bf16)
        out[high - 16 :, :] = two_terms(
            one_term(a_ref[at, high - 16 :, :]) + one_term(g_ref[1, high - 16 :, :])
        )

    return call(
        body, shape_of((high, width)), VM, [VM, VM], us=0.2, name="peer_last",
        room=12,
        after=after,
    )(grads, got)


def own_last(ids, grads, got, crossed, at, devices, after=()):
    _, high, width = grads.shape
    body_rows = high - 16
    bits = devices.bit_length() - 1
    size = body_rows // devices

    def body(ids_ref, a_ref, g_ref, c_ref, send, keep, vec, acc):
        acc[...] = (
            a_ref[at, 0:body_rows, :].astype(f32)
            + g_ref[0, 0:body_rows, :].astype(f32)
            + c_ref[0:body_rows, :].astype(f32)
        )
        shards(acc, ids_ref, devices, bits, size, send, keep)
        lines = (
            one_term(a_ref[at, body_rows:, :])
            + one_term(g_ref[0, body_rows:, :])
            + one_term(c_ref[body_rows:, :])
        )
        send[body_rows // 2 :, :] = two_terms(lines)
        vec[...] = lines

    return call(
        body,
        [
            shape_of((body_rows // 2 + 16, width)),
            shape_of((body_rows // 2, width), f32),
            shape_of((8, width), f32),
        ],
        [VM] * 3,
        [SM, VM, VM, VM],
        [pltpu.VMEM((body_rows, width), f32)],
        us=0.2,
        name="own_last",
        room=16,
        after=after,
    )(ids, grads, got, crossed)


def cut(keep, got, vec, after=()):
    high, width = keep.shape
    last = vec is not None
    tail = 16 if last else 0
    size = high // 4

    def body(*refs):
        keep_ref, got_ref = refs[:2]
        rest = refs[2:]
        if last:
            vec_ref, rest = rest[0], rest[1:]
            lines = vec_ref[...] + one_term(got_ref[high:, :])
            rest[4][...] = lines
        for p in range(4):
            span = slice(p * size, (p + 1) * size)
            total = keep_ref[span, :] + got_ref[span, :].astype(f32)
            if p == 0:
                rest[3][...] = total
            else:
                rest[p - 1][0:size, :] = total.astype(bf16)
                if last:
                    rest[p - 1][size:, :] = two_terms(lines)

    outs = [shape_of((size + tail, width))] * 3 + [shape_of((size, width), f32)]
    args = [keep, got]
    if last:
        outs.append(shape_of((8, width), f32))
        args.append(vec)
    return call(
        body, outs, [VM] * len(outs), [VM] * len(args), us=0.1, name="cut", room=8, after=after
    )(*args)


def gather_sum(keep, gots, vec, after=()):
    high, width = keep.shape
    last = vec is not None
    n = len(gots)

    def body(*refs):
        keep_ref, got_refs, rest = refs[0], refs[1 : 1 + n], refs[1 + n :]
        if last:
            vec_ref, rest = rest[0], rest[1:]
            lines = vec_ref[...]
            for got in got_refs:
                lines = lines + one_term(got[high:, :])
            rest[1][...] = lines
        total = keep_ref[...]
        for got in got_refs:
            total = total + got[0:high, :].astype(f32)
        rest[0][...] = total.astype(bf16)

    outs = [shape_of((high, width))]
    args = [keep, *gots]
    if last:
        outs.append(shape_of((8, width), f32))
        args.append(vec)
    return call(
        body, outs, [VM] * len(outs), [VM] * len(args), us=0.1, name="gather_sum", room=8, after=after
    )(*args)


def join(pieces, after=()):
    size, width = pieces[0].shape
    n = len(pieces)

    def body(*refs):
        for p in range(n):
            refs[n][p * size : (p + 1) * size, :] = refs[p][...]

    return call(
        body, shape_of((n * size, width)), VM, [VM] * n, us=0.1, name="join", room=4, after=after
    )(*pieces)


MASKS = (4, 2, 6)


def place_shards(ids_ref, pieces, devices, size, put):
    bits = devices.bit_length() - 1
    p = 0
    for piece in pieces:
        for q in range(piece.shape[0] // size):
            mirror = sum(((p >> j) & 1) << (bits - 1 - j) for j in range(bits))
            at = pl.multiple_of((ids_ref[0] ^ mirror) * size, 8)
            put(at, piece[q * size : (q + 1) * size, :].astype(f32))
            p += 1


def whole_grad(ids, pieces, devices, cuts, after=()):
    size, width = pieces[0].shape
    n = len(pieces)

    def body(ids_ref, *refs):
        outs = refs[n : n + len(cuts)]
        acc = refs[n + len(cuts)] if len(cuts) > 1 else outs[0]

        def put(at, rows):
            acc[pl.ds(at, size), :] = rows

        place_shards(ids_ref, refs[:n], devices, size, put)
        if len(cuts) > 1:
            base = 0
            for out, rows in zip(outs, cuts):
                out[...] = acc[base : base + rows, :]
                base += rows

    return call(
        body,
        [shape_of((rows, width), f32) for rows in cuts],
        [VM] * len(cuts),
        [SM] + [VM] * n,
        [pltpu.VMEM((size * devices, width), f32)] if len(cuts) > 1 else [],
        us=0.5,
        name="whole_grad",
        room=12,
        after=after,
    )(ids, *pieces)


def grad_input_rows(ids, dz1, mixes, parts, pooled, dims, after=()):
    devices, count, rows, quarter, full, width = dims
    here = rows // count
    tokens = here * full
    tile = here * quarter
    inner = mixes[0].shape[2]
    flat = [ref for p in parts for ref, _ in p]
    n = len(flat)
    turn = (1, 3, 2, 0)

    def body(ids_ref, dz_ref, m_a, m_b, pool_ref, *refs):
        w_refs = refs[:n]
        own, near, far = refs[n : n + 3]
        wq, acc = refs[n + 3 :]
        blocks = []
        at = 0
        for kk in range(count):
            m = len(parts[kk])
            blocks.append(
                whole_block(
                    w_refs[at : at + m], bases_of(parts[kk]), ids_ref[2], inner // 2, wq.at[kk % 2]
                )
            )
            at += m
        half = tokens // 2
        for i, kk in enumerate(turn):
            mix = (m_a, m_b)[i // 2]
            for m in range(2):
                span = slice(m * half, (m + 1) * half)
                part = mm(mix[i % 2, span, :], blocks[kk][...])
                if i == 0:
                    acc[span, :] = part + dz_ref[span, :]
                else:
                    acc[span, :] += part
        size = tile + here * SEGS
        for kk, (ref, base) in enumerate(piece_places((own, near, far, far), size)):
            for r in range(here):
                ref[base + r * quarter : base + (r + 1) * quarter, :] = acc[
                    r * full + kk * quarter : r * full + (kk + 1) * quarter, :
                ].astype(bf16)
            ref[base + tile : base + size, :] = pool_ref[...].astype(bf16)

    return call(
        body,
        [shape_of((m * (tile + here * SEGS), width)) for m in (1, 1, 2)],
        [VM] * 3,
        [SM] + [VM] * (4 + n),
        [
            pltpu.VMEM((2, inner, width), bf16),
            pltpu.VMEM((tokens, width), f32),
        ],
        us=6,
        name="grad_input_rows",
        room=22,
        after=after,
    )(ids, dz1, *mixes, pooled, *flat)


def land_grad(sent, pieces, dims, after=()):
    devices, count, rows, quarter, full, width = dims
    here = rows // count
    tile = here * quarter
    size = tile + here * SEGS

    def body(sent_ref, *refs):
        places = piece_places(refs[:count], size)
        out, pooled, sems = refs[count:]
        copies = []
        for kk, (ref, base) in enumerate(places):
            for j in range(here):
                at = kk * here + j
                copy = pltpu.make_async_copy(
                    ref.at[pl.ds(base + j * quarter, quarter)], out.at[sent_ref[at]], sems.at[at]
                )
                copy.start()
                copies.append(copy)
        for kk, (ref, base) in enumerate(places):
            lines = ref[base + tile : base + size, :].astype(f32)
            for j in range(here):
                pooled[sent_ref[kk * here + j]] = lines[j * SEGS : (j + 1) * SEGS]
        for copy in copies:
            copy.wait()

    return call(
        body,
        [shape_of((rows, quarter, width)), shape_of((rows, SEGS, width), f32)],
        [HB, VM],
        [SM] + [VM] * count,
        [pltpu.SemaphoreType.DMA((rows,))],
        us=0.5,
        name="land_grad",
        room=8,
        after=after,
    )(sent, *pieces)


def turn_output(hops, dims, after=()):
    devices, count, rows, quarter, full, width = dims
    cap, reach = rows // devices, devices // count
    part = cap * quarter
    tile = reach * part

    def body(*refs):
        hop_refs = refs[:reach]
        near, far, sems = refs[reach:]
        copies = []
        for kk, (ref, base) in enumerate(((near, 0), (far, 0), (far, tile))):
            for k in range(reach):
                copies.append(
                    pltpu.make_async_copy(
                        hop_refs[k].at[kk + 1],
                        ref.at[pl.ds(base + k * part, part)],
                        sems.at[kk * reach + k],
                    )
                )
        for copy in copies:
            copy.start()
        for copy in copies:
            copy.wait()

    return call(
        body,
        [shape_of((tile, width)), shape_of((2 * tile, width))],
        [VM, VM],
        [HB] * reach,
        [pltpu.SemaphoreType.DMA((3 * reach,))],
        us=0.1,
        name="turn_output",
        room=8,
        after=after,
    )(*hops)


def land_output(spots, hops, pieces, dims, after=()):
    devices, count, rows, quarter, full, width = dims
    here, cap, reach = rows // count, rows // devices, devices // count
    tile = here * quarter

    def body(spots_ref, *refs):
        hop_refs = refs[:reach]
        places = piece_places((None,) + refs[reach : reach + count - 1], tile)
        out, sems = refs[reach + count - 1 :]
        copies = []
        for kk in range(count):
            for j in range(here):
                at = kk * here + j
                if kk == 0:
                    src = hop_refs[j // cap].at[0, pl.ds((j % cap) * quarter, quarter)]
                else:
                    ref, base = places[kk]
                    src = ref.at[pl.ds(base + j * quarter, quarter)]
                copies.append(pltpu.make_async_copy(src, out.at[spots_ref[at]], sems.at[at]))
        for copy in copies:
            copy.start()
        for copy in copies:
            copy.wait()

    return call(
        body,
        shape_of((rows, quarter, width)),
        HB,
        [SM] + [VM] * (reach + count - 1),
        [pltpu.SemaphoreType.DMA((rows,))],
        us=0.5,
        name="land_output",
        room=8,
        after=after,
    )(spots, *hops, *pieces)


def swap(values, axis, bit):
    return lax.ppermute(values, axis, [(i, i ^ bit) for i in range(lax.axis_size(axis))])


def per_device(
    tokens_in, seg, route, w_qkv, b_qv, w_out, b_out, gain_attn, bias_attn, w_in, b_in, w_down,
    b_down, gain_ffn, bias_ffn, out_grad, pool_grad,
):
    devices, count = lax.axis_size("dp"), lax.axis_size("mp")
    rows, quarter, width = tokens_in.shape
    full = seg.shape[1]
    dims = (devices, count, rows, quarter, full, width)
    reach = devices // count
    head_width = w_qkv.shape[2]
    inner = 3 * head_width

    def hop(values, k):
        return lax.ppermute(
            values,
            ("dp", "mp"),
            [
                (s * count + f, (s ^ (f + count * k)) * count + f)
                for s in range(devices)
                for f in range(count)
            ],
        )

    wq = w_qkv.transpose(1, 2, 0).reshape(inner, width)
    half_rows = (inner + head_width) // 2
    *sends, segr, sent, spots, ids = prep_rows(
        route, seg, tokens_in, b_qv, b_in, (wq, w_out), dims
    )
    near_q, near_o, near_i, near_d = (swap(v, "mp", 1) for v in (wq, w_out, w_in, w_down))
    og_sends = prep_cot(spots, out_grad, dims, (near_q,))
    ogs = [hop(og_sends[k], k) for k in range(reach)]
    pieces = exchange(*sends, before=(near_q, near_o, near_i, near_d, *ogs))

    def later(values, after):
        return lax.optimization_barrier((values, after))[0]

    def crossed(half, bit, first, second):
        direct = later(swap(half, "mp", 2), first)
        relayed = swap(direct, "dp", bit)
        far = (direct, relayed)
        return [
            [(v, 0) for v in far],
            [(swap(direct, "mp", 1), 0), (swap(later(relayed, second), "mp", 1), 0)],
        ]

    below = sends[2].shape[0] - half_rows
    relay_q = swap(pieces[2][below:], "dp", 1)
    half_in = prep_halves((w_in,), 1, (pieces[2],))
    x, ol_a, qkv_a, p_a = attend(
        ids, segr, pieces, [[(wq, 0)], [(near_q, 0)]], (0, 1), inner, dims, True,
        (half_in,),
    )
    relay_q3 = swap(later(relay_q, x), "mp", 1)
    far_q = [(pieces[2], below), (relay_q, 0)]
    far_q3 = [(pieces[3], below), (relay_q3, 0)]
    half_dn = prep_halves((w_down,), 2, (x,))
    ol_b, qkv_b, p_b = attend(
        ids, segr, pieces, [far_q, far_q3], (2, 3), inner, dims, False, (half_dn,)
    )
    q_parts = [[(wq, 0)], [(near_q, 0)], far_q, far_q3]
    wo_parts = [[(w_out, 0)], [(near_o, 0)], far_q, far_q3]
    al, hat, inv, acc, hl0, hl1, gp0, gp1 = ffn_near(
        ids, x, (ol_a, ol_b), pieces, (b_out, gain_attn, bias_attn), wo_parts, (w_in, near_i),
        (w_down, near_d), inner, dims,
    )
    in_parts = [[(w_in, 0)], [(near_i, 0)], *crossed(half_in, 1, x, ol_b)]
    hl2, hl3, gp2, gp3 = ffn_far(ids, al, pieces, in_parts[2:], dims)
    dn_parts = [[(w_down, 0)], [(near_d, 0)], *crossed(half_dn, 2, x, al)]
    tk0, tk1, pooled, dz, low, ffn_sums, down_pair = ffn_down(
        ids, sent, segr, al, acc, (hl1, hl2, hl3), (b_down, gain_ffn, bias_ffn), ogs, pool_grad,
        dn_parts[2:], dims,
    )
    got_down = swap(down_pair, "mp", 1)
    *dus, bin_sums = ffn_back(ids, low, (gp0, gp1, gp2, gp3), dn_parts, dims)
    down_far = peer_grad(hl2, low, got_down, (bin_sums,))
    hops = [hop(t, k) for k, t in enumerate(lax.optimization_barrier((tk0, tk1, down_far))[:2])]
    crossed_down = swap(down_far, "mp", 2)
    dz1, low1, norm_sums, in_pair = norm_back_attn(
        ids, dus, al, dz, hat, inv, gain_attn, in_parts, dims, (down_far,)
    )
    got_in = swap(in_pair, "mp", 1)
    extras = (bin_sums, ffn_sums, norm_sums)
    mix_a, grads_a = attend_back(
        ids, low1, x,
        [(1, 1, ol_a, qkv_a, p_a, wo_parts[1]), (3, 1, ol_b, qkv_b, p_b, wo_parts[3])],
        extras, dims,
    )
    got_last = swap(grads_a, "mp", 1)
    in_far = peer_grad(al, dus[2], got_in, (grads_a,))
    crossed_in = swap(in_far, "mp", 2)
    turned = turn_output(hops, dims, (in_far,))
    send_down, keep_down = own_grad(
        ids, hl0, low, got_down, crossed_down, devices, (turned[0],)
    )
    mix_b, grads_b = attend_back(
        ids, low1, x,
        [(2, 0, ol_b, qkv_b, p_b, wo_parts[2]), (0, 0, ol_a, qkv_a, p_a, wo_parts[0])],
        extras, dims, (send_down,),
    )
    last_far = peer_last(grads_b, got_last, 0)
    crossed_last = swap(last_far, "mp", 2)

    def places_of(parts):
        return [swap(part, "dp", mask) for part, mask in zip(parts, MASKS)]

    cut_down = cut(keep_down, swap(send_down, "dp", 1), None, (last_far,))
    down_places = places_of(cut_down[:3])
    gx = grad_input_rows(ids, dz1, (mix_a, mix_b), q_parts, pooled, dims, (cut_down[0],))
    (shard_down,) = gather_sum(cut_down[3], down_places, None, (gx[0],))
    down_spread = [shard_down] + places_of([shard_down] * 3)
    send_in, keep_in = own_grad(
        ids, al, dus[0], got_in, crossed_in, devices, (shard_down,)
    )
    in_half = swap(send_in, "dp", 1)
    cut_in = cut(keep_in, in_half, None, (send_in,))
    in_places = places_of(cut_in[:3])
    half_down = join(down_spread, (cut_in[0],))
    down_spread.append(swap(half_down, "dp", 1))
    (shard_in,) = gather_sum(cut_in[3], in_places, None, (half_down,))
    in_spread = [shard_in] + places_of([shard_in] * 3)
    send, keep, vec = own_last(
        ids, grads_b, got_last, crossed_last, 1, devices, (shard_in,)
    )
    last_half = swap(send, "dp", 1)
    *gx, turned_near, turned_far, _ = lax.optimization_barrier((*gx, *turned, send))
    landed = exchange(None, turned_near, turned_far)[1:]
    gx_landed = exchange(*gx)
    half_in = join(in_spread, (send,))
    in_spread.append(swap(half_in, "dp", 1))
    cut_last = cut(keep, last_half, vec, (half_in,))
    last_places = places_of(cut_last[:3])
    shard_last, vec = gather_sum(cut_last[3], last_places, cut_last[4])
    last_spread = [shard_last] + places_of([shard_last] * 3)
    half_last = join(last_spread, (shard_last,))
    last_spread.append(swap(half_last, "dp", 1))
    (g_down,) = whole_grad(ids, down_spread, devices, (width,), (half_last,))
    (g_in,) = whole_grad(ids, in_spread, devices, (width,), (half_last,))
    tokens_out = land_output(spots, hops, landed, dims, (half_last,))
    grad_input, pooled_out = land_grad(sent, gx_landed, dims, (half_last,))
    g_qkv, g_out = whole_grad(ids, last_spread, devices, (inner, head_width))
    g_qkv = g_qkv.reshape(3, head_width, width).transpose(2, 0, 1)
    g_bqv = jnp.stack([vec[0, :head_width], vec[0, 256 : 256 + head_width]])
    return (
        tokens_out, pooled_out, grad_input, g_qkv, g_bqv, g_out,
        vec[2], vec[3], vec[4], g_in, vec[1], g_down, vec[5], vec[6], vec[7],
    )


def solution(mesh):
    devices, count = mesh.shape["dp"], mesh.shape["mp"]

    def body(*args):
        rows = args[0].shape[0]
        even = rows % devices == 0 and devices % count == 0 and count == 4
        even = even and devices & (devices - 1) == 0 and rows // count == 2 * (rows // devices)
        return (per_device if even else per_device_general)(*args)

    return jax.shard_map(
        body,
        mesh=mesh,
        in_specs=(
            P("dp", "mp", None),
            P(),
            P(),
            P(None, None, "mp"),
            P(None, "mp"),
            P("mp", None),
            P(),
            P(),
            P(),
            P(None, "mp"),
            P("mp"),
            P("mp", None),
            P(),
            P(),
            P(),
            P("dp", None, None),
            P("dp", None, None),
        ),
        out_specs=(
            P("dp", "mp", None),
            P("dp", None, None),
            P("dp", "mp", None),
            P(None, None, "mp"),
            P(None, "mp"),
            P("mp", None),
            P(),
            P(),
            P(),
            P(None, "mp"),
            P("mp"),
            P("mp", None),
            P(),
            P(),
            P(),
        ),
        check_vma=False,
    )
```
